256 devices in a mesh: ctx: 8 (over y, core), head: 32 (over x, z).
Axes of the slice: x: 4, y: 4, z: 8, core: 2. Of those that a mesh axis runs over, the one named last changes fastest.
Arguments:
- queries: bfloat16 [2048, 4096], P('head'), may hold values from -102 to 102
- span_keys: bfloat16 [2048, 1024], P('head'), may hold values from -6 to 6
- span_values: bfloat16 [2048, 1024], P('head'), may hold values from -3 to 3
- cache_keys: bfloat16 [65536, 1024], P(('ctx', 'head')), may hold values from -6 to 6
- cache_values: bfloat16 [65536, 1024], P(('ctx', 'head')), may hold values from -3 to 3
- cache_lengths: int32 [16], replicated, may hold values from 1 to 16384, 65536 in all
- span_lengths: int32 [16], replicated, may hold values from 1 to 512, 2048 in all
Outputs:
- attended: bfloat16 [2048, 4096], P('head')
The draws below stay inside these ranges and needn't reach their ends.
Inputs may be any that keep to these rules, and one draw needn't show every extreme that they name: cache_lengths sum to 65536. span_lengths sum to 2048.
All inputs are finite; a program needn't handle non-finite values.
Results may differ from the reference program's by a relative error of at most 0.0085.
The reference program's roundings to bfloat16 on the way count: a program that leaves them out, or rounds other values in their place, can miss the bound.
Values may be sent and summed in bfloat16 or wider, within the bound.
A program may use at most 192 MiB of HBM per device.

```python
import math
import jax
import jax.numpy as jnp
import numpy as np
from jax import lax

H = 32
KVH = 8
HD = 128
ROWS = 2048
KV_DEV = 256
NDOC = 16
CACHE = 65536
N_HEAD = 32


def draw_queries(key, part):
    first_key = jax.random.fold_in(jax.random.fold_in(key, 11), 0)
    base = jax.random.truncated_normal(first_key, -4.0, 4.0, (ROWS, H * HD), jnp.float32)
    return (1.5 * base).astype(jnp.bfloat16)


def levels(own_key, dims, cuts, smallest, high):
    loudness, own = 1.0, jax.random.fold_in(own_key, 6)
    for dim, parts in cuts:
        steps = jnp.exp(jax.random.uniform(jax.random.fold_in(own, dim), (parts,), jnp.float32, smallest / len(cuts), high / len(cuts)))
        loudness = loudness * jnp.repeat(steps, dims[dim] // parts).reshape([-1 if axis == dim else 1 for axis in range(len(dims))])
    return loudness


def split_up(number_of, total, reach, skew):
    weights = [(1 << 20) // math.isqrt(grade ** skew) + 1 for grade in range(2, number_of + 1)]
    surplus, holding = total - reach - (number_of - 1), [1] * (number_of - 1)
    while surplus > 0:
        free = [i for i in range(number_of - 1) if holding[i] < reach]
        whole, remaining = sum([weights[i] for i in free]), surplus
        for i in free:
            extra = min(reach - holding[i], max(1, remaining * weights[i] // whole), surplus)
            holding[i] = holding[i] + extra
            surplus = surplus - extra
    return np.array([reach] + holding)


def ragged_sizes(rng, amount, total, most, slope):
    if amount == 2:
        one = jax.random.randint(rng, (), max(1, total - most), min(most, total - 1) + 1)
        return jnp.stack([one, total - one])
    sizes = jnp.asarray(split_up(amount, total, most, slope), jnp.int32)
    couples = (amount - 1) // 2
    source_of, taker = sizes[1:1 + 2 * couples:2], sizes[2:2 + 2 * couples:2]
    slack = jnp.minimum(source_of - 1, most - taker)
    shifted = jax.random.randint(jax.random.fold_in(rng, 1), (couples,), 0, 1 << 20) % (slack + 1)
    sizes = sizes.at[1:1 + 2 * couples:2].set(source_of - shifted).at[2:2 + 2 * couples:2].set(taker + shifted)
    return sizes[jax.random.permutation(jax.random.fold_in(rng, 2), amount)]


def gaussian(stream_key, dims, scale, most, shards=(), kind=jnp.bfloat16):
    drawn = scale * jax.random.normal(stream_key, dims, jnp.float32)
    if shards:
        drawn = drawn * levels(stream_key, dims, shards, -0.22, 0.18)
    return jnp.clip(drawn, -most, most).astype(kind)


def setup_inputs(seed: int = 0) -> dict:
    streams_of = jax.random.split(jax.random.key(seed), 8)
    return {
        "queries": draw_queries(jax.random.fold_in(streams_of[7], 71), 0),
        "span_keys": gaussian(streams_of[1], (ROWS, KVH * HD), 1.0, 6.0, ((0, 32),)),
        "span_values": gaussian(streams_of[2], (ROWS, KVH * HD), 0.5, 3.0, ((0, 32),)),
        "cache_keys": gaussian(streams_of[3], (CACHE, KVH * HD), 1.0, 6.0, ((0, 256),)),
        "cache_values": gaussian(streams_of[4], (CACHE, KVH * HD), 0.5, 3.0, ((0, 256),)),
        "cache_lengths": ragged_sizes(streams_of[5], NDOC, CACHE, CACHE // 4, 2).astype(jnp.int32),
        "span_lengths": ragged_sizes(streams_of[6], NDOC, ROWS, ROWS // 4, 2).astype(jnp.int32),
    }


SCORE_FLOOR = -1e+30

def inverse_freq(head_dim):
    half_dim = head_dim // 2
    counter = jnp.arange(half_dim, dtype=jnp.float32)
    base_freq = 500000.0 ** (-2.0 * counter / head_dim)
    wavelen = 2.0 * math.pi / base_freq
    smooth = (8192.0 / wavelen - 1.0) / 3.0
    middle = (1.0 - smooth) * base_freq / 8.0 + smooth * base_freq
    return jnp.where(wavelen > 8192.0, base_freq / 8.0, jnp.where(wavelen < 2048.0, base_freq, middle))

def rotate(vectors, positions):
    head_dim = vectors.shape[-1]
    half_dim = head_dim // 2
    angle = positions.astype(jnp.float32)[:, None] * inverse_freq(head_dim)[None, :]
    cosine = jnp.cos(angle)[:, None, :]
    sine = jnp.sin(angle)[:, None, :]
    data = vectors.astype(jnp.float32)
    lower_half = data[..., :half_dim]
    upper_half = data[..., half_dim:]
    turned = jnp.concatenate([lower_half * cosine - upper_half * sine, upper_half * cosine + lower_half * sine], axis=-1)
    return turned.astype(jnp.bfloat16)

def lookup(doc_ids, table):
    slots = jnp.arange(table.shape[0], dtype=jnp.int32)
    return lax.optimization_barrier(jnp.sum(jnp.where(doc_ids[:, None] == slots[None, :], table[None, :], 0), axis=1)).astype(jnp.int32)

def documents(lengths, positions):
    ends = jnp.cumsum(lengths).astype(jnp.int32)
    doc_ids = lax.optimization_barrier(jnp.sum((positions[:, None] >= ends[None, :]).astype(jnp.int32), axis=1)).astype(jnp.int32)
    starts = (ends - lengths).astype(jnp.int32)
    return (doc_ids, (positions - lookup(doc_ids, starts)).astype(jnp.int32))

def reference(queries, span_keys, span_values, cache_keys, cache_values, cache_lengths, span_lengths):
    per_group = H // KVH
    row_ids = jnp.arange(ROWS, dtype=jnp.int32)
    row_docs, row_offsets = documents(span_lengths, row_ids)
    row_places = lookup(row_docs, cache_lengths) + row_offsets
    token_ids = jnp.arange(CACHE, dtype=jnp.int32)
    token_docs, token_places = documents(cache_lengths, token_ids)
    turned_queries = rotate(queries.reshape(ROWS, H, HD), row_places)
    turned_span = rotate(span_keys.reshape(ROWS, KVH, HD), row_places)
    turned_cache = rotate(cache_keys.reshape(CACHE, KVH, HD), token_places)
    query_sets = turned_queries.reshape(ROWS, KVH, per_group, HD).transpose(1, 0, 2, 3).reshape(KVH, ROWS * per_group, HD)
    cache_sets = turned_cache.transpose(1, 0, 2)
    value_sets = cache_values.reshape(CACHE, KVH, HD).transpose(1, 0, 2)
    span_sets = turned_span.transpose(1, 0, 2)
    span_value_sets = span_values.reshape(ROWS, KVH, HD).transpose(1, 0, 2)
    query_docs = jnp.repeat(row_docs, per_group)
    query_rows = jnp.repeat(row_ids, per_group)
    block_size = KV_DEV * N_HEAD
    block_count = CACHE // block_size
    score_scale = 1.0 / math.sqrt(HD)
    starts = jnp.arange(block_count, dtype=jnp.int32) * block_size

    def one_set(operands):
        query_block, cache_block, value_block, span_block, span_value_block = operands

        def cache_scores(start):
            key_block = lax.dynamic_slice_in_dim(cache_block, start, block_size, 0)
            doc_block = lax.dynamic_slice_in_dim(token_docs, start, block_size, 0)
            scores = jnp.dot(query_block, key_block.T, preferred_element_type=jnp.float32) * score_scale
            allowed = query_docs[:, None] == doc_block[None, :]
            return (scores, allowed)
        span_scores = jnp.dot(query_block, span_block.T, preferred_element_type=jnp.float32) * score_scale
        span_allowed = (query_docs[:, None] == row_docs[None, :]) & (row_ids[None, :] <= query_rows[:, None])
        highest = lax.optimization_barrier(jnp.max(jnp.where(span_allowed, span_scores, SCORE_FLOOR), axis=1))

        def max_pass(carry, start):
            scores, allowed = cache_scores(start)
            return (jnp.maximum(carry, lax.optimization_barrier(jnp.max(jnp.where(allowed, scores, SCORE_FLOOR), axis=1))), None)
        highest, _ = lax.scan(max_pass, highest, starts)
        span_weights = jnp.where(span_allowed, jnp.exp(span_scores - highest[:, None]), 0.0)
        totals = lax.optimization_barrier(jnp.sum(span_weights, axis=1))
        weighted = jnp.dot(span_weights.astype(jnp.bfloat16), span_value_block, preferred_element_type=jnp.float32)

        def sum_pass(carry, start):
            run_total, run_sum = carry
            scores, allowed = cache_scores(start)
            weights = jnp.where(allowed, jnp.exp(scores - highest[:, None]), 0.0)
            value_rows = lax.dynamic_slice_in_dim(value_block, start, block_size, 0)
            run_total = run_total + lax.optimization_barrier(jnp.sum(weights, axis=1))
            run_sum = run_sum + jnp.dot(weights.astype(jnp.bfloat16), value_rows, preferred_element_type=jnp.float32)
            return ((run_total, run_sum), None)
        (totals, weighted), _ = lax.scan(sum_pass, (totals, weighted), starts)
        return weighted / totals[:, None]
    outputs = lax.map(one_set, (query_sets, cache_sets, value_sets, span_sets, span_value_sets))
    return outputs.reshape(KVH, ROWS, per_group, HD).transpose(1, 0, 2, 3).reshape(ROWS, H * HD).astype(jnp.bfloat16)
```

```python
import functools
import math

import jax
import jax.numpy as jnp
import numpy as np
from jax import lax
from jax.experimental import pallas as pl
from jax.experimental.pallas import tpu as pltpu
from jax.sharding import PartitionSpec as P

HD = 128
GROUP = 4
X = 4
FLOOR = -1e30
MESH = pl.DeviceIdType.MESH
VMEM = pltpu.VMEM
SCALE = math.log2(math.e) / math.sqrt(HD)


def inverse_freq():
    counter = np.arange(HD // 2, dtype=np.float64)
    base = 500000.0 ** (-2.0 * counter / HD)
    wavelen = 2.0 * math.pi / base
    smooth = (8192.0 / wavelen - 1.0) / 3.0
    middle = (1.0 - smooth) * base / 8.0 + smooth * base
    freq = np.where(wavelen > 8192.0, base / 8.0, np.where(wavelen < 2048.0, base, middle))
    return np.concatenate([freq, freq]).astype(np.float32)[None, :]


class Place:
    def __init__(self, ctx_size, head_size):
        self.Y = ctx_size // 2
        self.Z = head_size // X
        ctx = lax.axis_index("ctx")
        head = lax.axis_index("head")
        self.ctx, self.head = ctx, head
        self.y = ctx // 2
        self.c = ctx % 2
        self.x = head // self.Z
        self.z = head % self.Z
        self.pair = self.x // 2
        self.hb = self.bit_of(self.x)
        self.k = 2 * self.y + self.hb
        self.sgn = 1 - 2 * self.c

    def bit_of(self, x):
        pair = x // 2
        return pair * 3 + x * (1 - 2 * pair)

    def dev(self, y=None, c=None, x=None, z=None):
        y = self.y if y is None else y
        c = self.c if c is None else c
        x = self.x if x is None else x
        z = self.z if z is None else z
        return (y * 2 + c, x * self.Z + z)

    def z_at(self, offset):
        return (self.z + self.sgn * offset + 2 * self.Z) % self.Z

    def along_z(self, offset):
        return self.dev(z=self.z_at(offset))

    def key_partner(self, d):
        k = (self.k + d) % (2 * self.Y)
        hb = k % 2
        x = self.pair * 3 + hb * (1 - 2 * self.pair)
        return k, self.dev(y=k // 2, x=x)


def barrier(devices):
    sem = pltpu.get_barrier_semaphore()
    for device in devices:
        pl.semaphore_signal(sem, inc=1, device_id=device, device_id_type=MESH)
    pl.semaphore_wait(sem, len(devices))


def remote(src, dst, send, recv, device):
    return pltpu.make_async_remote_copy(
        src_ref=src, dst_ref=dst, send_sem=send, recv_sem=recv, device_id=device, device_id_type=MESH
    )


def turn(data, cosine, sine):
    data = data.astype(jnp.float32)
    return (data * cosine + pltpu.roll(data, HD // 2, 1) * sine).astype(jnp.bfloat16)


def trig(place, freq):
    angle = place.astype(jnp.float32) * freq
    lane = lax.broadcasted_iota(jnp.int32, angle.shape, 1)
    sine = jnp.sin(angle)
    return jnp.cos(angle), jnp.where(lane < HD // 2, -sine, sine)


def ring_hops(Z):
    near, far = Z // 2 - 1, Z // 2
    hops = []
    for step in range(far):
        hops.append((0, step))
        if step < near:
            hops.append((1, step))
    return hops


def gather_kernel(
    sizes, cl, sl, freq_ref, q_ref, sk_ref, sv_ref, k_ref, v_ref,
    qo, ko, vo, sko, svo,
    q_in, sk_in, qs, sks, ks,
    q_in_sem, span_sem, v_send, v_recv, k_send, k_recv, x_send, x_recv, ring_send, ring_recv,
    core_send, core_recv, own_sem, pair_send, pair_recv,
):
    at = Place(*sizes)
    Y, Z = at.Y, at.Z
    heads = 2 * Y
    rows, tokens = q_ref.shape[0], k_ref.shape[0]
    ndoc = cl.shape[0]

    reads = []
    for hb in range(2):
        column = pl.multiple_of((2 * at.y + hb) * (GROUP * HD) + at.c * (2 * HD), 2 * HD)
        reads.append(
            pltpu.make_async_copy(q_ref.at[:, pl.ds(column, 2 * HD)], q_in.at[hb], q_in_sem.at[hb])
        )
    own = pl.multiple_of(at.k * HD, HD)
    theirs = pl.multiple_of((at.k + 1 - 2 * at.hb) * HD, HD)
    for i, column in enumerate((own, theirs)):
        reads.append(
            pltpu.make_async_copy(sk_ref.at[:, pl.ds(column, HD)], sk_in.at[i], span_sem.at[i])
        )
    for copy in reads:
        copy.start()
    sv_copy = pltpu.make_async_copy(sv_ref.at[:, pl.ds(own, HD)], svo.at[0], span_sem.at[2])
    sv_copy.start()
    v_own = pltpu.make_async_copy(v_ref.at[:, pl.ds(own, HD)], vo.at[at.k], own_sem.at[0])
    v_own.start()

    partners = [at.key_partner(d) for d in range(1, heads)]
    others = [at.dev(x=(at.x + dx) % X) for dx in range(1, X)]
    plus, minus = at.along_z(1), at.along_z(-1)
    other_core = at.dev(c=1 - at.c)
    outside = [at.dev(x=(at.x + 2) % X), at.dev(x=3 - at.x)]
    greet = [device for _, device in partners] + outside + [other_core, plus]
    if Z > 2:
        greet.append(minus)
    barrier(greet)

    order = sorted(range(1, heads), key=lambda d: -min(d, heads - d))
    v_copies = []
    for d in order:
        k, device = partners[d - 1]
        column = pl.multiple_of(k * HD, HD)
        copy = remote(
            v_ref.at[:, pl.ds(column, HD)], vo.at[at.k], v_send.at[d], v_recv.at[d], device
        )
        copy.start()
        v_copies.append(copy)

    freq = freq_ref[...]
    row = at.head * rows + lax.broadcasted_iota(jnp.int32, (rows, HD), 0)
    shift = jnp.zeros((rows, HD), jnp.int32)
    start = jnp.int32(0)
    for d in range(ndoc):
        shift = jnp.where(row >= start, cl[d] - start, shift)
        start = start + sl[d]
    cosine, sine = trig(row + shift, freq)
    for copy in reads:
        copy.wait()
    for hb in range(2):
        for h in range(2):
            qs[hb, h * rows : (h + 1) * rows, :] = turn(
                q_in[hb, :, h * HD : (h + 1) * HD], cosine, sine
            )
    sko[0] = turn(sk_in[0], cosine, sine)
    sks[...] = turn(sk_in[1], cosine, sine)

    x_copies = []
    for dx in range(1, X):
        x = (at.x + dx) % X
        copy = remote(
            qs.at[at.bit_of(x)], qo.at[at.c, at.z, at.x], x_send.at[dx], x_recv.at[dx], others[dx - 1]
        )
        copy.start()
        x_copies.append(copy)
    mate = at.dev(x=at.pair * 3 + (1 - at.hb) * (1 - 2 * at.pair))
    pair_copies = [
        remote(sks, sko.at[1], pair_send.at[0], pair_recv.at[0], mate),
        remote(sv_ref.at[:, pl.ds(theirs, HD)], svo.at[1], pair_send.at[1], pair_recv.at[1], mate),
    ]
    for copy in pair_copies:
        copy.start()
    q_own = pltpu.make_async_copy(qs.at[at.hb], qo.at[at.c, at.z, at.x], own_sem.at[1])
    q_own.start()

    def ring_copy(direction, step, n):
        offset = -step if direction == 0 else step
        x = (at.x - n + X) % X
        part = qo.at[at.c, at.z_at(offset), x]
        return remote(
            part, part, ring_send.at[direction, step, n], ring_recv.at[direction, step, n],
            plus if direction == 0 else minus,
        )

    def arrived(direction, step, n):
        offset = -(step + 1) if direction == 0 else step + 1
        x = (at.x - n + X) % X
        part = qo.at[at.c, at.z_at(offset), x]
        remote(
            part, part, ring_send.at[direction, step, n], ring_recv.at[direction, step, n], plus
        ).wait_recv()

    def core_copy(i, offset):
        slab = qo.at[at.c, at.z_at(offset)]
        return remote(slab, slab, core_send.at[i], core_recv.at[i], other_core)

    hops = ring_hops(Z)
    ring = []
    for n in range(X):
        if n == 0:
            q_own.wait()
        else:
            x_copies[n - 1].wait_recv()
        for direction in range(2):
            if (direction, 0) in hops:
                copy = ring_copy(direction, 0, n)
                copy.start()
                ring.append(copy)
    cores = [core_copy(0, 0)]
    cores[0].start()

    token = (at.ctx * sizes[1] + at.head) * tokens + lax.broadcasted_iota(jnp.int32, (tokens, HD), 0)
    first = jnp.zeros((tokens, HD), jnp.int32)
    start = jnp.int32(0)
    for d in range(ndoc):
        first = jnp.where(token >= start, start, first)
        start = start + cl[d]
    cosine, sine = trig(token - first, freq)
    k_copies = []
    for d in order:
        k, device = partners[d - 1]
        column = pl.multiple_of(k * HD, HD)
        ks[d - 1] = turn(k_ref[:, pl.ds(column, HD)], cosine, sine)
        copy = remote(ks.at[d - 1], ko.at[at.k], k_send.at[d], k_recv.at[d], device)
        copy.start()
        k_copies.append(copy)
    ko[at.k] = turn(k_ref[:, pl.ds(own, HD)], cosine, sine)

    for i, (direction, step) in enumerate(hops):
        onward = (direction, step + 1) in hops
        for n in range(X):
            arrived(direction, step, n)
            if onward:
                copy = ring_copy(direction, step + 1, n)
                copy.start()
                ring.append(copy)
        copy = core_copy(i + 1, -(step + 1) if direction == 0 else step + 1)
        copy.start()
        cores.append(copy)

    for i in range(Z):
        if i == 0:
            offset = 0
        else:
            direction, step = hops[i - 1]
            offset = (step + 1) if direction == 0 else -(step + 1)
        slab = qo.at[1 - at.c, at.z_at(offset)]
        remote(slab, slab, core_send.at[i], core_recv.at[i], other_core).wait_recv()
    for copy in v_copies + k_copies + pair_copies:
        copy.wait_recv()
    for copy in v_copies + k_copies + pair_copies + x_copies + ring + cores:
        copy.wait_send()
    v_own.wait()
    sv_copy.wait()


def attend_kernel(sizes, cl, sl, q_ref, k_ref, v_ref, sk_ref, sv_ref, part_ref, stat_ref, acc):
    at = Place(*sizes)
    Z = at.Z
    blocks, tokens, _ = k_ref.shape
    rows = q_ref.shape[3] // 2
    lanes = 4 * rows
    ndoc = cl.shape[0]

    half = lax.broadcasted_iota(jnp.int32, (2, Z, 2 * X, 2 * rows), 2)
    stat_ref[...] = jnp.where(half < X, FLOOR, 0.0)
    acc[...] = jnp.zeros_like(acc)
    lane = lax.broadcasted_iota(jnp.int32, (1, lanes), 1) % rows

    def absorb(keys, values_t, n, row_low, row_high, masked):
        x, z = n // Z, n % Z
        q = jnp.concatenate([q_ref[0, z, x], q_ref[1, z, x]], axis=0)
        s = lax.dot_general(
            keys, q, (((1,), (1,)), ((), ())), preferred_element_type=jnp.float32
        )
        row = n * rows + lane
        s = masked(s * SCALE, row)
        m_old = jnp.concatenate(
            [stat_ref[0, z, pl.ds(x, 1), :], stat_ref[1, z, pl.ds(x, 1), :]], axis=1
        )
        l_old = jnp.concatenate(
            [stat_ref[0, z, pl.ds(X + x, 1), :], stat_ref[1, z, pl.ds(X + x, 1), :]], axis=1
        )
        here = (row >= row_low) & (row < row_high)
        m_new = jnp.where(here, jnp.maximum(m_old, jnp.max(s, axis=0, keepdims=True)), m_old)
        w = jnp.exp2(s - jnp.where(here, m_new, -FLOOR))
        factor = jnp.exp2(m_old - m_new)
        l_new = l_old * factor + jnp.sum(w, axis=0, keepdims=True)
        o = jnp.dot(values_t, w.astype(jnp.bfloat16), preferred_element_type=jnp.float32)
        for c in range(2):
            part = slice(c * 2 * rows, (c + 1) * 2 * rows)
            stat_ref[c, z, pl.ds(x, 1), :] = m_new[:, part]
            stat_ref[c, z, pl.ds(X + x, 1), :] = l_new[:, part]
            acc[c, z, x] = acc[c, z, x] * factor[:, part] + o[:, part]

    def block_step(b, carry):
        first = (((b // 2) * 2 + at.c) * sizes[1] + (at.pair * 3 + (b % 2) * (1 - 2 * at.pair)) * Z + at.z) * tokens
        keys = k_ref[b]
        values_t = v_ref[b].T
        token = first + lax.broadcasted_iota(jnp.int32, (tokens, lanes), 0)

        def doc_step(d, carry):
            cache_start, span_start = carry
            cache_end, span_end = cache_start + cl[d], span_start + sl[d]
            overlap = (cache_end > first) & (cache_start < first + tokens)

            def masked(s, row):
                return jnp.where((token >= cache_start) & (token < cache_end), s, FLOOR)

            def chunk(n, carry):
                absorb(keys, values_t, n, span_start, span_end, masked)
                return carry

            low = span_start // rows
            high = jnp.where(overlap, (span_end + rows - 1) // rows, low)
            lax.fori_loop(low, high, chunk, 0)
            return cache_end, span_end

        lax.fori_loop(0, ndoc, doc_step, (jnp.int32(0), jnp.int32(0)))
        return carry

    lax.fori_loop(0, blocks, block_step, 0)

    mate = at.pair * 3 + (1 - at.hb) * (1 - 2 * at.pair)
    own_chunk = jnp.where(at.c == 0, at.x, mate) * Z + at.z
    first = own_chunk * rows
    keys = sk_ref[at.c]
    values_t = sv_ref[at.c].T
    token = first + lax.broadcasted_iota(jnp.int32, (rows, lanes), 0)

    def span_step(d, span_start):
        span_end = span_start + sl[d]
        overlap = (span_end > first) & (span_start < first + rows)

        def masked(s, row):
            return jnp.where((token >= span_start) & (token < span_end) & (token <= row), s, FLOOR)

        def chunk(n, carry):
            absorb(keys, values_t, n, jnp.maximum(span_start, first), span_end, masked)
            return carry

        low = own_chunk
        high = jnp.where(overlap, (span_end + rows - 1) // rows, low)
        lax.fori_loop(low, high, chunk, 0)
        return span_end

    lax.fori_loop(0, ndoc, span_step, jnp.int32(0))

    part_ref[...] = acc[...].astype(jnp.bfloat16)


def reduce_kernel(
    sizes, part_ref, stat_ref, out_ref,
    cr, cr_stat, sb, sb_stat, rb, rb_stat, fb, fb_stat, xr, xr_stat,
    core_send, core_recv, core_stat_send, core_stat_recv,
    ring_send, ring_recv, ring_stat_send, ring_stat_recv,
    x_send, x_recv, x_stat_send, x_stat_recv, out_send, out_recv, own_sem,
):
    at = Place(*sizes)
    Y, Z = at.Y, at.Z
    rows = out_ref.shape[0]
    others = [at.dev(x=(at.x + dx) % X) for dx in range(1, X)]
    plus, minus = at.along_z(1), at.along_z(-1)
    other_core = at.dev(c=1 - at.c)
    ends = [
        at.dev(y=(at.y + dy) % Y, c=(at.c + dc) % 2)
        for dc in range(2)
        for dy in range(Y)
        if dy or dc
    ]
    greet = others + ends + [plus]
    if Z > 2:
        greet.append(minus)
    barrier(greet)

    hops = ring_hops(Z)

    def slab_offset(direction, step):
        return Z // 2 - step if direction == 0 else -(Z // 2 - 1 - step)

    offsets = [slab_offset(*hop) for hop in hops] + [0]
    sent = []
    for i, offset in enumerate(offsets):
        z = at.z_at(-offset)
        a = remote(
            stat_ref.at[1 - at.c, z], cr_stat.at[z], core_stat_send.at[i], core_stat_recv.at[i],
            other_core,
        )
        b = remote(part_ref.at[1 - at.c, z], cr.at[z], core_send.at[i], core_recv.at[i], other_core)
        a.start()
        b.start()
        sent += [a, b]

    def from_core(i, offset):
        z = at.z_at(offset)
        remote(
            stat_ref.at[at.c, z], cr_stat.at[z], core_stat_send.at[i], core_stat_recv.at[i], other_core
        ).wait_recv()
        remote(
            part_ref.at[at.c, z], cr.at[z], core_send.at[i], core_recv.at[i], other_core
        ).wait_recv()
        return [(part_ref.at[at.c, z], stat_ref.at[at.c, z]), (cr.at[z], cr_stat.at[z])]

    def ring_in(direction, step, x):
        if x is None:
            remote(
                sb_stat.at[direction, step], rb_stat.at[direction, step],
                ring_stat_send.at[direction, step], ring_stat_recv.at[direction, step], plus,
            ).wait_recv()
        else:
            remote(
                sb.at[direction, step, x], rb.at[direction, step, x],
                ring_send.at[direction, step, x], ring_recv.at[direction, step, x], plus,
            ).wait_recv()

    def join(sources, came, to, to_stat, emit_stat, emit):
        for direction, step in came:
            ring_in(direction, step, None)
            sources = sources + [(rb.at[direction, step], rb_stat.at[direction, step])]
        stats = [stat[...] for _, stat in sources]
        top = functools.reduce(jnp.maximum, [s[:X] for s in stats])
        factors = [jnp.exp2(s[:X] - top) for s in stats]
        to_stat[:X, :] = top
        to_stat[X:, :] = sum(s[X:] * f for s, f in zip(stats, factors))
        emit_stat()
        for x in range(X):
            for direction, step in came:
                ring_in(direction, step, x)
            to[x] = sum(
                part[x].astype(jnp.float32) * f[x : x + 1] for (part, _), f in zip(sources, factors)
            ).astype(jnp.bfloat16)
            emit(x)

    for i, (direction, step) in enumerate(hops):
        device = plus if direction == 0 else minus

        def emit_stat():
            copy = remote(
                sb_stat.at[direction, step], rb_stat.at[direction, step],
                ring_stat_send.at[direction, step], ring_stat_recv.at[direction, step], device,
            )
            copy.start()
            sent.append(copy)

        def emit(x):
            copy = remote(
                sb.at[direction, step, x], rb.at[direction, step, x],
                ring_send.at[direction, step, x], ring_recv.at[direction, step, x], device,
            )
            copy.start()
            sent.append(copy)

        join(
            from_core(i, slab_offset(direction, step)),
            [(direction, step - 1)] if step else [],
            sb.at[direction, step], sb_stat.at[direction, step], emit_stat, emit,
        )

    came = [(0, Z // 2 - 1)] + ([(1, Z // 2 - 2)] if Z > 2 else [])
    join(from_core(Z - 1, 0), came, fb, fb_stat, lambda: None, lambda x: None)
    x_copies = []
    for dx in range(1, X):
        x = (at.x + dx) % X
        a = remote(fb_stat, xr_stat.at[at.x], x_stat_send.at[dx], x_stat_recv.at[dx], others[dx - 1])
        b = remote(fb.at[x], xr.at[at.x], x_send.at[dx], x_recv.at[dx], others[dx - 1])
        a.start()
        b.start()
        sent += [a, b]
        x_copies += [a, b]
    own = [
        pltpu.make_async_copy(fb.at[at.x], xr.at[at.x], own_sem.at[0]),
        pltpu.make_async_copy(fb_stat, xr_stat.at[at.x], own_sem.at[1]),
    ]
    for copy in own:
        copy.start()
    for copy in own:
        copy.wait()
    for copy in x_copies:
        copy.wait_recv()

    outs = []
    for hb, (one, two) in enumerate(((0, 3), (1, 2))):
        tops = [xr_stat[n, pl.ds(at.x, 1), :] for n in (one, two)]
        totals = [xr_stat[n, pl.ds(X + at.x, 1), :] for n in (one, two)]
        top = jnp.maximum(*tops)
        factors = [jnp.exp2(t - top) for t in tops]
        total = totals[0] * factors[0] + totals[1] * factors[1]
        value = xr[one].astype(jnp.float32) * factors[0] + xr[two].astype(jnp.float32) * factors[1]
        value = (value / total).T.astype(jnp.bfloat16)
        for h in range(2):
            column = pl.multiple_of((2 * at.y + hb) * (GROUP * HD) + at.c * (2 * HD) + h * HD, HD)
            out_ref[:, pl.ds(column, HD)] = value[h * rows : (h + 1) * rows]
        column = pl.multiple_of((2 * at.y + hb) * (GROUP * HD) + at.c * (2 * HD), 2 * HD)
        part = out_ref.at[:, pl.ds(column, 2 * HD)]
        for i, device in enumerate(ends):
            copy = remote(part, part, out_send.at[hb, i], out_recv.at[hb, i], device)
            copy.start()
            sent.append(copy)
    for hb in range(2):
        i = 0
        for dc in range(2):
            for dy in range(Y):
                if dy or dc:
                    y, c = (at.y - dy + Y) % Y, (at.c - dc + 2) % 2
                    column = pl.multiple_of((2 * y + hb) * (GROUP * HD) + c * (2 * HD), 2 * HD)
                    part = out_ref.at[:, pl.ds(column, 2 * HD)]
                    remote(part, part, out_send.at[hb, i], out_recv.at[hb, i], other_core).wait_recv()
                    i += 1
    for copy in sent:
        copy.wait_send()


def body(queries, span_keys, span_values, cache_keys, cache_values, cache_lengths, span_lengths):
    sizes = (lax.axis_size("ctx"), lax.axis_size("head"))
    Y, Z = sizes[0] // 2, sizes[1] // X
    heads = 2 * Y
    rows, tokens = queries.shape[0], cache_keys.shape[0]
    bf16, f32 = jnp.bfloat16, jnp.float32
    smem = pl.BlockSpec(memory_space=pltpu.SMEM)
    vmem = pl.BlockSpec(memory_space=pltpu.VMEM)
    hbm = pl.BlockSpec(memory_space=pl.ANY)
    dma = pltpu.SemaphoreType.DMA
    freq = jnp.asarray(inverse_freq())
    half = Z // 2

    q_all, k_all, v_all, sk, sv = pl.pallas_call(
        functools.partial(gather_kernel, sizes),
        out_shape=(
            jax.ShapeDtypeStruct((2, Z, X, 2 * rows, HD), bf16),
            jax.ShapeDtypeStruct((heads, tokens, HD), bf16),
            jax.ShapeDtypeStruct((heads, tokens, HD), bf16),
            jax.ShapeDtypeStruct((2, rows, HD), bf16),
            jax.ShapeDtypeStruct((2, rows, HD), bf16),
        ),
        in_specs=[smem, smem, vmem, hbm, hbm, hbm, vmem, hbm],
        out_specs=(vmem,) * 5,
        scratch_shapes=[
            VMEM((2, rows, 2 * HD), bf16),
            VMEM((2, rows, HD), bf16),
            VMEM((2, 2 * rows, HD), bf16),
            VMEM((rows, HD), bf16),
            VMEM((heads - 1, tokens, HD), bf16),
            dma((2,)), dma((3,)), dma((heads,)), dma((heads,)), dma((heads,)), dma((heads,)),
            dma((X,)), dma((X,)), dma((2, half, X)), dma((2, half, X)), dma((Z,)), dma((Z,)),
            dma((2,)), dma((2,)), dma((2,)),
        ],
        compiler_params=pltpu.CompilerParams(
            collective_id=0, has_side_effects=True, vmem_limit_bytes=40 * 1024 * 1024
        ),
        name="gather",
    )(cache_lengths, span_lengths, freq, queries, span_keys, span_values, cache_keys, cache_values)

    parts, stats = pl.pallas_call(
        functools.partial(attend_kernel, sizes),
        out_shape=(
            jax.ShapeDtypeStruct((2, Z, X, HD, 2 * rows), bf16),
            jax.ShapeDtypeStruct((2, Z, 2 * X, 2 * rows), f32),
        ),
        in_specs=[smem, smem] + [vmem] * 5,
        out_specs=(vmem, vmem),
        scratch_shapes=[VMEM((2, Z, X, HD, 2 * rows), f32)],
        compiler_params=pltpu.CompilerParams(vmem_limit_bytes=40 * 1024 * 1024),
        name="attend",
    )(cache_lengths, span_lengths, q_all, k_all, v_all, sk, sv)

    piece, stat = (HD, 2 * rows), (2 * X, 2 * rows)
    return pl.pallas_call(
        functools.partial(reduce_kernel, sizes),
        out_shape=jax.ShapeDtypeStruct(queries.shape, bf16),
        in_specs=[vmem, vmem],
        out_specs=vmem,
        scratch_shapes=[
            VMEM((Z, X) + piece, bf16), VMEM((Z,) + stat, f32),
            VMEM((2, half, X) + piece, bf16), VMEM((2, half) + stat, f32),
            VMEM((2, half, X) + piece, bf16), VMEM((2, half) + stat, f32),
            VMEM((X,) + piece, bf16), VMEM(stat, f32),
            VMEM((X,) + piece, bf16), VMEM((X,) + stat, f32),
            dma((Z,)), dma((Z,)), dma((Z,)), dma((Z,)),
            dma((2, half, X)), dma((2, half, X)), dma((2, half)), dma((2, half)),
            dma((X,)), dma((X,)), dma((X,)), dma((X,)),
            dma((2, 2 * Y)), dma((2, 2 * Y)), dma((2,)),
        ],
        compiler_params=pltpu.CompilerParams(
            collective_id=1, has_side_effects=True, vmem_limit_bytes=40 * 1024 * 1024
        ),
        name="reduce",
    )(parts, stats)


def solution(mesh):
    placed = (
        P("head", None),
        P("head", None),
        P("head", None),
        P(("ctx", "head"), None),
        P(("ctx", "head"), None),
        P(),
        P(),
    )
    return jax.shard_map(
        body, mesh=mesh, in_specs=placed, out_specs=P("head", None), check_vma=False
    )
```

```python
import functools
import math

import jax
import jax.numpy as jnp
import numpy as np
from jax import lax
from jax.experimental import pallas as pl
from jax.experimental.pallas import tpu as pltpu
from jax.sharding import PartitionSpec as P

HD = 128
GROUP = 4
X = 4
FLOOR = -1e30
MESH = pl.DeviceIdType.MESH
VMEM = pltpu.VMEM
SCALE = math.log2(math.e) / math.sqrt(HD)


def inverse_freq():
    counter = np.arange(HD // 2, dtype=np.float64)
    base = 500000.0 ** (-2.0 * counter / HD)
    wavelen = 2.0 * math.pi / base
    smooth = (8192.0 / wavelen - 1.0) / 3.0
    middle = (1.0 - smooth) * base / 8.0 + smooth * base
    freq = np.where(wavelen > 8192.0, base / 8.0, np.where(wavelen < 2048.0, base, middle))
    return np.concatenate([freq, freq]).astype(np.float32)[None, :]


class Place:
    def __init__(self, ctx_size, head_size):
        self.Y = ctx_size // 2
        self.Z = head_size // X
        ctx = lax.axis_index("ctx")
        head = lax.axis_index("head")
        self.ctx, self.head = ctx, head
        self.y = ctx // 2
        self.c = ctx % 2
        self.x = head // self.Z
        self.z = head % self.Z
        self.pair = self.x // 2
        self.hb = self.bit_of(self.x)
        self.k = 2 * self.y + self.hb
        self.sgn = 1 - 2 * self.c

    def bit_of(self, x):
        pair = x // 2
        return pair * 3 + x * (1 - 2 * pair)

    def dev(self, y=None, c=None, x=None, z=None):
        y = self.y if y is None else y
        c = self.c if c is None else c
        x = self.x if x is None else x
        z = self.z if z is None else z
        return (y * 2 + c, x * self.Z + z)

    def z_at(self, offset):
        return (self.z + self.sgn * offset + 2 * self.Z) % self.Z

    def along_z(self, offset):
        return self.dev(z=self.z_at(offset))

    def key_partner(self, d):
        k = (self.k + d) % (2 * self.Y)
        hb = k % 2
        x = self.pair * 3 + hb * (1 - 2 * self.pair)
        return k, self.dev(y=k // 2, x=x)


def barrier(devices):
    sem = pltpu.get_barrier_semaphore()
    for device in devices:
        pl.semaphore_signal(sem, inc=1, device_id=device, device_id_type=MESH)
    pl.semaphore_wait(sem, len(devices))


def remote(src, dst, send, recv, device):
    return pltpu.make_async_remote_copy(
        src_ref=src, dst_ref=dst, send_sem=send, recv_sem=recv, device_id=device, device_id_type=MESH
    )


def turn(data, cosine, sine):
    data = data.astype(jnp.float32)
    return (data * cosine + pltpu.roll(data, HD // 2, 1) * sine).astype(jnp.bfloat16)


def trig(place, freq):
    angle = place.astype(jnp.float32) * freq
    lane = lax.broadcasted_iota(jnp.int32, angle.shape, 1)
    sine = jnp.sin(angle)
    return jnp.cos(angle), jnp.where(lane < HD // 2, -sine, sine)


def ring_hops(Z):
    near, far = Z // 2 - 1, Z // 2
    hops = []
    for step in range(far):
        hops.append((0, step))
        if step < near:
            hops.append((1, step))
    return hops


def gather_kernel(
    sizes, cl_ref, sl_ref, freq_ref, q_ref, sk_ref, sv_ref, k_ref, v_ref,
    qo, ko, vo, sko, svo,
    cl, sl, freq_in, k_in, q_in, sk_in, qs, sks, ks, in_sem,
    q_in_sem, span_sem, v_send, v_recv, k_send, k_recv, x_send, x_recv, ring_send, ring_recv,
    core_send, core_recv, own_sem, pair_send, pair_recv,
):
    at = Place(*sizes)
    Y, Z = at.Y, at.Z
    heads = 2 * Y
    rows, tokens = q_ref.shape[0], k_ref.shape[0]
    ndoc = cl.shape[0]

    reads = [
        pltpu.make_async_copy(cl_ref, cl, in_sem.at[0]),
        pltpu.make_async_copy(sl_ref, sl, in_sem.at[1]),
        pltpu.make_async_copy(freq_ref, freq_in, in_sem.at[2]),
    ]
    k_read = pltpu.make_async_copy(k_ref, k_in, in_sem.at[3])
    for hb in range(2):
        column = pl.multiple_of((2 * at.y + hb) * (GROUP * HD) + at.c * (2 * HD), 2 * HD)
        reads.append(
            pltpu.make_async_copy(q_ref.at[:, pl.ds(column, 2 * HD)], q_in.at[hb], q_in_sem.at[hb])
        )
    own = pl.multiple_of(at.k * HD, HD)
    theirs = pl.multiple_of((at.k + 1 - 2 * at.hb) * HD, HD)
    for i, column in enumerate((own, theirs)):
        reads.append(
            pltpu.make_async_copy(sk_ref.at[:, pl.ds(column, HD)], sk_in.at[i], span_sem.at[i])
        )
    for copy in reads:
        copy.start()
    k_read.start()
    sv_copy = pltpu.make_async_copy(sv_ref.at[:, pl.ds(own, HD)], svo.at[0], span_sem.at[2])
    sv_copy.start()
    v_own = pltpu.make_async_copy(v_ref.at[:, pl.ds(own, HD)], vo.at[at.k], own_sem.at[0])
    v_own.start()

    partners = [at.key_partner(d) for d in range(1, heads)]
    others = [at.dev(x=(at.x + dx) % X) for dx in range(1, X)]
    plus, minus = at.along_z(1), at.along_z(-1)
    other_core = at.dev(c=1 - at.c)
    outside = [at.dev(x=(at.x + 2) % X), at.dev(x=3 - at.x)]
    greet = [device for _, device in partners] + outside + [other_core, plus]
    if Z > 2:
        greet.append(minus)
    barrier(greet)

    order = sorted(range(1, heads), key=lambda d: -min(d, heads - d))
    v_copies = []
    for d in order:
        k, device = partners[d - 1]
        column = pl.multiple_of(k * HD, HD)
        copy = remote(
            v_ref.at[:, pl.ds(column, HD)], vo.at[at.k], v_send.at[d], v_recv.at[d], device
        )
        copy.start()
        v_copies.append(copy)

    for copy in reads:
        copy.wait()
    freq = freq_in[...]
    row = at.head * rows + lax.broadcasted_iota(jnp.int32, (rows, HD), 0)
    shift = jnp.zeros((rows, HD), jnp.int32)
    start = jnp.int32(0)
    for d in range(ndoc):
        shift = jnp.where(row >= start, cl[d] - start, shift)
        start = start + sl[d]
    cosine, sine = trig(row + shift, freq)
    for hb in range(2):
        for h in range(2):
            qs[hb, h * rows : (h + 1) * rows, :] = turn(
                q_in[hb, :, h * HD : (h + 1) * HD], cosine, sine
            )
    sko[0] = turn(sk_in[0], cosine, sine)
    sks[...] = turn(sk_in[1], cosine, sine)

    x_copies = []
    for dx in range(1, X):
        x = (at.x + dx) % X
        copy = remote(
            qs.at[at.bit_of(x)], qo.at[at.c, at.z, at.x], x_send.at[dx], x_recv.at[dx], others[dx - 1]
        )
        copy.start()
        x_copies.append(copy)
    mate = at.dev(x=at.pair * 3 + (1 - at.hb) * (1 - 2 * at.pair))
    pair_copies = [
        remote(sks, sko.at[1], pair_send.at[0], pair_recv.at[0], mate),
        remote(sv_ref.at[:, pl.ds(theirs, HD)], svo.at[1], pair_send.at[1], pair_recv.at[1], mate),
    ]
    for copy in pair_copies:
        copy.start()
    q_own = pltpu.make_async_copy(qs.at[at.hb], qo.at[at.c, at.z, at.x], own_sem.at[1])
    q_own.start()

    def ring_copy(direction, step, n):
        offset = -step if direction == 0 else step
        x = (at.x - n + X) % X
        part = qo.at[at.c, at.z_at(offset), x]
        return remote(
            part, part, ring_send.at[direction, step, n], ring_recv.at[direction, step, n],
            plus if direction == 0 else minus,
        )

    def arrived(direction, step, n):
        offset = -(step + 1) if direction == 0 else step + 1
        x = (at.x - n + X) % X
        part = qo.at[at.c, at.z_at(offset), x]
        remote(
            part, part, ring_send.at[direction, step, n], ring_recv.at[direction, step, n], plus
        ).wait_recv()

    def core_copy(i, offset):
        slab = qo.at[at.c, at.z_at(offset)]
        return remote(slab, slab, core_send.at[i], core_recv.at[i], other_core)

    hops = ring_hops(Z)
    ring = []
    for n in range(X):
        if n == 0:
            q_own.wait()
        else:
            x_copies[n - 1].wait_recv()
        for direction in range(2):
            if (direction, 0) in hops:
                copy = ring_copy(direction, 0, n)
                copy.start()
                ring.append(copy)
    cores = [core_copy(0, 0)]
    cores[0].start()

    token = (at.ctx * sizes[1] + at.head) * tokens + lax.broadcasted_iota(jnp.int32, (tokens, HD), 0)
    first = jnp.zeros((tokens, HD), jnp.int32)
    start = jnp.int32(0)
    for d in range(ndoc):
        first = jnp.where(token >= start, start, first)
        start = start + cl[d]
    cosine, sine = trig(token - first, freq)
    k_read.wait()
    k_copies = []
    for d in order:
        k, device = partners[d - 1]
        column = pl.multiple_of(k * HD, HD)
        ks[d - 1] = turn(k_in[:, pl.ds(column, HD)], cosine, sine)
        copy = remote(ks.at[d - 1], ko.at[at.k], k_send.at[d], k_recv.at[d], device)
        copy.start()
        k_copies.append(copy)
    ko[at.k] = turn(k_in[:, pl.ds(own, HD)], cosine, sine)

    for step in range(Z // 2):
        both = [direction for direction in range(2) if (direction, step) in hops]
        for n in range(X):
            for direction in both:
                arrived(direction, step, n)
                if (direction, step + 1) in hops:
                    copy = ring_copy(direction, step + 1, n)
                    copy.start()
                    ring.append(copy)
        for direction in both:
            i = hops.index((direction, step))
            copy = core_copy(i + 1, -(step + 1) if direction == 0 else step + 1)
            copy.start()
            cores.append(copy)

    for i in range(Z):
        if i == 0:
            offset = 0
        else:
            direction, step = hops[i - 1]
            offset = (step + 1) if direction == 0 else -(step + 1)
        slab = qo.at[1 - at.c, at.z_at(offset)]
        remote(slab, slab, core_send.at[i], core_recv.at[i], other_core).wait_recv()
    for copy in v_copies + k_copies + pair_copies:
        copy.wait_recv()
    for copy in v_copies + k_copies + pair_copies + x_copies + ring + cores:
        copy.wait_send()
    v_own.wait()
    sv_copy.wait()


def attend_kernel(
    sizes, cl_ref, sl_ref, q_hbm, k_hbm, v_hbm, sk_hbm, sv_hbm, part_ref, stat_ref,
    acc, cl, sl, q_ref, k_ref, v_ref, vt_ref, s_even, s_odd, w_odd, f_odd,
    cache_at, span_at, g_block, g_low, g_high, g_first, g_end, g_causal, e_group, e_chunk, in_sem,
):
    at = Place(*sizes)
    Z = at.Z
    blocks, tokens, _ = k_hbm.shape
    rows = sk_hbm.shape[1]
    lanes = 4 * rows
    ndoc = cl.shape[0]
    pairs = (
        (cl_ref, cl), (sl_ref, sl), (k_hbm, k_ref.at[pl.ds(0, blocks)]),
        (q_hbm, q_ref), (v_hbm, v_ref.at[pl.ds(0, blocks)]),
        (sk_hbm.at[at.c], k_ref.at[blocks, pl.ds(0, rows)]),
        (sv_hbm.at[at.c], v_ref.at[blocks, pl.ds(0, rows)]),
    )
    reads = [pltpu.make_async_copy(a, b, in_sem.at[i]) for i, (a, b) in enumerate(pairs)]
    for copy in reads:
        copy.start()

    k_ref[blocks, rows:, :] = jnp.zeros((tokens - rows, HD), jnp.bfloat16)
    v_ref[blocks, rows:, :] = jnp.zeros((tokens - rows, HD), jnp.bfloat16)
    half = lax.broadcasted_iota(jnp.int32, (2, Z, 2 * X, 2 * rows), 2)
    stat_ref[...] = jnp.where(half < X, FLOOR, 0.0)
    acc[...] = jnp.zeros_like(acc)
    w_odd[...] = jnp.zeros_like(w_odd)
    f_odd[...] = jnp.ones_like(f_odd)
    reads[0].wait()
    reads[1].wait()

    cache_at[0] = jnp.int32(0)
    span_at[0] = jnp.int32(0)
    for d in range(ndoc):
        cache_at[d + 1] = cache_at[d] + cl[d]
        span_at[d + 1] = span_at[d] + sl[d]

    far = jnp.int32(1 << 20)

    def none(group):
        g_block[group], g_low[group], g_high[group] = jnp.int32(0), jnp.int32(0), jnp.int32(0)
        g_first[group], g_end[group], g_causal[group] = jnp.int32(0), jnp.int32(0), far

    none(0)
    e_group[0], e_chunk[0] = jnp.int32(0), jnp.int32(0)

    def add_block(counts, block, starts, first, width, causal, row_first):
        doc_first, doc_last = jnp.int32(0), jnp.int32(0)
        for d in range(1, ndoc):
            doc_first += (starts[d] <= first).astype(jnp.int32)
            doc_last += (starts[d] < first + width).astype(jnp.int32)

        def add_doc(d, counts):
            group, entry = counts
            g_block[group] = block
            g_low[group] = jnp.maximum(starts[d] - first, 0)
            g_high[group] = jnp.minimum(starts[d + 1] - first, width)
            g_first[group] = jnp.maximum(span_at[d], row_first)
            g_end[group] = span_at[d + 1]
            g_causal[group] = causal
            low = jnp.maximum(span_at[d], row_first) // rows
            high = (span_at[d + 1] + rows - 1) // rows

            def add_chunk(n, entry):
                e_group[entry] = group
                e_chunk[entry] = n
                return entry + 1

            return group + 1, lax.fori_loop(low, high, add_chunk, entry)

        return lax.fori_loop(doc_first, doc_last + 1, add_doc, counts)

    def cache_block(b, counts):
        x = at.pair * 3 + (b % 2) * (1 - 2 * at.pair)
        first = (((b // 2) * 2 + at.c) * sizes[1] + x * Z + at.z) * tokens
        return add_block(counts, b, cache_at, first, tokens, far, 0)

    counts = lax.fori_loop(0, blocks, cache_block, (jnp.int32(1), jnp.int32(1)))
    mate = at.pair * 3 + (1 - at.hb) * (1 - 2 * at.pair)
    first = (jnp.where(at.c == 0, at.x, mate) * Z + at.z) * rows
    _, count = add_block(counts, jnp.int32(blocks), span_at, first, rows, -first, first)
    for i in range(4):
        e_group[count + i], e_chunk[count + i] = jnp.int32(0), jnp.int32(0)

    for copy in reads[2:]:
        copy.wait()

    def turn_over(b, carry):
        vt_ref[b] = v_ref[b].T
        return carry

    lax.fori_loop(0, blocks + 1, turn_over, 0)

    lane = lax.broadcasted_iota(jnp.int32, (1, lanes), 1) % rows
    token = lax.broadcasted_iota(jnp.int32, (tokens, lanes), 0)

    def scores(i):
        n = e_chunk[i]
        x, z = n // Z, n % Z
        q = jnp.concatenate([q_ref[0, z, x], q_ref[1, z, x]], axis=0)
        return lax.dot_general(
            k_ref[g_block[e_group[i]]], q, (((1,), (1,)), ((), ())),
            preferred_element_type=jnp.float32,
        )

    def soften(i, s):
        group, n = e_group[i], e_chunk[i]
        x, z = n // Z, n % Z
        row = n * rows + lane
        here = (row >= g_first[group]) & (row < g_end[group])
        high = jnp.minimum(g_high[group], row + g_causal[group] + 1)
        s = jnp.where((token >= g_low[group]) & (token < high), s * SCALE, FLOOR)
        m_old = jnp.concatenate([stat_ref[c, z, pl.ds(x, 1), :] for c in range(2)], axis=1)
        l_old = jnp.concatenate([stat_ref[c, z, pl.ds(X + x, 1), :] for c in range(2)], axis=1)
        m_new = jnp.where(here, jnp.maximum(m_old, jnp.max(s, axis=0, keepdims=True)), m_old)
        w = jnp.exp2(s - jnp.where(here, m_new, -FLOOR))
        factor = jnp.exp2(m_old - m_new)
        l_new = l_old * factor + jnp.sum(w, axis=0, keepdims=True)
        for c in range(2):
            part = slice(c * 2 * rows, (c + 1) * 2 * rows)
            stat_ref[c, z, pl.ds(x, 1), :] = m_new[:, part]
            stat_ref[c, z, pl.ds(X + x, 1), :] = l_new[:, part]
        return w.astype(jnp.bfloat16), factor

    def product(i, w):
        return jnp.dot(vt_ref[g_block[e_group[i]]], w, preferred_element_type=jnp.float32)

    def update(i, o, factor):
        n = e_chunk[i]
        x, z = n // Z, n % Z
        for c in range(2):
            part = slice(c * 2 * rows, (c + 1) * 2 * rows)
            acc[c, z, x] = acc[c, z, x] * factor[:, part] + o[:, part]

    s_even[...] = scores(1)

    def step(j, carry):
        i = 2 * j + 1
        s_odd[...] = scores(i + 1)
        o_before = product(i - 1, w_odd[...])
        w, factor = soften(i, s_even[...])
        update(i - 1, o_before, f_odd[...])
        s_even[...] = scores(i + 2)
        o = product(i, w)
        w_next, factor_next = soften(i + 1, s_odd[...])
        update(i, o, factor)
        w_odd[...] = w_next
        f_odd[...] = factor_next
        return carry

    steps = count // 2
    lax.fori_loop(0, steps, step, 0)
    update(2 * steps, product(2 * steps, w_odd[...]), f_odd[...])
    part_ref[...] = acc[...].astype(jnp.bfloat16)


def reduce_kernel(
    sizes, part_hbm, stat_hbm, out_ref,
    part_ref, stat_ref, cr, cr_stat, sb, sb_stat, rb, rb_stat, fb, fb_stat, xr, xr_stat,
    core_send, core_recv, core_stat_send, core_stat_recv,
    ring_send, ring_recv, ring_stat_send, ring_stat_recv,
    x_send, x_recv, x_stat_send, x_stat_recv, out_send, out_recv, own_sem, in_sem,
):
    at = Place(*sizes)
    Y, Z = at.Y, at.Z
    rows = out_ref.shape[0]
    reads = [
        pltpu.make_async_copy(stat_hbm.at[at.c], stat_ref, in_sem.at[0]),
        pltpu.make_async_copy(part_hbm.at[at.c], part_ref, in_sem.at[1]),
    ]
    for copy in reads:
        copy.start()
    others = [at.dev(x=(at.x + dx) % X) for dx in range(1, X)]
    plus, minus = at.along_z(1), at.along_z(-1)
    other_core = at.dev(c=1 - at.c)
    ends = [
        at.dev(y=(at.y + dy) % Y, c=(at.c + dc) % 2)
        for dc in range(2)
        for dy in range(Y)
        if dy or dc
    ]
    greet = others + ends + [plus]
    if Z > 2:
        greet.append(minus)
    barrier(greet)

    hops = ring_hops(Z)

    def slab_offset(direction, step):
        return Z // 2 - step if direction == 0 else -(Z // 2 - 1 - step)

    offsets = [slab_offset(*hop) for hop in hops] + [0]
    sent = []
    for i, offset in enumerate(offsets):
        z = at.z_at(-offset)
        a = remote(
            stat_hbm.at[1 - at.c, z], cr_stat.at[z], core_stat_send.at[i], core_stat_recv.at[i],
            other_core,
        )
        b = remote(part_hbm.at[1 - at.c, z], cr.at[z], core_send.at[i], core_recv.at[i], other_core)
        a.start()
        b.start()
        sent += [a, b]

    def from_core(i, offset):
        z = at.z_at(offset)
        remote(
            stat_ref.at[z], cr_stat.at[z], core_stat_send.at[i], core_stat_recv.at[i], other_core
        ).wait_recv()
        remote(
            part_ref.at[z], cr.at[z], core_send.at[i], core_recv.at[i], other_core
        ).wait_recv()
        return [(part_ref.at[z], stat_ref.at[z]), (cr.at[z], cr_stat.at[z])]

    def ring_in(direction, step, x):
        if x is None:
            remote(
                sb_stat.at[direction, step], rb_stat.at[direction, step],
                ring_stat_send.at[direction, step], ring_stat_recv.at[direction, step], plus,
            ).wait_recv()
        else:
            remote(
                sb.at[direction, step, x], rb.at[direction, step, x],
                ring_send.at[direction, step, x], ring_recv.at[direction, step, x], plus,
            ).wait_recv()

    def join(sources, came, to, to_stat, emit):
        for direction, step in came:
            ring_in(direction, step, None)
            sources = sources + [(rb.at[direction, step], rb_stat.at[direction, step])]
        stats = [stat[...] for _, stat in sources]
        top = functools.reduce(jnp.maximum, [s[:X] for s in stats])
        factors = [jnp.exp2(s[:X] - top) for s in stats]
        to_stat[:X, :] = top
        to_stat[X:, :] = sum(s[X:] * f for s, f in zip(stats, factors))
        emit(None)

        def piece(x):
            for direction, step in came:
                ring_in(direction, step, x)
            to[x] = sum(
                part[x].astype(jnp.float32) * f[x : x + 1] for (part, _), f in zip(sources, factors)
            ).astype(jnp.bfloat16)
            emit(x)

        return piece

    def ring_out(direction, step):
        device = plus if direction == 0 else minus

        def emit(x):
            if x is None:
                copy = remote(
                    sb_stat.at[direction, step], rb_stat.at[direction, step],
                    ring_stat_send.at[direction, step], ring_stat_recv.at[direction, step], device,
                )
            else:
                copy = remote(
                    sb.at[direction, step, x], rb.at[direction, step, x],
                    ring_send.at[direction, step, x], ring_recv.at[direction, step, x], device,
                )
            copy.start()
            sent.append(copy)

        return emit

    for copy in reads:
        copy.wait()
    for step in range(Z // 2):
        pieces = [
            join(
                from_core(i, slab_offset(*hop)), [(hop[0], step - 1)] if step else [],
                sb.at[hop[0], step], sb_stat.at[hop[0], step], ring_out(*hop),
            )
            for i, hop in enumerate(hops)
            if hop[1] == step
        ]
        for x in range(X):
            for piece in pieces:
                piece(x)

    came = [(0, Z // 2 - 1)] + ([(1, Z // 2 - 2)] if Z > 2 else [])
    piece = join(from_core(Z - 1, 0), came, fb, fb_stat, lambda x: None)
    x_copies = []
    for dx in range(1, X):
        copy = remote(
            fb_stat, xr_stat.at[at.x], x_stat_send.at[dx], x_stat_recv.at[dx], others[dx - 1]
        )
        copy.start()
        x_copies.append(copy)
    for x in range(X):
        piece(x)
    for dx in range(1, X):
        x = (at.x + dx) % X
        copy = remote(fb.at[x], xr.at[at.x], x_send.at[dx], x_recv.at[dx], others[dx - 1])
        copy.start()
        x_copies.append(copy)
    sent += x_copies
    own = [
        pltpu.make_async_copy(fb.at[at.x], xr.at[at.x], own_sem.at[0]),
        pltpu.make_async_copy(fb_stat, xr_stat.at[at.x], own_sem.at[1]),
    ]
    for copy in own:
        copy.start()
    for copy in own:
        copy.wait()
    for copy in x_copies:
        copy.wait_recv()

    outs = []
    for hb, (one, two) in enumerate(((0, 3), (1, 2))):
        tops = [xr_stat[n, pl.ds(at.x, 1), :] for n in (one, two)]
        totals = [xr_stat[n, pl.ds(X + at.x, 1), :] for n in (one, two)]
        top = jnp.maximum(*tops)
        factors = [jnp.exp2(t - top) for t in tops]
        total = totals[0] * factors[0] + totals[1] * factors[1]
        value = xr[one].astype(jnp.float32) * factors[0] + xr[two].astype(jnp.float32) * factors[1]
        value = (value / total).T.astype(jnp.bfloat16)
        for h in range(2):
            column = pl.multiple_of((2 * at.y + hb) * (GROUP * HD) + at.c * (2 * HD) + h * HD, HD)
            out_ref[:, pl.ds(column, HD)] = value[h * rows : (h + 1) * rows]
        column = pl.multiple_of((2 * at.y + hb) * (GROUP * HD) + at.c * (2 * HD), 2 * HD)
        part = out_ref.at[:, pl.ds(column, 2 * HD)]
        for i, device in enumerate(ends):
            copy = remote(part, part, out_send.at[hb, i], out_recv.at[hb, i], device)
            copy.start()
            sent.append(copy)
    for hb in range(2):
        i = 0
        for dc in range(2):
            for dy in range(Y):
                if dy or dc:
                    y, c = (at.y - dy + Y) % Y, (at.c - dc + 2) % 2
                    column = pl.multiple_of((2 * y + hb) * (GROUP * HD) + c * (2 * HD), 2 * HD)
                    part = out_ref.at[:, pl.ds(column, 2 * HD)]
                    remote(part, part, out_send.at[hb, i], out_recv.at[hb, i], other_core).wait_recv()
                    i += 1
    for copy in sent:
        copy.wait_send()


def body(queries, span_keys, span_values, cache_keys, cache_values, cache_lengths, span_lengths):
    sizes = (lax.axis_size("ctx"), lax.axis_size("head"))
    Y, Z = sizes[0] // 2, sizes[1] // X
    heads = 2 * Y
    rows, tokens = queries.shape[0], cache_keys.shape[0]
    bf16, f32 = jnp.bfloat16, jnp.float32
    lengths = pltpu.SMEM(cache_lengths.shape, jnp.int32)
    vmem = pl.BlockSpec(memory_space=pltpu.VMEM)
    hbm = pl.BlockSpec(memory_space=pltpu.HBM)
    dma = pltpu.SemaphoreType.DMA
    freq = jnp.asarray(inverse_freq())
    half = Z // 2

    q_all, k_all, v_all, sk, sv = pl.pallas_call(
        functools.partial(gather_kernel, sizes),
        out_shape=(
            jax.ShapeDtypeStruct((2, Z, X, 2 * rows, HD), bf16),
            jax.ShapeDtypeStruct((heads, tokens, HD), bf16),
            jax.ShapeDtypeStruct((heads, tokens, HD), bf16),
            jax.ShapeDtypeStruct((2, rows, HD), bf16),
            jax.ShapeDtypeStruct((2, rows, HD), bf16),
        ),
        in_specs=[hbm] * 8,
        out_specs=(vmem,) * 5,
        scratch_shapes=[
            lengths, lengths, VMEM(freq.shape, f32), VMEM((tokens, heads * HD), bf16),
            VMEM((2, rows, 2 * HD), bf16),
            VMEM((2, rows, HD), bf16),
            VMEM((2, 2 * rows, HD), bf16),
            VMEM((rows, HD), bf16),
            VMEM((heads - 1, tokens, HD), bf16),
            dma((4,)), dma((2,)), dma((3,)), dma((heads,)), dma((heads,)), dma((heads,)), dma((heads,)),
            dma((X,)), dma((X,)), dma((2, half, X)), dma((2, half, X)), dma((Z,)), dma((Z,)),
            dma((2,)), dma((2,)), dma((2,)),
        ],
        compiler_params=pltpu.CompilerParams(
            collective_id=0, has_side_effects=True, vmem_limit_bytes=60 * 1024 * 1024
        ),
        name="gather",
    )(cache_lengths, span_lengths, freq, queries, span_keys, span_values, cache_keys, cache_values)

    ndoc = cache_lengths.shape[0]
    groups = (heads + 1) * ndoc + 1
    entries = (heads + 1) * (X * Z + ndoc) + 8

    def numbers(n):
        return pltpu.SMEM((n,), jnp.int32)

    parts, stats = pl.pallas_call(
        functools.partial(attend_kernel, sizes),
        out_shape=(
            jax.ShapeDtypeStruct((2, Z, X, HD, 2 * rows), bf16),
            jax.ShapeDtypeStruct((2, Z, 2 * X, 2 * rows), f32),
        ),
        in_specs=[hbm] * 7,
        out_specs=(vmem, vmem),
        scratch_shapes=[
            VMEM((2, Z, X, HD, 2 * rows), f32), lengths, lengths, VMEM(q_all.shape, bf16),
            VMEM((heads + 1, tokens, HD), bf16), VMEM((heads + 1, tokens, HD), bf16),
            VMEM((heads + 1, HD, tokens), bf16),
            VMEM((tokens, 4 * rows), f32), VMEM((tokens, 4 * rows), f32),
            VMEM((tokens, 4 * rows), bf16), VMEM((1, 4 * rows), f32),
            numbers(ndoc + 1), numbers(ndoc + 1), *[numbers(groups)] * 6,
            numbers(entries), numbers(entries), dma((7,)),
        ],
        compiler_params=pltpu.CompilerParams(vmem_limit_bytes=60 * 1024 * 1024),
        name="attend",
    )(cache_lengths, span_lengths, q_all, k_all, v_all, sk, sv)

    piece, stat = (HD, 2 * rows), (2 * X, 2 * rows)
    return pl.pallas_call(
        functools.partial(reduce_kernel, sizes),
        out_shape=jax.ShapeDtypeStruct(queries.shape, bf16),
        in_specs=[hbm, hbm],
        out_specs=vmem,
        scratch_shapes=[
            VMEM((Z, X) + piece, bf16), VMEM((Z,) + stat, f32),
            VMEM((Z, X) + piece, bf16), VMEM((Z,) + stat, f32),
            VMEM((2, half, X) + piece, bf16), VMEM((2, half) + stat, f32),
            VMEM((2, half, X) + piece, bf16), VMEM((2, half) + stat, f32),
            VMEM((X,) + piece, bf16), VMEM(stat, f32),
            VMEM((X,) + piece, bf16), VMEM((X,) + stat, f32),
            dma((Z,)), dma((Z,)), dma((Z,)), dma((Z,)),
            dma((2, half, X)), dma((2, half, X)), dma((2, half)), dma((2, half)),
            dma((X,)), dma((X,)), dma((X,)), dma((X,)),
            dma((2, 2 * Y)), dma((2, 2 * Y)), dma((2,)), dma((2,)),
        ],
        compiler_params=pltpu.CompilerParams(
            collective_id=1, has_side_effects=True, vmem_limit_bytes=60 * 1024 * 1024
        ),
        name="reduce",
    )(parts, stats)


def solution(mesh):
    placed = (
        P("head", None),
        P("head", None),
        P("head", None),
        P(("ctx", "head"), None),
        P(("ctx", "head"), None),
        P(),
        P(),
    )
    return jax.shard_map(
        body, mesh=mesh, in_specs=placed, out_specs=P("head", None), check_vma=False
    )
```

```python
import functools
import math

import jax
import jax.numpy as jnp
import numpy as np
from jax import lax
from jax.experimental import pallas as pl
from jax.experimental.pallas import tpu as pltpu
from jax.sharding import PartitionSpec as P

HD = 128
GROUP = 4
X = 4
FLOOR = -1e30
MESH = pl.DeviceIdType.MESH
VMEM = pltpu.VMEM
SCALE = math.log2(math.e) / math.sqrt(HD)


def inverse_freq():
    counter = np.arange(HD // 2, dtype=np.float64)
    base = 500000.0 ** (-2.0 * counter / HD)
    wavelen = 2.0 * math.pi / base
    smooth = (8192.0 / wavelen - 1.0) / 3.0
    middle = (1.0 - smooth) * base / 8.0 + smooth * base
    freq = np.where(wavelen > 8192.0, base / 8.0, np.where(wavelen < 2048.0, base, middle))
    return np.concatenate([freq, freq]).astype(np.float32)[None, :]


class Place:
    def __init__(self, ctx_size, head_size):
        self.Y = ctx_size // 2
        self.Z = head_size // X
        ctx = lax.axis_index("ctx")
        head = lax.axis_index("head")
        self.ctx, self.head = ctx, head
        self.y = ctx // 2
        self.c = ctx % 2
        self.x = head // self.Z
        self.z = head % self.Z
        self.pair = self.x // 2
        self.hb = self.bit_of(self.x)
        self.k = 2 * self.y + self.hb
        self.mate = self.pair * 3 + (1 - self.hb) * (1 - 2 * self.pair)
        self.sgn = 1 - 2 * self.c

    def bit_of(self, x):
        pair = x // 2
        return pair * 3 + x * (1 - 2 * pair)

    def dev(self, y=None, c=None, x=None, z=None):
        y = self.y if y is None else y
        c = self.c if c is None else c
        x = self.x if x is None else x
        z = self.z if z is None else z
        return (y * 2 + c, x * self.Z + z)

    def z_at(self, offset):
        return (self.z + self.sgn * offset + 2 * self.Z) % self.Z

    def along_z(self, offset):
        return self.dev(z=self.z_at(offset))

    def around(self):
        return [
            (dz, dx, self.dev(x=(self.x + dx) % X, z=self.z_at(dz)))
            for dz in (1, -1, 0)
            for dx in range(X)
            if dz or dx
        ]

    def key_partner(self, d):
        k = (self.k + d) % (2 * self.Y)
        hb = k % 2
        x = self.pair * 3 + hb * (1 - 2 * self.pair)
        return k, self.dev(y=k // 2, x=x)


def barrier(devices):
    sem = pltpu.get_barrier_semaphore()
    for device in devices:
        pl.semaphore_signal(sem, inc=1, device_id=device, device_id_type=MESH)
    pl.semaphore_wait(sem, len(devices))


def remote(src, dst, send, recv, device):
    return pltpu.make_async_remote_copy(
        src_ref=src, dst_ref=dst, send_sem=send, recv_sem=recv, device_id=device, device_id_type=MESH
    )


def turn(data, cosine, sine):
    data = data.astype(jnp.float32)
    return (data * cosine + pltpu.roll(data, HD // 2, 1) * sine).astype(jnp.bfloat16)


def trig(place, freq):
    angle = place.astype(jnp.float32) * freq
    lane = lax.broadcasted_iota(jnp.int32, angle.shape, 1)
    sine = jnp.sin(angle)
    return jnp.cos(angle), jnp.where(lane < HD // 2, -sine, sine)


def gather_kernel(
    sizes, cl_ref, sl_ref, freq_ref, q_ref, sk_ref, sv_ref, k_ref, v_ref,
    qo, ko, vo, sko, svo,
    cl, sl, freq_in, k_in, q_in, sk_in, qs, sks, ks, in_sem,
    q_in_sem, span_sem, v_send, v_recv, k_send, k_recv, q_send, q_recv, on_send,
    core_send, core_recv, own_sem, pair_send, pair_recv,
):
    at = Place(*sizes)
    Y, Z = at.Y, at.Z
    heads = 2 * Y
    rows, tokens = q_ref.shape[0], k_ref.shape[0]
    ndoc = cl.shape[0]

    reads = [
        pltpu.make_async_copy(cl_ref, cl, in_sem.at[0]),
        pltpu.make_async_copy(sl_ref, sl, in_sem.at[1]),
        pltpu.make_async_copy(freq_ref, freq_in, in_sem.at[2]),
    ]
    k_read = pltpu.make_async_copy(k_ref, k_in, in_sem.at[3])
    for hb in range(2):
        column = pl.multiple_of((2 * at.y + hb) * (GROUP * HD) + at.c * (2 * HD), 2 * HD)
        reads.append(
            pltpu.make_async_copy(q_ref.at[:, pl.ds(column, 2 * HD)], q_in.at[hb], q_in_sem.at[hb])
        )
    own = pl.multiple_of(at.k * HD, HD)
    theirs = pl.multiple_of((at.k + 1 - 2 * at.hb) * HD, HD)
    for i, column in enumerate((own, theirs)):
        reads.append(
            pltpu.make_async_copy(sk_ref.at[:, pl.ds(column, HD)], sk_in.at[i], span_sem.at[i])
        )
    for copy in reads:
        copy.start()
    k_read.start()
    sv_copy = pltpu.make_async_copy(sv_ref.at[:, pl.ds(own, HD)], svo.at[0], span_sem.at[2])
    sv_copy.start()
    v_own = pltpu.make_async_copy(v_ref.at[:, pl.ds(own, HD)], vo.at[at.k], own_sem.at[0])
    v_own.start()

    partners = [at.key_partner(d) for d in range(1, heads)]
    other_core = at.dev(c=1 - at.c)
    around = at.around()
    greet = [at.dev(y=(at.y + dy) % Y, x=x) for dy in range(1, Y) for x in (at.x, at.mate)]
    greet += [device for _, _, device in around] + [at.along_z(2), at.along_z(-2), other_core]
    barrier(greet)

    order = sorted(range(1, heads), key=lambda d: -min(d, heads - d))
    v_copies = []
    for d in order:
        k, device = partners[d - 1]
        column = pl.multiple_of(k * HD, HD)
        copy = remote(
            v_ref.at[:, pl.ds(column, HD)], vo.at[at.k], v_send.at[d], v_recv.at[d], device
        )
        copy.start()
        v_copies.append(copy)

    for copy in reads:
        copy.wait()
    freq = freq_in[...]
    row = at.head * rows + lax.broadcasted_iota(jnp.int32, (rows, HD), 0)
    shift = jnp.zeros((rows, HD), jnp.int32)
    start = jnp.int32(0)
    for d in range(ndoc):
        shift = jnp.where(row >= start, cl[d] - start, shift)
        start = start + sl[d]
    cosine, sine = trig(row + shift, freq)
    for hb in range(2):
        for h in range(2):
            qs[hb, h * rows : (h + 1) * rows, :] = turn(
                q_in[hb, :, h * HD : (h + 1) * HD], cosine, sine
            )
    sko[0] = turn(sk_in[0], cosine, sine)
    sks[...] = turn(sk_in[1], cosine, sine)

    q_own = pltpu.make_async_copy(qs.at[at.hb], qo.at[at.c, at.z, at.x], own_sem.at[1])
    q_own.start()
    first_copies = []
    for dz, dx, device in around:
        copy = remote(
            qs.at[at.bit_of((at.x + dx) % X)], qo.at[at.c, at.z, at.x],
            q_send.at[dz + 1, dx], q_recv.at[-dz + 4, dx], device,
        )
        copy.start()
        first_copies.append(copy)
    pair_copies = [
        remote(sks, sko.at[1], pair_send.at[0], pair_recv.at[0], at.dev(x=at.mate)),
        remote(
            sv_ref.at[:, pl.ds(theirs, HD)], svo.at[1], pair_send.at[1], pair_recv.at[1],
            at.dev(x=at.mate),
        ),
    ]
    for copy in pair_copies:
        copy.start()

    onward = []

    def piece(offset, n):
        return qo.at[at.c, at.z_at(offset), (at.x - n + X) % X]

    def arrived(offset, n):
        part = piece(offset, n)
        remote(part, part, q_send.at[0, 0], q_recv.at[offset + 4, n], other_core).wait_recv()

    def pass_on(offset, n, far):
        part = piece(offset, n)
        copy = remote(
            part, part, on_send.at[len(onward)], q_recv.at[offset - far + 4, n], at.along_z(far)
        )
        copy.start()
        onward.append(copy)

    slabs = (0, -1, 1, -2, 2, -3, 3, -4)
    cores = []

    def to_core(offset):
        i = slabs.index(offset)
        slab = qo.at[at.c, at.z_at(offset)]
        copy = remote(slab, slab, core_send.at[i], core_recv.at[i], other_core)
        copy.start()
        cores.append(copy)

    token = (at.ctx * sizes[1] + at.head) * tokens + lax.broadcasted_iota(jnp.int32, (tokens, HD), 0)
    first = jnp.zeros((tokens, HD), jnp.int32)
    start = jnp.int32(0)
    for d in range(ndoc):
        first = jnp.where(token >= start, start, first)
        start = start + cl[d]
    cosine, sine = trig(token - first, freq)
    k_read.wait()
    k_copies = []
    for d in order:
        k, device = partners[d - 1]
        column = pl.multiple_of(k * HD, HD)
        ks[d - 1] = turn(k_in[:, pl.ds(column, HD)], cosine, sine)
        copy = remote(ks.at[d - 1], ko.at[at.k], k_send.at[d], k_recv.at[d], device)
        copy.start()
        k_copies.append(copy)
    ko[at.k] = turn(k_in[:, pl.ds(own, HD)], cosine, sine)

    for n in range(X):
        for offset in (-1, 1):
            arrived(offset, n)
            pass_on(offset, n, -offset)
    q_own.wait()
    for n in range(1, X):
        arrived(0, n)
    for offset in (0, -1, 1):
        to_core(offset)
    for n in range(X):
        for offset in (-2, 2):
            arrived(offset, n)
            if offset == -2:
                pass_on(offset, n, 2)
            pass_on(offset, n, -offset // 2)
    for offset in (-2, 2):
        to_core(offset)
    for offset in (-3, 3, -4):
        for n in range(X):
            arrived(offset, n)
        to_core(offset)

    for i, offset in enumerate(slabs):
        slab = qo.at[1 - at.c, at.z_at(-offset)]
        remote(slab, slab, core_send.at[i], core_recv.at[i], other_core).wait_recv()
    for copy in v_copies + k_copies + pair_copies:
        copy.wait_recv()
    for copy in v_copies + k_copies + pair_copies + first_copies + onward + cores:
        copy.wait_send()
    v_own.wait()
    sv_copy.wait()


def attend_kernel(
    sizes, cl_ref, sl_ref, q_hbm, k_hbm, v_hbm, sk_hbm, sv_hbm, part_ref, stat_ref,
    acc, cl, sl, q_ref, k_ref, v_ref, vt_ref, s_even, s_odd, w_odd, f_odd,
    cache_at, span_at, g_block, g_low, g_high, g_first, g_end, g_causal, e_group, e_chunk, in_sem,
):
    at = Place(*sizes)
    Z = at.Z
    blocks, tokens, _ = k_hbm.shape
    rows = sk_hbm.shape[1]
    lanes = 4 * rows
    ndoc = cl.shape[0]
    pairs = (
        (cl_ref, cl), (sl_ref, sl), (k_hbm, k_ref.at[pl.ds(0, blocks)]),
        (q_hbm, q_ref), (v_hbm, v_ref.at[pl.ds(0, blocks)]),
        (sk_hbm.at[at.c], k_ref.at[blocks, pl.ds(0, rows)]),
        (sv_hbm.at[at.c], v_ref.at[blocks, pl.ds(0, rows)]),
    )
    reads = [pltpu.make_async_copy(a, b, in_sem.at[i]) for i, (a, b) in enumerate(pairs)]
    for copy in reads:
        copy.start()

    k_ref[blocks, rows:, :] = jnp.zeros((tokens - rows, HD), jnp.bfloat16)
    v_ref[blocks, rows:, :] = jnp.zeros((tokens - rows, HD), jnp.bfloat16)
    half = lax.broadcasted_iota(jnp.int32, (2, Z, 2 * X, 2 * rows), 2)
    stat_ref[...] = jnp.where(half < X, FLOOR, 0.0)
    acc[...] = jnp.zeros_like(acc)
    w_odd[...] = jnp.zeros_like(w_odd)
    f_odd[...] = jnp.ones_like(f_odd)
    reads[0].wait()
    reads[1].wait()

    cache_at[0] = jnp.int32(0)
    span_at[0] = jnp.int32(0)
    for d in range(ndoc):
        cache_at[d + 1] = cache_at[d] + cl[d]
        span_at[d + 1] = span_at[d] + sl[d]

    far = jnp.int32(1 << 20)

    def none(group):
        g_block[group], g_low[group], g_high[group] = jnp.int32(0), jnp.int32(0), jnp.int32(0)
        g_first[group], g_end[group], g_causal[group] = jnp.int32(0), jnp.int32(0), far

    none(0)
    e_group[0], e_chunk[0] = jnp.int32(0), jnp.int32(0)

    def add_block(counts, block, starts, first, width, causal, row_first):
        doc_first, doc_last = jnp.int32(0), jnp.int32(0)
        for d in range(1, ndoc):
            doc_first += (starts[d] <= first).astype(jnp.int32)
            doc_last += (starts[d] < first + width).astype(jnp.int32)

        def add_doc(d, counts):
            group, entry = counts
            g_block[group] = block
            g_low[group] = jnp.maximum(starts[d] - first, 0)
            g_high[group] = jnp.minimum(starts[d + 1] - first, width)
            g_first[group] = jnp.maximum(span_at[d], row_first)
            g_end[group] = span_at[d + 1]
            g_causal[group] = causal
            low = jnp.maximum(span_at[d], row_first) // rows
            high = (span_at[d + 1] + rows - 1) // rows

            def add_chunk(n, entry):
                e_group[entry] = group
                e_chunk[entry] = n
                return entry + 1

            return group + 1, lax.fori_loop(low, high, add_chunk, entry)

        return lax.fori_loop(doc_first, doc_last + 1, add_doc, counts)

    def cache_block(b, counts):
        x = at.pair * 3 + (b % 2) * (1 - 2 * at.pair)
        first = (((b // 2) * 2 + at.c) * sizes[1] + x * Z + at.z) * tokens
        return add_block(counts, b, cache_at, first, tokens, far, 0)

    counts = lax.fori_loop(0, blocks, cache_block, (jnp.int32(1), jnp.int32(1)))
    first = (jnp.where(at.c == 0, at.x, at.mate) * Z + at.z) * rows
    _, count = add_block(counts, jnp.int32(blocks), span_at, first, rows, -first, first)
    for i in range(4):
        e_group[count + i], e_chunk[count + i] = jnp.int32(0), jnp.int32(0)

    for copy in reads[2:]:
        copy.wait()

    def turn_over(b, carry):
        vt_ref[b] = v_ref[b].T
        return carry

    lax.fori_loop(0, blocks + 1, turn_over, 0)

    lane = lax.broadcasted_iota(jnp.int32, (1, lanes), 1) % rows
    token = lax.broadcasted_iota(jnp.int32, (tokens, lanes), 0)

    def scores(i):
        n = e_chunk[i]
        x, z = n // Z, n % Z
        q = jnp.concatenate([q_ref[0, z, x], q_ref[1, z, x]], axis=0)
        return lax.dot_general(
            k_ref[g_block[e_group[i]]], q, (((1,), (1,)), ((), ())),
            preferred_element_type=jnp.float32,
        )

    def soften(i, s):
        group, n = e_group[i], e_chunk[i]
        x, z = n // Z, n % Z
        row = n * rows + lane
        here = (row >= g_first[group]) & (row < g_end[group])
        high = jnp.minimum(g_high[group], row + g_causal[group] + 1)
        s = jnp.where((token >= g_low[group]) & (token < high), s * SCALE, FLOOR)
        m_old = jnp.concatenate([stat_ref[c, z, pl.ds(x, 1), :] for c in range(2)], axis=1)
        l_old = jnp.concatenate([stat_ref[c, z, pl.ds(X + x, 1), :] for c in range(2)], axis=1)
        m_new = jnp.where(here, jnp.maximum(m_old, jnp.max(s, axis=0, keepdims=True)), m_old)
        w = jnp.exp2(s - jnp.where(here, m_new, -FLOOR))
        factor = jnp.exp2(m_old - m_new)
        l_new = l_old * factor + jnp.sum(w, axis=0, keepdims=True)
        for c in range(2):
            part = slice(c * 2 * rows, (c + 1) * 2 * rows)
            stat_ref[c, z, pl.ds(x, 1), :] = m_new[:, part]
            stat_ref[c, z, pl.ds(X + x, 1), :] = l_new[:, part]
        return w.astype(jnp.bfloat16), factor

    def product(i, w):
        return jnp.dot(vt_ref[g_block[e_group[i]]], w, preferred_element_type=jnp.float32)

    def update(i, o, factor):
        n = e_chunk[i]
        x, z = n // Z, n % Z
        for c in range(2):
            part = slice(c * 2 * rows, (c + 1) * 2 * rows)
            acc[c, z, x] = acc[c, z, x] * factor[:, part] + o[:, part]

    s_even[...] = scores(1)

    def step(j, carry):
        i = 2 * j + 1
        s_odd[...] = scores(i + 1)
        o_before = product(i - 1, w_odd[...])
        w, factor = soften(i, s_even[...])
        update(i - 1, o_before, f_odd[...])
        s_even[...] = scores(i + 2)
        o = product(i, w)
        w_next, factor_next = soften(i + 1, s_odd[...])
        update(i, o, factor)
        w_odd[...] = w_next
        f_odd[...] = factor_next
        return carry

    steps = count // 2
    lax.fori_loop(0, steps, step, 0)
    update(2 * steps, product(2 * steps, w_odd[...]), f_odd[...])
    part_ref[...] = acc[...].astype(jnp.bfloat16)


def reduce_kernel(
    sizes, part_hbm, stat_hbm, out_ref,
    part_ref, stat_ref, cr, cr_stat, sb, sb_stat, rb, rb_stat, fb, fb_stat, xr, xr_stat, factor_ref,
    core_send, core_recv, core_stat_send, core_stat_recv,
    ring_send, ring_recv, ring_stat_send, ring_stat_recv,
    x_send, x_recv, x_stat_send, x_stat_recv, out_send, out_recv, cross_send, cross_recv, own_sem,
    in_sem,
):
    at = Place(*sizes)
    Y, Z = at.Y, at.Z
    rows = out_ref.shape[0]
    reads = [
        pltpu.make_async_copy(stat_hbm.at[at.c], stat_ref, in_sem.at[0]),
        pltpu.make_async_copy(part_hbm.at[at.c], part_ref, in_sem.at[1]),
    ]
    for copy in reads:
        copy.start()
    other_core = at.dev(c=1 - at.c)
    around = at.around()
    ends = [at.dev(y=(at.y + dy) % Y) for dy in range(1, Y)]
    greet = [device for _, _, device in around] + ends
    barrier(greet + [at.along_z(2), at.along_z(-2), other_core])

    slabs = (4, 3, -3, 2, -2, 1, -1, 0)
    sent = []
    for i, offset in enumerate(slabs):
        z = at.z_at(-offset)
        a = remote(
            stat_hbm.at[1 - at.c, z], cr_stat.at[z], core_stat_send.at[i], core_stat_recv.at[i],
            other_core,
        )
        b = remote(part_hbm.at[1 - at.c, z], cr.at[z], core_send.at[i], core_recv.at[i], other_core)
        a.start()
        b.start()
        sent += [a, b]

    def both_cores(offset):
        i, z = slabs.index(offset), at.z_at(offset)
        remote(
            stat_ref.at[z], cr_stat.at[z], core_stat_send.at[i], core_stat_recv.at[i], other_core
        ).wait_recv()
        remote(part_ref.at[z], cr.at[z], core_send.at[i], core_recv.at[i], other_core).wait_recv()
        return [(part_ref.at[z], stat_ref.at[z]), (cr.at[z], cr_stat.at[z])]

    def ring_in(n, x):
        if x is None:
            remote(
                sb_stat.at[n], rb_stat.at[n], ring_stat_send.at[n], ring_stat_recv.at[n], other_core
            ).wait_recv()
        else:
            remote(
                sb.at[n, x], rb.at[n, x], ring_send.at[n, x], ring_recv.at[n, x], other_core
            ).wait_recv()

    def ring_out(n, device):
        def emit(x):
            if x is None:
                copy = remote(
                    sb_stat.at[n], rb_stat.at[n], ring_stat_send.at[n], ring_stat_recv.at[n], device
                )
            else:
                copy = remote(
                    sb.at[n, x], rb.at[n, x], ring_send.at[n, x], ring_recv.at[n, x], device
                )
            copy.start()
            sent.append(copy)

        return emit

    def join(sources, came, to, to_stat, emit, hold=None):
        for n in came:
            ring_in(n, None)
            sources = sources + [(rb.at[n], rb_stat.at[n])]
        stats = [stat[...] for _, stat in sources]
        top = functools.reduce(jnp.maximum, [s[:X] for s in stats])
        factors = [jnp.exp2(s[:X] - top) for s in stats]
        to_stat[:X, :] = top
        to_stat[X:, :] = sum(s[X:] * f for s, f in zip(stats, factors))
        emit(None)
        if hold is not None:
            for i, f in enumerate(factors):
                hold[i] = f

        def factor(i, x):
            return factors[i][x : x + 1] if hold is None else hold[i, pl.ds(x, 1), :]

        def piece(x):
            for n in came:
                ring_in(n, x)
            to[x] = sum(
                part[x].astype(jnp.float32) * factor(i, x) for i, (part, _) in enumerate(sources)
            ).astype(jnp.bfloat16)
            emit(x)

        return piece

    for copy in reads:
        copy.wait()
    stages = (
        ((4, 2, 0, ()), (3, 1, 1, ()), (-3, -1, 2, ())),
        ((2, 1, 3, (0, 1)), (-2, -1, 4, (2,))),
    )
    for stage in stages:
        pieces = [
            join(
                both_cores(offset), came, sb.at[n], sb_stat.at[n], ring_out(n, at.along_z(far))
            )
            for offset, far, n, came in stage
        ]
        for x in range(X):
            for piece in pieces:
                piece(x)

    def column_out(dz):
        def emit(x):
            for dx in range(X):
                if (dz or dx) and x is None:
                    copy = remote(
                        fb_stat.at[dz + 1], xr_stat.at[-dz + 1, at.x], x_stat_send.at[dz + 1, dx],
                        x_stat_recv.at[-dz + 1, dx], at.dev(x=(at.x + dx) % X, z=at.z_at(dz)),
                    )
                    copy.start()
                    sent.append(copy)

        return emit

    own = []
    for last in ((0,), (1, -1)):
        pieces = [
            join(
                both_cores(dz), {0: (), 1: (3,), -1: (4,)}[dz], fb.at[dz + 1], fb_stat.at[dz + 1],
                column_out(dz), factor_ref.at[dz + 1],
            )
            for dz in last
        ]
        for dx in range(X):
            for dz, piece in zip(last, pieces):
                x = (at.x + dx) % X
                piece(x)
                if dz or dx:
                    copy = remote(
                        fb.at[dz + 1, x], xr.at[-dz + 1, at.x], x_send.at[dz + 1, dx],
                        x_recv.at[-dz + 1, dx], at.dev(x=x, z=at.z_at(dz)),
                    )
                    copy.start()
                    sent.append(copy)
                else:
                    own = [
                        pltpu.make_async_copy(fb.at[1, at.x], xr.at[1, at.x], own_sem.at[0]),
                        pltpu.make_async_copy(fb_stat.at[1], xr_stat.at[1, at.x], own_sem.at[1]),
                    ]
                    for copy in own:
                        copy.start()
    for copy in own:
        copy.wait()
    for dz in (0, 1, -1):
        for dx in range(X):
            if dz or dx:
                remote(
                    fb_stat.at[0], xr_stat.at[dz + 1, at.x], x_stat_send.at[dz + 1, dx],
                    x_stat_recv.at[dz + 1, dx], other_core,
                ).wait_recv()
                remote(
                    fb.at[0, 0], xr.at[dz + 1, at.x], x_send.at[dz + 1, dx], x_recv.at[dz + 1, dx],
                    other_core,
                ).wait_recv()

    def columns(y, hb, c):
        first = pl.multiple_of((2 * y + hb) * (GROUP * HD) + c * (2 * HD), 2 * HD)
        return out_ref.at[:, pl.ds(first, 2 * HD)]

    def cross(hb, dy):
        part = columns((at.y - dy + Y) % Y, hb, at.c)
        copy = remote(part, part, cross_send.at[hb, dy], cross_recv.at[hb, dy], other_core)
        copy.start()
        sent.append(copy)

    for hb, pair in enumerate(((0, 3), (1, 2))):
        sources = [(d, n) for n in pair for d in range(3)]
        tops = [xr_stat[d, n, pl.ds(at.x, 1), :] for d, n in sources]
        totals = [xr_stat[d, n, pl.ds(X + at.x, 1), :] for d, n in sources]
        top = functools.reduce(jnp.maximum, tops)
        factors = [jnp.exp2(t - top) for t in tops]
        total = sum(t * f for t, f in zip(totals, factors))
        value = sum(xr[d, n].astype(jnp.float32) * f for (d, n), f in zip(sources, factors))
        value = (value / total).T.astype(jnp.bfloat16)
        part = columns(at.y, hb, at.c)
        for h in range(2):
            part[:, h * HD : (h + 1) * HD] = value[h * rows : (h + 1) * rows]
        for dy in range(1, Y):
            copy = remote(part, part, out_send.at[hb, dy], out_recv.at[hb, dy], ends[dy - 1])
            copy.start()
            sent.append(copy)
        cross(hb, 0)
    near = sorted(range(1, Y), key=lambda dy: min(dy, Y - dy))
    for hb in range(2):
        for dy in near:
            part = columns((at.y - dy + Y) % Y, hb, at.c)
            remote(part, part, out_send.at[hb, dy], out_recv.at[hb, dy], other_core).wait_recv()
            cross(hb, dy)
    for hb in range(2):
        for dy in range(Y):
            part = columns((at.y - dy + Y) % Y, hb, 1 - at.c)
            remote(part, part, cross_send.at[hb, dy], cross_recv.at[hb, dy], other_core).wait_recv()
    for copy in sent:
        copy.wait_send()


def body(queries, span_keys, span_values, cache_keys, cache_values, cache_lengths, span_lengths):
    sizes = (lax.axis_size("ctx"), lax.axis_size("head"))
    Y, Z = sizes[0] // 2, sizes[1] // X
    heads = 2 * Y
    rows, tokens = queries.shape[0], cache_keys.shape[0]
    bf16, f32 = jnp.bfloat16, jnp.float32
    lengths = pltpu.SMEM(cache_lengths.shape, jnp.int32)
    vmem = pl.BlockSpec(memory_space=pltpu.VMEM)
    hbm = pl.BlockSpec(memory_space=pltpu.HBM)
    dma = pltpu.SemaphoreType.DMA
    freq = jnp.asarray(inverse_freq())

    q_all, k_all, v_all, sk, sv = pl.pallas_call(
        functools.partial(gather_kernel, sizes),
        out_shape=(
            jax.ShapeDtypeStruct((2, Z, X, 2 * rows, HD), bf16),
            jax.ShapeDtypeStruct((heads, tokens, HD), bf16),
            jax.ShapeDtypeStruct((heads, tokens, HD), bf16),
            jax.ShapeDtypeStruct((2, rows, HD), bf16),
            jax.ShapeDtypeStruct((2, rows, HD), bf16),
        ),
        in_specs=[hbm] * 8,
        out_specs=(vmem,) * 5,
        scratch_shapes=[
            lengths, lengths, VMEM(freq.shape, f32), VMEM((tokens, heads * HD), bf16),
            VMEM((2, rows, 2 * HD), bf16),
            VMEM((2, rows, HD), bf16),
            VMEM((2, 2 * rows, HD), bf16),
            VMEM((rows, HD), bf16),
            VMEM((heads - 1, tokens, HD), bf16),
            dma((4,)), dma((2,)), dma((3,)), dma((heads,)), dma((heads,)), dma((heads,)), dma((heads,)),
            dma((3, X)), dma((Z, X)), dma((5 * X,)), dma((Z,)), dma((Z,)),
            dma((2,)), dma((2,)), dma((2,)),
        ],
        compiler_params=pltpu.CompilerParams(
            collective_id=0, has_side_effects=True, vmem_limit_bytes=60 * 1024 * 1024
        ),
        name="gather",
    )(cache_lengths, span_lengths, freq, queries, span_keys, span_values, cache_keys, cache_values)

    ndoc = cache_lengths.shape[0]
    groups = (heads + 1) * ndoc + 1
    entries = (heads + 1) * (X * Z + ndoc) + 8

    def numbers(n):
        return pltpu.SMEM((n,), jnp.int32)

    parts, stats = pl.pallas_call(
        functools.partial(attend_kernel, sizes),
        out_shape=(
            jax.ShapeDtypeStruct((2, Z, X, HD, 2 * rows), bf16),
            jax.ShapeDtypeStruct((2, Z, 2 * X, 2 * rows), f32),
        ),
        in_specs=[hbm] * 7,
        out_specs=(vmem, vmem),
        scratch_shapes=[
            VMEM((2, Z, X, HD, 2 * rows), f32), lengths, lengths, VMEM(q_all.shape, bf16),
            VMEM((heads + 1, tokens, HD), bf16), VMEM((heads + 1, tokens, HD), bf16),
            VMEM((heads + 1, HD, tokens), bf16),
            VMEM((tokens, 4 * rows), f32), VMEM((tokens, 4 * rows), f32),
            VMEM((tokens, 4 * rows), bf16), VMEM((1, 4 * rows), f32),
            numbers(ndoc + 1), numbers(ndoc + 1), *[numbers(groups)] * 6,
            numbers(entries), numbers(entries), dma((7,)),
        ],
        compiler_params=pltpu.CompilerParams(vmem_limit_bytes=60 * 1024 * 1024),
        name="attend",
    )(cache_lengths, span_lengths, q_all, k_all, v_all, sk, sv)

    piece, stat = (HD, 2 * rows), (2 * X, 2 * rows)
    return pl.pallas_call(
        functools.partial(reduce_kernel, sizes),
        out_shape=jax.ShapeDtypeStruct(queries.shape, bf16),
        in_specs=[hbm, hbm],
        out_specs=vmem,
        scratch_shapes=[
            VMEM((Z, X) + piece, bf16), VMEM((Z,) + stat, f32),
            VMEM((Z, X) + piece, bf16), VMEM((Z,) + stat, f32),
            VMEM((5, X) + piece, bf16), VMEM((5,) + stat, f32),
            VMEM((5, X) + piece, bf16), VMEM((5,) + stat, f32),
            VMEM((3, X) + piece, bf16), VMEM((3,) + stat, f32),
            VMEM((3, X) + piece, bf16), VMEM((3, X) + stat, f32),
            VMEM((3, 3, X, 2 * rows), f32),
            dma((Z,)), dma((Z,)), dma((Z,)), dma((Z,)),
            dma((5, X)), dma((5, X)), dma((5,)), dma((5,)),
            dma((3, X)), dma((3, X)), dma((3, X)), dma((3, X)),
            dma((2, Y)), dma((2, Y)), dma((2, Y)), dma((2, Y)), dma((2,)), dma((2,)),
        ],
        compiler_params=pltpu.CompilerParams(
            collective_id=1, has_side_effects=True, vmem_limit_bytes=60 * 1024 * 1024
        ),
        name="reduce",
    )(parts, stats)


def solution(mesh):
    placed = (
        P("head", None),
        P("head", None),
        P("head", None),
        P(("ctx", "head"), None),
        P(("ctx", "head"), None),
        P(),
        P(),
    )
    return jax.shard_map(
        body, mesh=mesh, in_specs=placed, out_specs=P("head", None), check_vma=False
    )
```

```python
import functools
import math

import jax
import jax.numpy as jnp
import numpy as np
from jax import lax
from jax.experimental import pallas as pl
from jax.experimental.pallas import tpu as pltpu
from jax.sharding import PartitionSpec as P

HD = 128
GROUP = 4
X = 4
FLOOR = -1e30
MESH = pl.DeviceIdType.MESH
VMEM = pltpu.VMEM
SCALE = math.log2(math.e) / math.sqrt(HD)


def inverse_freq():
    counter = np.arange(HD // 2, dtype=np.float64)
    base = 500000.0 ** (-2.0 * counter / HD)
    wavelen = 2.0 * math.pi / base
    smooth = (8192.0 / wavelen - 1.0) / 3.0
    middle = (1.0 - smooth) * base / 8.0 + smooth * base
    freq = np.where(wavelen > 8192.0, base / 8.0, np.where(wavelen < 2048.0, base, middle))
    return np.concatenate([freq, freq]).astype(np.float32)[None, :]


class Place:
    def __init__(self, ctx_size, head_size):
        self.Y = ctx_size // 2
        self.Z = head_size // X
        ctx = lax.axis_index("ctx")
        head = lax.axis_index("head")
        self.ctx, self.head = ctx, head
        self.y = ctx // 2
        self.c = ctx % 2
        self.x = head // self.Z
        self.z = head % self.Z
        self.pair = self.x // 2
        self.hb = self.bit_of(self.x)
        self.k = 2 * self.y + self.hb
        self.mate = self.pair * 3 + (1 - self.hb) * (1 - 2 * self.pair)
        self.sgn = 1 - 2 * self.c

    def bit_of(self, x):
        pair = x // 2
        return pair * 3 + x * (1 - 2 * pair)

    def dev(self, y=None, c=None, x=None, z=None):
        y = self.y if y is None else y
        c = self.c if c is None else c
        x = self.x if x is None else x
        z = self.z if z is None else z
        return (y * 2 + c, x * self.Z + z)

    def z_at(self, offset):
        return (self.z + self.sgn * offset + 2 * self.Z) % self.Z

    def along_z(self, offset):
        return self.dev(z=self.z_at(offset))

    def around(self):
        return [
            (dz, dx, self.dev(x=(self.x + dx) % X, z=self.z_at(dz)))
            for dz in (1, -1, 0)
            for dx in range(X)
            if dz or dx
        ]

    def key_partner(self, d):
        k = (self.k + d) % (2 * self.Y)
        hb = k % 2
        x = self.pair * 3 + hb * (1 - 2 * self.pair)
        return k, self.dev(y=k // 2, x=x)


def barrier(devices):
    sem = pltpu.get_barrier_semaphore()
    for device in devices:
        pl.semaphore_signal(sem, inc=1, device_id=device, device_id_type=MESH)
    pl.semaphore_wait(sem, len(devices))


def remote(src, dst, send, recv, device):
    return pltpu.make_async_remote_copy(
        src_ref=src, dst_ref=dst, send_sem=send, recv_sem=recv, device_id=device, device_id_type=MESH
    )


def turn(data, cosine, sine):
    data = data.astype(jnp.float32)
    return (data * cosine + pltpu.roll(data, HD // 2, 1) * sine).astype(jnp.bfloat16)


def trig(place, freq):
    angle = place.astype(jnp.float32) * freq
    lane = lax.broadcasted_iota(jnp.int32, angle.shape, 1)
    sine = jnp.sin(angle)
    return jnp.cos(angle), jnp.where(lane < HD // 2, -sine, sine)


def gather_kernel(
    sizes, cl_ref, sl_ref, freq_ref, q_ref, sk_ref, sv_ref, k_ref, v_ref,
    qo, ko, vo, sko, svo,
    cl, sl, freq_in, k_in, q_in, sk_in, qs, qb, sks, ks, in_sem,
    q_in_sem, span_sem, v_send, v_recv, k_send, k_recv, q_send, q_recv, on_send,
    core_send, core_recv, own_sem, q_own_sem, pair_send, pair_recv,
):
    at = Place(*sizes)
    Y, Z = at.Y, at.Z
    heads = 2 * Y
    rows, tokens = q_ref.shape[0], k_ref.shape[0]
    ndoc = cl.shape[0]

    reads = [
        pltpu.make_async_copy(cl_ref, cl, in_sem.at[0]),
        pltpu.make_async_copy(sl_ref, sl, in_sem.at[1]),
        pltpu.make_async_copy(freq_ref, freq_in, in_sem.at[2]),
    ]
    k_read = pltpu.make_async_copy(k_ref, k_in, in_sem.at[3])
    for hb in range(2):
        column = pl.multiple_of((2 * at.y + hb) * (GROUP * HD) + at.c * (2 * HD), 2 * HD)
        reads.append(
            pltpu.make_async_copy(q_ref.at[:, pl.ds(column, 2 * HD)], q_in.at[hb], q_in_sem.at[hb])
        )
    own = pl.multiple_of(at.k * HD, HD)
    theirs = pl.multiple_of((at.k + 1 - 2 * at.hb) * HD, HD)
    for i, column in enumerate((own, theirs)):
        reads.append(
            pltpu.make_async_copy(sk_ref.at[:, pl.ds(column, HD)], sk_in.at[i], span_sem.at[i])
        )
    for copy in reads:
        copy.start()
    k_read.start()
    sv_copy = pltpu.make_async_copy(sv_ref.at[:, pl.ds(own, HD)], svo.at[0], span_sem.at[2])
    sv_copy.start()
    v_own = pltpu.make_async_copy(v_ref.at[:, pl.ds(own, HD)], vo.at[at.k], own_sem.at[0])
    v_own.start()

    partners = [at.key_partner(d) for d in range(1, heads)]
    other_core = at.dev(c=1 - at.c)
    around = at.around()
    greet = [at.dev(y=(at.y + dy) % Y, x=x) for dy in range(1, Y) for x in (at.x, at.mate)]
    greet += [device for _, _, device in around] + [at.along_z(2), at.along_z(-2), other_core]
    barrier(greet)

    for copy in reads:
        copy.wait()
    freq = freq_in[...]
    row = at.head * rows + lax.broadcasted_iota(jnp.int32, (rows, HD), 0)
    shift = jnp.zeros((rows, HD), jnp.int32)
    start = jnp.int32(0)
    for d in range(ndoc):
        shift = jnp.where(row >= start, cl[d] - start, shift)
        start = start + sl[d]
    cosine, sine = trig(row + shift, freq)
    for hb in range(2):
        for h in range(2):
            qs[hb, h * rows : (h + 1) * rows, :] = turn(
                q_in[hb, :, h * HD : (h + 1) * HD], cosine, sine
            )
    for i in range(2):
        sks[i] = turn(sk_in[i], cosine, sine)

    q_own = pltpu.make_async_copy(qs.at[at.hb], qb.at[at.z, at.x], own_sem.at[1])
    q_own.start()
    first_copies = []
    for dz, dx, device in around:
        copy = remote(
            qs.at[at.bit_of((at.x + dx) % X)], qb.at[at.z, at.x],
            q_send.at[dz + 1, dx], q_recv.at[-dz + 4, dx], device,
        )
        copy.start()
        first_copies.append(copy)
    pair_copies = [
        remote(sks.at[1], sko.at[1], pair_send.at[0], pair_recv.at[0], at.dev(x=at.mate)),
        remote(
            sv_ref.at[:, pl.ds(theirs, HD)], svo.at[1], pair_send.at[1], pair_recv.at[1],
            at.dev(x=at.mate),
        ),
    ]
    sk_own = pltpu.make_async_copy(sks.at[0], sko.at[0], own_sem.at[2])
    for copy in pair_copies + [sk_own]:
        copy.start()

    onward = []

    def piece(offset, n):
        return qb.at[at.z_at(offset), (at.x - n + X) % X]

    def arrived(offset, n):
        part = piece(offset, n)
        remote(part, part, q_send.at[0, 0], q_recv.at[offset + 4, n], other_core).wait_recv()

    def pass_on(offset, n, far):
        part = piece(offset, n)
        copy = remote(
            part, part, on_send.at[len(onward)], q_recv.at[offset - far + 4, n], at.along_z(far)
        )
        copy.start()
        onward.append(copy)

    slabs = (0, -1, 1, -2, 2, -3, 3, -4)
    cores, kept = [], []

    def to_core(offset):
        i = slabs.index(offset)
        z = at.z_at(offset)
        copy = remote(
            qb.at[z], qo.at[at.c, z], core_send.at[i], core_recv.at[i], other_core
        )
        copy.start()
        cores.append(copy)
        copy = pltpu.make_async_copy(qb.at[z], qo.at[at.c, z], q_own_sem.at[i])
        copy.start()
        kept.append(copy)

    order = sorted(range(1, heads), key=lambda d: -min(d, heads - d))
    v_copies = []
    for d in order:
        k, device = partners[d - 1]
        column = pl.multiple_of(k * HD, HD)
        copy = remote(
            v_ref.at[:, pl.ds(column, HD)], vo.at[at.k], v_send.at[d], v_recv.at[d], device
        )
        copy.start()
        v_copies.append(copy)

    token = (at.ctx * sizes[1] + at.head) * tokens + lax.broadcasted_iota(jnp.int32, (tokens, HD), 0)
    first = jnp.zeros((tokens, HD), jnp.int32)
    start = jnp.int32(0)
    for d in range(ndoc):
        first = jnp.where(token >= start, start, first)
        start = start + cl[d]
    cosine, sine = trig(token - first, freq)
    k_read.wait()
    k_copies = []
    for d in order:
        k, device = partners[d - 1]
        column = pl.multiple_of(k * HD, HD)
        ks[d] = turn(k_in[:, pl.ds(column, HD)], cosine, sine)
        copy = remote(ks.at[d], ko.at[at.k], k_send.at[d], k_recv.at[d], device)
        copy.start()
        k_copies.append(copy)
    ks[0] = turn(k_in[:, pl.ds(own, HD)], cosine, sine)
    k_own = pltpu.make_async_copy(ks.at[0], ko.at[at.k], own_sem.at[3])
    k_own.start()

    for n in range(X):
        for offset in (-1, 1):
            arrived(offset, n)
            pass_on(offset, n, -offset)
    q_own.wait()
    for n in range(1, X):
        arrived(0, n)
    for offset in (0, -1, 1):
        to_core(offset)
    for n in range(X):
        for offset in (-2, 2):
            arrived(offset, n)
            if offset == -2:
                pass_on(offset, n, 2)
            pass_on(offset, n, -offset // 2)
    for offset in (-2, 2):
        to_core(offset)
    for offset in (-3, 3, -4):
        for n in range(X):
            arrived(offset, n)
        to_core(offset)

    for i, offset in enumerate(slabs):
        z = at.z_at(-offset)
        remote(
            qb.at[z], qo.at[1 - at.c, z], core_send.at[i], core_recv.at[i], other_core
        ).wait_recv()
    for copy in v_copies + k_copies + pair_copies:
        copy.wait_recv()
    for copy in v_copies + k_copies + pair_copies + first_copies + onward + cores:
        copy.wait_send()
    for copy in kept + [v_own, k_own, sk_own, sv_copy]:
        copy.wait()


def attend_kernel(
    sizes, cl_ref, sl_ref, q_hbm, k_hbm, v_hbm, sk_hbm, sv_hbm, part_hbm, stat_ref,
    part_ref, acc, cl, sl, q_ref, k_ref, v_ref, vt_ref, s_even, s_odd, w_odd, f_odd,
    cache_at, span_at, g_block, g_low, g_high, g_first, g_end, g_causal, e_group, e_chunk, in_sem, out_sem,
):
    at = Place(*sizes)
    Z = at.Z
    blocks, tokens, _ = k_hbm.shape
    rows = sk_hbm.shape[1]
    lanes = 4 * rows
    ndoc = cl.shape[0]
    pairs = (
        (cl_ref, cl), (sl_ref, sl), (k_hbm, k_ref.at[pl.ds(0, blocks)]),
        (q_hbm, q_ref), (v_hbm, v_ref.at[pl.ds(0, blocks)]),
        (sk_hbm.at[at.c], k_ref.at[blocks, pl.ds(0, rows)]),
        (sv_hbm.at[at.c], v_ref.at[blocks, pl.ds(0, rows)]),
    )
    reads = [pltpu.make_async_copy(a, b, in_sem.at[i]) for i, (a, b) in enumerate(pairs)]
    for copy in reads:
        copy.start()

    k_ref[blocks, rows:, :] = jnp.zeros((tokens - rows, HD), jnp.bfloat16)
    v_ref[blocks, rows:, :] = jnp.zeros((tokens - rows, HD), jnp.bfloat16)
    half = lax.broadcasted_iota(jnp.int32, (2, Z, 2 * X, 2 * rows), 2)
    stat_ref[...] = jnp.where(half < X, FLOOR, 0.0)
    acc[...] = jnp.zeros_like(acc)
    w_odd[...] = jnp.zeros_like(w_odd)
    f_odd[...] = jnp.ones_like(f_odd)
    reads[0].wait()
    reads[1].wait()

    cache_at[0] = jnp.int32(0)
    span_at[0] = jnp.int32(0)
    for d in range(ndoc):
        cache_at[d + 1] = cache_at[d] + cl[d]
        span_at[d + 1] = span_at[d] + sl[d]

    far = jnp.int32(1 << 20)

    def none(group):
        g_block[group], g_low[group], g_high[group] = jnp.int32(0), jnp.int32(0), jnp.int32(0)
        g_first[group], g_end[group], g_causal[group] = jnp.int32(0), jnp.int32(0), far

    none(0)
    e_group[0], e_chunk[0] = jnp.int32(0), jnp.int32(0)

    def add_block(counts, block, starts, first, width, causal, row_first):
        doc_first, doc_last = jnp.int32(0), jnp.int32(0)
        for d in range(1, ndoc):
            doc_first += (starts[d] <= first).astype(jnp.int32)
            doc_last += (starts[d] < first + width).astype(jnp.int32)

        def add_doc(d, counts):
            group, entry = counts
            g_block[group] = block
            g_low[group] = jnp.maximum(starts[d] - first, 0)
            g_high[group] = jnp.minimum(starts[d + 1] - first, width)
            g_first[group] = jnp.maximum(span_at[d], row_first)
            g_end[group] = span_at[d + 1]
            g_causal[group] = causal
            low = jnp.maximum(span_at[d], row_first) // rows
            high = (span_at[d + 1] + rows - 1) // rows

            def add_chunk(n, entry):
                e_group[entry] = group
                e_chunk[entry] = n
                return entry + 1

            return group + 1, lax.fori_loop(low, high, add_chunk, entry)

        return lax.fori_loop(doc_first, doc_last + 1, add_doc, counts)

    def cache_block(b, counts):
        x = at.pair * 3 + (b % 2) * (1 - 2 * at.pair)
        first = (((b // 2) * 2 + at.c) * sizes[1] + x * Z + at.z) * tokens
        return add_block(counts, b, cache_at, first, tokens, far, 0)

    counts = lax.fori_loop(0, blocks, cache_block, (jnp.int32(1), jnp.int32(1)))
    first = (jnp.where(at.c == 0, at.x, at.mate) * Z + at.z) * rows
    _, count = add_block(counts, jnp.int32(blocks), span_at, first, rows, -first, first)
    for i in range(4):
        e_group[count + i], e_chunk[count + i] = jnp.int32(0), jnp.int32(0)

    for copy in reads[2:]:
        copy.wait()

    def turn_over(b, carry):
        vt_ref[b] = v_ref[b].T
        return carry

    lax.fori_loop(0, blocks + 1, turn_over, 0)

    lane = lax.broadcasted_iota(jnp.int32, (1, lanes), 1) % rows
    token = lax.broadcasted_iota(jnp.int32, (tokens, lanes), 0)

    def scores(i):
        n = e_chunk[i]
        x, z = n // Z, n % Z
        q = jnp.concatenate([q_ref[0, z, x], q_ref[1, z, x]], axis=0)
        return lax.dot_general(
            k_ref[g_block[e_group[i]]], q, (((1,), (1,)), ((), ())),
            preferred_element_type=jnp.float32,
        )

    def soften(i, s):
        group, n = e_group[i], e_chunk[i]
        x, z = n // Z, n % Z
        row = n * rows + lane
        here = (row >= g_first[group]) & (row < g_end[group])
        high = jnp.minimum(g_high[group], row + g_causal[group] + 1)
        s = jnp.where((token >= g_low[group]) & (token < high), s * SCALE, FLOOR)
        m_old = jnp.concatenate([stat_ref[c, z, pl.ds(x, 1), :] for c in range(2)], axis=1)
        l_old = jnp.concatenate([stat_ref[c, z, pl.ds(X + x, 1), :] for c in range(2)], axis=1)
        m_new = jnp.where(here, jnp.maximum(m_old, jnp.max(s, axis=0, keepdims=True)), m_old)
        w = jnp.exp2(s - jnp.where(here, m_new, -FLOOR))
        factor = jnp.exp2(m_old - m_new)
        l_new = l_old * factor + jnp.sum(w, axis=0, keepdims=True)
        for c in range(2):
            part = slice(c * 2 * rows, (c + 1) * 2 * rows)
            stat_ref[c, z, pl.ds(x, 1), :] = m_new[:, part]
            stat_ref[c, z, pl.ds(X + x, 1), :] = l_new[:, part]
        return w.astype(jnp.bfloat16), factor

    def product(i, w):
        return jnp.dot(vt_ref[g_block[e_group[i]]], w, preferred_element_type=jnp.float32)

    def update(i, o, factor):
        n = e_chunk[i]
        x, z = n // Z, n % Z
        for c in range(2):
            part = slice(c * 2 * rows, (c + 1) * 2 * rows)
            acc[c, z, x] = acc[c, z, x] * factor[:, part] + o[:, part]

    s_even[...] = scores(1)

    def step(j, carry):
        i = 2 * j + 1
        s_odd[...] = scores(i + 1)
        o_before = product(i - 1, w_odd[...])
        w, factor = soften(i, s_even[...])
        update(i - 1, o_before, f_odd[...])
        s_even[...] = scores(i + 2)
        o = product(i, w)
        w_next, factor_next = soften(i + 1, s_odd[...])
        update(i, o, factor)
        w_odd[...] = w_next
        f_odd[...] = factor_next
        return carry

    steps = count // 2
    lax.fori_loop(0, steps, step, 0)
    update(2 * steps, product(2 * steps, w_odd[...]), f_odd[...])

    def leave(i):
        c, z = i // Z, i % Z
        return pltpu.make_async_copy(part_ref.at[c, z], part_hbm.at[c, z], out_sem.at[i])

    def slab(i, carry):
        part_ref[i // Z, i % Z] = acc[i // Z, i % Z].astype(jnp.bfloat16)
        leave(i).start()
        return carry

    def left(i, carry):
        leave(i).wait()
        return carry

    lax.fori_loop(0, 2 * Z, slab, 0)
    lax.fori_loop(0, 2 * Z, left, 0)


def reduce_kernel(
    sizes, part_hbm, stat_hbm, out_ref,
    part_ref, stat_ref, cr, cr_stat, sb, sb_stat, rb, rb_stat, fb, fb_stat, xr, xr_stat, factor_ref,
    core_send, core_recv, core_stat_send, core_stat_recv,
    ring_send, ring_recv, ring_stat_send, ring_stat_recv,
    x_send, x_recv, x_stat_send, x_stat_recv, out_send, out_recv, cross_send, cross_recv, own_sem,
    in_sem,
):
    at = Place(*sizes)
    Y, Z = at.Y, at.Z
    rows = out_ref.shape[0]
    reads = [
        pltpu.make_async_copy(stat_hbm.at[at.c], stat_ref, in_sem.at[0]),
        pltpu.make_async_copy(part_hbm.at[at.c], part_ref, in_sem.at[1]),
    ]
    for copy in reads:
        copy.start()
    other_core = at.dev(c=1 - at.c)
    around = at.around()
    ends = [at.dev(y=(at.y + dy) % Y) for dy in range(1, Y)]
    greet = [device for _, _, device in around] + ends
    barrier(greet + [at.along_z(2), at.along_z(-2), other_core])

    slabs = (4, 3, -3, 2, -2, 1, -1, 0)
    sent = []
    for i, offset in enumerate(slabs):
        z = at.z_at(-offset)
        a = remote(
            stat_hbm.at[1 - at.c, z], cr_stat.at[z], core_stat_send.at[i], core_stat_recv.at[i],
            other_core,
        )
        b = remote(part_hbm.at[1 - at.c, z], cr.at[z], core_send.at[i], core_recv.at[i], other_core)
        a.start()
        b.start()
        sent += [a, b]

    def both_cores(offset):
        i, z = slabs.index(offset), at.z_at(offset)
        remote(
            stat_ref.at[z], cr_stat.at[z], core_stat_send.at[i], core_stat_recv.at[i], other_core
        ).wait_recv()
        remote(part_ref.at[z], cr.at[z], core_send.at[i], core_recv.at[i], other_core).wait_recv()
        return [(part_ref.at[z], stat_ref.at[z]), (cr.at[z], cr_stat.at[z])]

    def ring_in(n, x):
        if x is None:
            remote(
                sb_stat.at[n], rb_stat.at[n], ring_stat_send.at[n], ring_stat_recv.at[n], other_core
            ).wait_recv()
        else:
            remote(
                sb.at[n, x], rb.at[n, x], ring_send.at[n, x], ring_recv.at[n, x], other_core
            ).wait_recv()

    def ring_out(n, device):
        def emit(x):
            if x is None:
                copy = remote(
                    sb_stat.at[n], rb_stat.at[n], ring_stat_send.at[n], ring_stat_recv.at[n], device
                )
            else:
                copy = remote(
                    sb.at[n, x], rb.at[n, x], ring_send.at[n, x], ring_recv.at[n, x], device
                )
            copy.start()
            sent.append(copy)

        return emit

    def join(sources, came, to, to_stat, emit, hold=None):
        for n in came:
            ring_in(n, None)
            sources = sources + [(rb.at[n], rb_stat.at[n])]
        stats = [stat[...] for _, stat in sources]
        top = functools.reduce(jnp.maximum, [s[:X] for s in stats])
        factors = [jnp.exp2(s[:X] - top) for s in stats]
        to_stat[:X, :] = top
        to_stat[X:, :] = sum(s[X:] * f for s, f in zip(stats, factors))
        emit(None)
        if hold is not None:
            for i, f in enumerate(factors):
                hold[i] = f

        def factor(i, x):
            return factors[i][x : x + 1] if hold is None else hold[i, pl.ds(x, 1), :]

        def piece(x):
            for n in came:
                ring_in(n, x)
            to[x] = sum(
                part[x].astype(jnp.float32) * factor(i, x) for i, (part, _) in enumerate(sources)
            ).astype(jnp.bfloat16)
            emit(x)

        return piece

    for copy in reads:
        copy.wait()
    stages = (
        ((4, 2, 0, ()), (3, 1, 1, ()), (-3, -1, 2, ())),
        ((2, 1, 3, (0, 1)), (-2, -1, 4, (2,))),
    )
    def work(stage):
        pieces = [
            join(
                both_cores(offset), came, sb.at[n], sb_stat.at[n], ring_out(n, at.along_z(far))
            )
            for offset, far, n, came in stage
        ]
        for x in range(X):
            for piece in pieces:
                piece(x)

    def column_out(dz):
        def emit(x):
            for dx in range(X):
                if (dz or dx) and x is None:
                    copy = remote(
                        fb_stat.at[dz + 1], xr_stat.at[-dz + 1, at.x], x_stat_send.at[dz + 1, dx],
                        x_stat_recv.at[-dz + 1, dx], at.dev(x=(at.x + dx) % X, z=at.z_at(dz)),
                    )
                    copy.start()
                    sent.append(copy)

        return emit

    own = []

    def finish(last):
        pieces = [
            join(
                both_cores(dz), {0: (), 1: (3,), -1: (4,)}[dz], fb.at[dz + 1], fb_stat.at[dz + 1],
                column_out(dz), factor_ref.at[dz + 1],
            )
            for dz in last
        ]
        for dx in range(X):
            for dz, piece in zip(last, pieces):
                x = (at.x + dx) % X
                piece(x)
                if dz or dx:
                    copy = remote(
                        fb.at[dz + 1, x], xr.at[-dz + 1, at.x], x_send.at[dz + 1, dx],
                        x_recv.at[-dz + 1, dx], at.dev(x=x, z=at.z_at(dz)),
                    )
                    copy.start()
                    sent.append(copy)
                else:
                    own.extend((
                        pltpu.make_async_copy(fb.at[1, at.x], xr.at[1, at.x], own_sem.at[0]),
                        pltpu.make_async_copy(fb_stat.at[1], xr_stat.at[1, at.x], own_sem.at[1]),
                    ))
                    for copy in own:
                        copy.start()

    work(stages[0])
    finish((0,))
    work(stages[1])
    finish((1, -1))
    for copy in own:
        copy.wait()
    for dz in (0, 1, -1):
        for dx in range(X):
            if dz or dx:
                remote(
                    fb_stat.at[0], xr_stat.at[dz + 1, at.x], x_stat_send.at[dz + 1, dx],
                    x_stat_recv.at[dz + 1, dx], other_core,
                ).wait_recv()
                remote(
                    fb.at[0, 0], xr.at[dz + 1, at.x], x_send.at[dz + 1, dx], x_recv.at[dz + 1, dx],
                    other_core,
                ).wait_recv()

    def columns(y, hb, c):
        first = pl.multiple_of((2 * y + hb) * (GROUP * HD) + c * (2 * HD), 2 * HD)
        return out_ref.at[:, pl.ds(first, 2 * HD)]

    def cross(hb, dy):
        part = columns((at.y - dy + Y) % Y, hb, at.c)
        copy = remote(part, part, cross_send.at[hb, dy], cross_recv.at[hb, dy], other_core)
        copy.start()
        sent.append(copy)

    for hb, pair in enumerate(((0, 3), (1, 2))):
        sources = [(d, n) for n in pair for d in range(3)]
        tops = [xr_stat[d, n, pl.ds(at.x, 1), :] for d, n in sources]
        totals = [xr_stat[d, n, pl.ds(X + at.x, 1), :] for d, n in sources]
        top = functools.reduce(jnp.maximum, tops)
        factors = [jnp.exp2(t - top) for t in tops]
        total = sum(t * f for t, f in zip(totals, factors))
        value = sum(xr[d, n].astype(jnp.float32) * f for (d, n), f in zip(sources, factors))
        value = (value / total).T.astype(jnp.bfloat16)
        part = columns(at.y, hb, at.c)
        for h in range(2):
            part[:, h * HD : (h + 1) * HD] = value[h * rows : (h + 1) * rows]
        for dy in range(1, Y):
            copy = remote(part, part, out_send.at[hb, dy], out_recv.at[hb, dy], ends[dy - 1])
            copy.start()
            sent.append(copy)
        cross(hb, 0)
    near = sorted(range(1, Y), key=lambda dy: min(dy, Y - dy))
    for hb in range(2):
        for dy in near:
            part = columns((at.y - dy + Y) % Y, hb, at.c)
            remote(part, part, out_send.at[hb, dy], out_recv.at[hb, dy], other_core).wait_recv()
            cross(hb, dy)
    for hb in range(2):
        for dy in range(Y):
            part = columns((at.y - dy + Y) % Y, hb, 1 - at.c)
            remote(part, part, cross_send.at[hb, dy], cross_recv.at[hb, dy], other_core).wait_recv()
    for copy in sent:
        copy.wait_send()


def body(queries, span_keys, span_values, cache_keys, cache_values, cache_lengths, span_lengths):
    sizes = (lax.axis_size("ctx"), lax.axis_size("head"))
    Y, Z = sizes[0] // 2, sizes[1] // X
    heads = 2 * Y
    rows, tokens = queries.shape[0], cache_keys.shape[0]
    bf16, f32 = jnp.bfloat16, jnp.float32
    lengths = pltpu.SMEM(cache_lengths.shape, jnp.int32)
    vmem = pl.BlockSpec(memory_space=pltpu.VMEM)
    hbm = pl.BlockSpec(memory_space=pltpu.HBM)
    dma = pltpu.SemaphoreType.DMA
    freq = jnp.asarray(inverse_freq())

    q_all, k_all, v_all, sk, sv = pl.pallas_call(
        functools.partial(gather_kernel, sizes),
        out_shape=(
            jax.ShapeDtypeStruct((2, Z, X, 2 * rows, HD), bf16),
            jax.ShapeDtypeStruct((heads, tokens, HD), bf16),
            jax.ShapeDtypeStruct((heads, tokens, HD), bf16),
            jax.ShapeDtypeStruct((2, rows, HD), bf16),
            jax.ShapeDtypeStruct((2, rows, HD), bf16),
        ),
        in_specs=[hbm] * 8,
        out_specs=(hbm,) * 5,
        scratch_shapes=[
            lengths, lengths, VMEM(freq.shape, f32), VMEM((tokens, heads * HD), bf16),
            VMEM((2, rows, 2 * HD), bf16),
            VMEM((2, rows, HD), bf16),
            VMEM((2, 2 * rows, HD), bf16),
            VMEM((Z, X, 2 * rows, HD), bf16),
            VMEM((2, rows, HD), bf16),
            VMEM((heads, tokens, HD), bf16),
            dma((4,)), dma((2,)), dma((3,)), dma((heads,)), dma((heads,)), dma((heads,)), dma((heads,)),
            dma((3, X)), dma((Z, X)), dma((5 * X,)), dma((Z,)), dma((Z,)),
            dma((4,)), dma((Z,)), dma((2,)), dma((2,)),
        ],
        compiler_params=pltpu.CompilerParams(
            collective_id=0, has_side_effects=True, vmem_limit_bytes=60 * 1024 * 1024
        ),
        name="gather",
    )(cache_lengths, span_lengths, freq, queries, span_keys, span_values, cache_keys, cache_values)

    ndoc = cache_lengths.shape[0]
    groups = (heads + 1) * ndoc + 1
    entries = (heads + 1) * (X * Z + ndoc) + 8

    def numbers(n):
        return pltpu.SMEM((n,), jnp.int32)

    parts, stats = pl.pallas_call(
        functools.partial(attend_kernel, sizes),
        out_shape=(
            jax.ShapeDtypeStruct((2, Z, X, HD, 2 * rows), bf16),
            jax.ShapeDtypeStruct((2, Z, 2 * X, 2 * rows), f32),
        ),
        in_specs=[hbm] * 7,
        out_specs=(hbm, vmem),
        scratch_shapes=[
            VMEM((2, Z, X, HD, 2 * rows), bf16),
            VMEM((2, Z, X, HD, 2 * rows), f32), lengths, lengths, VMEM(q_all.shape, bf16),
            VMEM((heads + 1, tokens, HD), bf16), VMEM((heads + 1, tokens, HD), bf16),
            VMEM((heads + 1, HD, tokens), bf16),
            VMEM((tokens, 4 * rows), f32), VMEM((tokens, 4 * rows), f32),
            VMEM((tokens, 4 * rows), bf16), VMEM((1, 4 * rows), f32),
            numbers(ndoc + 1), numbers(ndoc + 1), *[numbers(groups)] * 6,
            numbers(entries), numbers(entries), dma((7,)), dma((2 * Z,)),
        ],
        compiler_params=pltpu.CompilerParams(vmem_limit_bytes=60 * 1024 * 1024),
        name="attend",
    )(cache_lengths, span_lengths, q_all, k_all, v_all, sk, sv)

    piece, stat = (HD, 2 * rows), (2 * X, 2 * rows)
    return pl.pallas_call(
        functools.partial(reduce_kernel, sizes),
        out_shape=jax.ShapeDtypeStruct(queries.shape, bf16),
        in_specs=[hbm, hbm],
        out_specs=vmem,
        scratch_shapes=[
            VMEM((Z, X) + piece, bf16), VMEM((Z,) + stat, f32),
            VMEM((Z, X) + piece, bf16), VMEM((Z,) + stat, f32),
            VMEM((5, X) + piece, bf16), VMEM((5,) + stat, f32),
            VMEM((5, X) + piece, bf16), VMEM((5,) + stat, f32),
            VMEM((3, X) + piece, bf16), VMEM((3,) + stat, f32),
            VMEM((3, X) + piece, bf16), VMEM((3, X) + stat, f32),
            VMEM((3, 3, X, 2 * rows), f32),
            dma((Z,)), dma((Z,)), dma((Z,)), dma((Z,)),
            dma((5, X)), dma((5, X)), dma((5,)), dma((5,)),
            dma((3, X)), dma((3, X)), dma((3, X)), dma((3, X)),
            dma((2, Y)), dma((2, Y)), dma((2, Y)), dma((2, Y)), dma((2,)), dma((2,)),
        ],
        compiler_params=pltpu.CompilerParams(
            collective_id=1, has_side_effects=True, vmem_limit_bytes=60 * 1024 * 1024
        ),
        name="reduce",
    )(parts, stats)


def solution(mesh):
    placed = (
        P("head", None),
        P("head", None),
        P("head", None),
        P(("ctx", "head"), None),
        P(("ctx", "head"), None),
        P(),
        P(),
    )
    return jax.shard_map(
        body, mesh=mesh, in_specs=placed, out_specs=P("head", None), check_vma=False
    )
```

```python
import functools
import math

import jax
import jax.numpy as jnp
import numpy as np
from jax import lax
from jax.experimental import pallas as pl
from jax.experimental.pallas import tpu as pltpu
from jax.sharding import PartitionSpec as P

HD = 128
GROUP = 4
X = 4
FLOOR = -1e30
MESH = pl.DeviceIdType.MESH
VMEM = pltpu.VMEM
SCALE = math.log2(math.e) / math.sqrt(HD)


def inverse_freq():
    counter = np.arange(HD // 2, dtype=np.float64)
    base = 500000.0 ** (-2.0 * counter / HD)
    wavelen = 2.0 * math.pi / base
    smooth = (8192.0 / wavelen - 1.0) / 3.0
    middle = (1.0 - smooth) * base / 8.0 + smooth * base
    freq = np.where(wavelen > 8192.0, base / 8.0, np.where(wavelen < 2048.0, base, middle))
    return np.concatenate([freq, freq]).astype(np.float32)[None, :]


class Place:
    def __init__(self, ctx_size, head_size):
        self.Y = ctx_size // 2
        self.Z = head_size // X
        ctx = lax.axis_index("ctx")
        head = lax.axis_index("head")
        self.ctx, self.head = ctx, head
        self.y = ctx // 2
        self.c = ctx % 2
        self.x = head // self.Z
        self.z = head % self.Z
        self.pair = self.x // 2
        self.hb = self.bit_of(self.x)
        self.k = 2 * self.y + self.hb
        self.mate = self.pair * 3 + (1 - self.hb) * (1 - 2 * self.pair)
        self.sgn = 1 - 2 * self.c

    def bit_of(self, x):
        pair = x // 2
        return pair * 3 + x * (1 - 2 * pair)

    def dev(self, y=None, c=None, x=None, z=None):
        y = self.y if y is None else y
        c = self.c if c is None else c
        x = self.x if x is None else x
        z = self.z if z is None else z
        return (y * 2 + c, x * self.Z + z)

    def z_at(self, offset):
        return (self.z + self.sgn * offset + 2 * self.Z) % self.Z

    def along_z(self, offset):
        return self.dev(z=self.z_at(offset))

    def around(self):
        return [
            (dz, dx, self.dev(x=(self.x + dx) % X, z=self.z_at(dz)))
            for dz in (1, -1, 0)
            for dx in range(X)
            if dz or dx
        ]

    def key_partner(self, d):
        k = (self.k + d) % (2 * self.Y)
        hb = k % 2
        x = self.pair * 3 + hb * (1 - 2 * self.pair)
        return k, self.dev(y=k // 2, x=x)


def barrier(devices):
    sem = pltpu.get_barrier_semaphore()
    for device in devices:
        pl.semaphore_signal(sem, inc=1, device_id=device, device_id_type=MESH)
    pl.semaphore_wait(sem, len(devices))


def remote(src, dst, send, recv, device):
    return pltpu.make_async_remote_copy(
        src_ref=src, dst_ref=dst, send_sem=send, recv_sem=recv, device_id=device, device_id_type=MESH
    )


def turn(data, cosine, sine):
    data = data.astype(jnp.float32)
    return (data * cosine + pltpu.roll(data, HD // 2, 1) * sine).astype(jnp.bfloat16)


def trig(place, freq):
    angle = place.astype(jnp.float32) * freq
    lane = lax.broadcasted_iota(jnp.int32, angle.shape, 1)
    sine = jnp.sin(angle)
    return jnp.cos(angle), jnp.where(lane < HD // 2, -sine, sine)


def gather_kernel(
    sizes, cl_ref, sl_ref, freq_ref, q_ref, sk_ref, sv_ref, k_ref, v_ref,
    qo, ko, vo, sko, svo,
    cl, sl, freq_in, k_in, q_in, sk_in, qs, qb, sks, ks, in_sem,
    q_in_sem, span_sem, v_send, v_recv, k_send, k_recv, q_send, q_recv, on_send,
    core_send, core_recv, own_sem, q_own_sem, pair_send, pair_recv,
):
    at = Place(*sizes)
    Y, Z = at.Y, at.Z
    heads = 2 * Y
    rows, tokens = q_ref.shape[0], k_ref.shape[0]
    ndoc = cl.shape[0]

    reads = [
        pltpu.make_async_copy(cl_ref, cl, in_sem.at[0]),
        pltpu.make_async_copy(sl_ref, sl, in_sem.at[1]),
        pltpu.make_async_copy(freq_ref, freq_in, in_sem.at[2]),
    ]
    k_read = pltpu.make_async_copy(k_ref, k_in, in_sem.at[3])
    for hb in range(2):
        column = pl.multiple_of((2 * at.y + hb) * (GROUP * HD) + at.c * (2 * HD), 2 * HD)
        reads.append(
            pltpu.make_async_copy(q_ref.at[:, pl.ds(column, 2 * HD)], q_in.at[hb], q_in_sem.at[hb])
        )
    own = pl.multiple_of(at.k * HD, HD)
    theirs = pl.multiple_of((at.k + 1 - 2 * at.hb) * HD, HD)
    for i, column in enumerate((own, theirs)):
        reads.append(
            pltpu.make_async_copy(sk_ref.at[:, pl.ds(column, HD)], sk_in.at[i], span_sem.at[i])
        )
    for copy in reads:
        copy.start()
    k_read.start()
    sv_copy = pltpu.make_async_copy(sv_ref.at[:, pl.ds(own, HD)], svo.at[0], span_sem.at[2])
    sv_copy.start()
    v_own = pltpu.make_async_copy(v_ref.at[:, pl.ds(own, HD)], vo.at[at.k], own_sem.at[0])
    v_own.start()

    partners = [at.key_partner(d) for d in range(1, heads)]
    other_core = at.dev(c=1 - at.c)
    around = at.around()
    greet = [at.dev(y=(at.y + dy) % Y, x=x) for dy in range(1, Y) for x in (at.x, at.mate)]
    greet += [device for _, _, device in around] + [at.along_z(2), at.along_z(-2), other_core]
    barrier(greet)

    for copy in reads:
        copy.wait()
    freq = freq_in[...]
    row = at.head * rows + lax.broadcasted_iota(jnp.int32, (rows, HD), 0)
    shift = jnp.zeros((rows, HD), jnp.int32)
    start = jnp.int32(0)
    for d in range(ndoc):
        shift = jnp.where(row >= start, cl[d] - start, shift)
        start = start + sl[d]
    cosine, sine = trig(row + shift, freq)
    for hb in range(2):
        for h in range(2):
            qs[hb, h * rows : (h + 1) * rows, :] = turn(
                q_in[hb, :, h * HD : (h + 1) * HD], cosine, sine
            )
    for i in range(2):
        sks[i] = turn(sk_in[i], cosine, sine)

    q_own = pltpu.make_async_copy(qs.at[at.hb], qb.at[at.z, at.x], own_sem.at[1])
    q_own.start()
    first_copies = []
    for dz, dx, device in around:
        copy = remote(
            qs.at[at.bit_of((at.x + dx) % X)], qb.at[at.z, at.x],
            q_send.at[dz + 1, dx], q_recv.at[-dz + 4, dx], device,
        )
        copy.start()
        first_copies.append(copy)
    pair_copies = [
        remote(sks.at[1], sko.at[1], pair_send.at[0], pair_recv.at[0], at.dev(x=at.mate)),
        remote(
            sv_ref.at[:, pl.ds(theirs, HD)], svo.at[1], pair_send.at[1], pair_recv.at[1],
            at.dev(x=at.mate),
        ),
    ]
    sk_own = pltpu.make_async_copy(sks.at[0], sko.at[0], own_sem.at[2])
    for copy in pair_copies + [sk_own]:
        copy.start()

    onward = []

    def piece(offset, n):
        return qb.at[at.z_at(offset), (at.x - n + X) % X]

    def arrived(offset, n):
        part = piece(offset, n)
        remote(part, part, q_send.at[0, 0], q_recv.at[offset + 4, n], other_core).wait_recv()

    def pass_on(offset, n, far):
        part = piece(offset, n)
        copy = remote(
            part, part, on_send.at[len(onward)], q_recv.at[offset - far + 4, n], at.along_z(far)
        )
        copy.start()
        onward.append(copy)

    slabs = (0, -1, 1, -2, 2, -3, 3, -4)
    cores, kept = [], []

    def to_core(offset):
        i = slabs.index(offset)
        z = at.z_at(offset)
        copy = remote(
            qb.at[z], qo.at[at.c, z], core_send.at[i], core_recv.at[i], other_core
        )
        copy.start()
        cores.append(copy)
        copy = pltpu.make_async_copy(qb.at[z], qo.at[at.c, z], q_own_sem.at[i])
        copy.start()
        kept.append(copy)

    order = sorted(range(1, heads), key=lambda d: -min(d, heads - d))
    v_copies = []
    for d in order:
        k, device = partners[d - 1]
        column = pl.multiple_of(k * HD, HD)
        copy = remote(
            v_ref.at[:, pl.ds(column, HD)], vo.at[at.k], v_send.at[d], v_recv.at[d], device
        )
        copy.start()
        v_copies.append(copy)

    token = (at.ctx * sizes[1] + at.head) * tokens + lax.broadcasted_iota(jnp.int32, (tokens, HD), 0)
    first = jnp.zeros((tokens, HD), jnp.int32)
    start = jnp.int32(0)
    for d in range(ndoc):
        first = jnp.where(token >= start, start, first)
        start = start + cl[d]
    cosine, sine = trig(token - first, freq)
    k_read.wait()
    k_copies = []
    for d in order:
        k, device = partners[d - 1]
        column = pl.multiple_of(k * HD, HD)
        ks[d] = turn(k_in[:, pl.ds(column, HD)], cosine, sine)
        copy = remote(ks.at[d], ko.at[at.k], k_send.at[d], k_recv.at[d], device)
        copy.start()
        k_copies.append(copy)
    ks[0] = turn(k_in[:, pl.ds(own, HD)], cosine, sine)
    k_own = pltpu.make_async_copy(ks.at[0], ko.at[at.k], own_sem.at[3])
    k_own.start()

    for n in range(X):
        for offset in (-1, 1):
            arrived(offset, n)
            pass_on(offset, n, -offset)
    q_own.wait()
    for n in range(1, X):
        arrived(0, n)
    for offset in (0, -1, 1):
        to_core(offset)
    for n in range(X):
        for offset in (-2, 2):
            arrived(offset, n)
            if offset == -2:
                pass_on(offset, n, 2)
            pass_on(offset, n, -offset // 2)
    for offset in (-2, 2):
        to_core(offset)
    for offset in (-3, 3, -4):
        for n in range(X):
            arrived(offset, n)
        to_core(offset)

    for i, offset in enumerate(slabs):
        z = at.z_at(-offset)
        remote(
            qb.at[z], qo.at[1 - at.c, z], core_send.at[i], core_recv.at[i], other_core
        ).wait_recv()
    for copy in v_copies + k_copies + pair_copies:
        copy.wait_recv()
    for copy in v_copies + k_copies + pair_copies + first_copies + onward + cores:
        copy.wait_send()
    for copy in kept + [v_own, k_own, sk_own, sv_copy]:
        copy.wait()


def attend_kernel(
    sizes, cl_ref, sl_ref, q_hbm, k_hbm, v_hbm, sk_hbm, sv_hbm, part_ref, stat_ref,
    acc, cl, sl, q_ref, k_ref, v_ref, vt_ref, s_even, s_odd, w_odd, f_odd,
    cache_at, span_at, g_block, g_low, g_high, g_first, g_end, g_causal, e_group, e_chunk, in_sem,
):
    at = Place(*sizes)
    Z = at.Z
    blocks, tokens, _ = k_hbm.shape
    rows = sk_hbm.shape[1]
    lanes = 4 * rows
    ndoc = cl.shape[0]
    pairs = (
        (cl_ref, cl), (sl_ref, sl), (k_hbm, k_ref.at[pl.ds(0, blocks)]),
        (q_hbm, q_ref), (v_hbm, v_ref.at[pl.ds(0, blocks)]),
        (sk_hbm.at[at.c], k_ref.at[blocks, pl.ds(0, rows)]),
        (sv_hbm.at[at.c], v_ref.at[blocks, pl.ds(0, rows)]),
    )
    reads = [pltpu.make_async_copy(a, b, in_sem.at[i]) for i, (a, b) in enumerate(pairs)]
    for copy in reads:
        copy.start()

    k_ref[blocks, rows:, :] = jnp.zeros((tokens - rows, HD), jnp.bfloat16)
    v_ref[blocks, rows:, :] = jnp.zeros((tokens - rows, HD), jnp.bfloat16)
    half = lax.broadcasted_iota(jnp.int32, (2, Z, 2 * X, 2 * rows), 2)
    stat_ref[...] = jnp.where(half < X, FLOOR, 0.0)
    acc[...] = jnp.zeros_like(acc)
    w_odd[...] = jnp.zeros_like(w_odd)
    f_odd[...] = jnp.ones_like(f_odd)
    reads[0].wait()
    reads[1].wait()

    cache_at[0] = jnp.int32(0)
    span_at[0] = jnp.int32(0)
    for d in range(ndoc):
        cache_at[d + 1] = cache_at[d] + cl[d]
        span_at[d + 1] = span_at[d] + sl[d]

    far = jnp.int32(1 << 20)

    def none(group):
        g_block[group], g_low[group], g_high[group] = jnp.int32(0), jnp.int32(0), jnp.int32(0)
        g_first[group], g_end[group], g_causal[group] = jnp.int32(0), jnp.int32(0), far

    none(0)
    e_group[0], e_chunk[0] = jnp.int32(0), jnp.int32(0)

    def add_block(counts, block, starts, first, width, causal, row_first):
        doc_first, doc_last = jnp.int32(0), jnp.int32(0)
        for d in range(1, ndoc):
            doc_first += (starts[d] <= first).astype(jnp.int32)
            doc_last += (starts[d] < first + width).astype(jnp.int32)

        def add_doc(d, counts):
            group, entry = counts
            g_block[group] = block
            g_low[group] = jnp.maximum(starts[d] - first, 0)
            g_high[group] = jnp.minimum(starts[d + 1] - first, width)
            g_first[group] = jnp.maximum(span_at[d], row_first)
            g_end[group] = span_at[d + 1]
            g_causal[group] = causal
            low = jnp.maximum(span_at[d], row_first) // rows
            high = (span_at[d + 1] + rows - 1) // rows

            def add_chunk(n, entry):
                e_group[entry] = group
                e_chunk[entry] = n
                return entry + 1

            return group + 1, lax.fori_loop(low, high, add_chunk, entry)

        return lax.fori_loop(doc_first, doc_last + 1, add_doc, counts)

    def cache_block(b, counts):
        x = at.pair * 3 + (b % 2) * (1 - 2 * at.pair)
        first = (((b // 2) * 2 + at.c) * sizes[1] + x * Z + at.z) * tokens
        return add_block(counts, b, cache_at, first, tokens, far, 0)

    counts = lax.fori_loop(0, blocks, cache_block, (jnp.int32(1), jnp.int32(1)))
    first = (jnp.where(at.c == 0, at.x, at.mate) * Z + at.z) * rows
    _, count = add_block(counts, jnp.int32(blocks), span_at, first, rows, -first, first)
    for i in range(4):
        e_group[count + i], e_chunk[count + i] = jnp.int32(0), jnp.int32(0)

    for copy in reads[2:]:
        copy.wait()

    def turn_over(b, carry):
        vt_ref[b] = v_ref[b].T
        return carry

    lax.fori_loop(0, blocks + 1, turn_over, 0)

    lane = lax.broadcasted_iota(jnp.int32, (1, lanes), 1) % rows
    token = lax.broadcasted_iota(jnp.int32, (tokens, lanes), 0)

    def scores(i):
        n = e_chunk[i]
        x, z = n // Z, n % Z
        q = jnp.concatenate([q_ref[0, z, x], q_ref[1, z, x]], axis=0)
        return lax.dot_general(
            k_ref[g_block[e_group[i]]], q, (((1,), (1,)), ((), ())),
            preferred_element_type=jnp.float32,
        )

    def soften(i, s):
        group, n = e_group[i], e_chunk[i]
        x, z = n // Z, n % Z
        row = n * rows + lane
        here = (row >= g_first[group]) & (row < g_end[group])
        high = jnp.minimum(g_high[group], row + g_causal[group] + 1)
        s = jnp.where((token >= g_low[group]) & (token < high), s * SCALE, FLOOR)
        m_old = jnp.concatenate([stat_ref[c, z, pl.ds(x, 1), :] for c in range(2)], axis=1)
        l_old = jnp.concatenate([stat_ref[c, z, pl.ds(X + x, 1), :] for c in range(2)], axis=1)
        m_new = jnp.where(here, jnp.maximum(m_old, jnp.max(s, axis=0, keepdims=True)), m_old)
        w = jnp.exp2(s - jnp.where(here, m_new, -FLOOR))
        factor = jnp.exp2(m_old - m_new)
        l_new = l_old * factor + jnp.sum(w, axis=0, keepdims=True)
        for c in range(2):
            part = slice(c * 2 * rows, (c + 1) * 2 * rows)
            stat_ref[c, z, pl.ds(x, 1), :] = m_new[:, part]
            stat_ref[c, z, pl.ds(X + x, 1), :] = l_new[:, part]
        return w.astype(jnp.bfloat16), factor

    def product(i, w):
        return jnp.dot(vt_ref[g_block[e_group[i]]], w, preferred_element_type=jnp.float32)

    def update(i, o, factor):
        n = e_chunk[i]
        x, z = n // Z, n % Z
        for c in range(2):
            part = slice(c * 2 * rows, (c + 1) * 2 * rows)
            acc[c, z, x] = acc[c, z, x] * factor[:, part] + o[:, part]

    s_even[...] = scores(1)

    def step(j, carry):
        i = 2 * j + 1
        s_odd[...] = scores(i + 1)
        o_before = product(i - 1, w_odd[...])
        w, factor = soften(i, s_even[...])
        update(i - 1, o_before, f_odd[...])
        s_even[...] = scores(i + 2)
        o = product(i, w)
        w_next, factor_next = soften(i + 1, s_odd[...])
        update(i, o, factor)
        w_odd[...] = w_next
        f_odd[...] = factor_next
        return carry

    steps = count // 2
    lax.fori_loop(0, steps, step, 0)
    update(2 * steps, product(2 * steps, w_odd[...]), f_odd[...])
    part_ref[...] = acc[...].astype(jnp.bfloat16)


def reduce_kernel(
    sizes, part_hbm, stat_all, out_ref,
    part_ref, cr, cr_stat, sb, sb_stat, rb, rb_stat, fb, fb_stat, xr, xr_stat, factor_ref,
    core_send, core_recv, core_stat_send, core_stat_recv,
    ring_send, ring_recv, ring_stat_send, ring_stat_recv,
    x_send, x_recv, x_stat_send, x_stat_recv, out_send, out_recv, cross_send, cross_recv, own_sem,
    in_sem,
):
    at = Place(*sizes)
    Y, Z = at.Y, at.Z
    rows = out_ref.shape[0]
    read = pltpu.make_async_copy(part_hbm.at[at.c], part_ref, in_sem.at[0])
    read.start()
    stat_ref = stat_all.at[at.c]
    other_core = at.dev(c=1 - at.c)
    around = at.around()
    ends = [at.dev(y=(at.y + dy) % Y) for dy in range(1, Y)]
    greet = [device for _, _, device in around] + ends
    barrier(greet + [at.along_z(2), at.along_z(-2), other_core])

    slabs = (4, 3, -3, 2, -2, 1, -1, 0)
    stats_over = remote(
        stat_all.at[1 - at.c], cr_stat, core_stat_send.at[0], core_stat_recv.at[0], other_core
    )
    stats_over.start()
    sent = [stats_over]
    for i, offset in enumerate(slabs):
        z = at.z_at(-offset)
        copy = remote(
            part_hbm.at[1 - at.c, z], cr.at[z], core_send.at[i], core_recv.at[i], other_core
        )
        copy.start()
        sent.append(copy)

    def both_cores(offset):
        i, z = slabs.index(offset), at.z_at(offset)
        remote(part_ref.at[z], cr.at[z], core_send.at[i], core_recv.at[i], other_core).wait_recv()
        return [(part_ref.at[z], stat_ref.at[z]), (cr.at[z], cr_stat.at[z])]

    def ring_in(n, x):
        if x is None:
            remote(
                sb_stat.at[n], rb_stat.at[n], ring_stat_send.at[n], ring_stat_recv.at[n], other_core
            ).wait_recv()
        else:
            remote(
                sb.at[n, x], rb.at[n, x], ring_send.at[n, x], ring_recv.at[n, x], other_core
            ).wait_recv()

    def ring_out(n, device):
        def emit(x):
            if x is None:
                copy = remote(
                    sb_stat.at[n], rb_stat.at[n], ring_stat_send.at[n], ring_stat_recv.at[n], device
                )
            else:
                copy = remote(
                    sb.at[n, x], rb.at[n, x], ring_send.at[n, x], ring_recv.at[n, x], device
                )
            copy.start()
            sent.append(copy)

        return emit

    def join(sources, came, to, to_stat, emit, hold=None):
        for n in came:
            ring_in(n, None)
            sources = sources + [(rb.at[n], rb_stat.at[n])]
        stats = [stat[...] for _, stat in sources]
        top = functools.reduce(jnp.maximum, [s[:X] for s in stats])
        factors = [jnp.exp2(s[:X] - top) for s in stats]
        to_stat[:X, :] = top
        to_stat[X:, :] = sum(s[X:] * f for s, f in zip(stats, factors))
        emit(None)
        if hold is not None:
            for i, f in enumerate(factors):
                hold[i] = f

        def factor(i, x):
            return factors[i][x : x + 1] if hold is None else hold[i, pl.ds(x, 1), :]

        def piece(x):
            for n in came:
                ring_in(n, x)
            to[x] = sum(
                part[x].astype(jnp.float32) * factor(i, x) for i, (part, _) in enumerate(sources)
            ).astype(jnp.bfloat16)
            emit(x)

        return piece

    read.wait()
    stats_over.wait_recv()
    stages = (
        ((4, 2, 0, ()), (3, 1, 1, ()), (-3, -1, 2, ())),
        ((2, 1, 3, (0, 1)), (-2, -1, 4, (2,))),
    )
    def work(stage):
        pieces = [
            join(
                both_cores(offset), came, sb.at[n], sb_stat.at[n], ring_out(n, at.along_z(far))
            )
            for offset, far, n, came in stage
        ]
        for x in range(X):
            for piece in pieces:
                piece(x)

    def column_out(dz):
        def emit(x):
            for dx in range(X):
                if (dz or dx) and x is None:
                    copy = remote(
                        fb_stat.at[dz + 1], xr_stat.at[-dz + 1, at.x], x_stat_send.at[dz + 1, dx],
                        x_stat_recv.at[-dz + 1, dx], at.dev(x=(at.x + dx) % X, z=at.z_at(dz)),
                    )
                    copy.start()
                    sent.append(copy)

        return emit

    own = []

    def finish(last):
        pieces = [
            join(
                both_cores(dz), {0: (), 1: (3,), -1: (4,)}[dz], fb.at[dz + 1], fb_stat.at[dz + 1],
                column_out(dz), factor_ref.at[dz + 1],
            )
            for dz in last
        ]
        for dx in range(X):
            for dz, piece in zip(last, pieces):
                x = (at.x + dx) % X
                piece(x)
                if dz or dx:
                    copy = remote(
                        fb.at[dz + 1, x], xr.at[-dz + 1, at.x], x_send.at[dz + 1, dx],
                        x_recv.at[-dz + 1, dx], at.dev(x=x, z=at.z_at(dz)),
                    )
                    copy.start()
                    sent.append(copy)
                else:
                    own.extend((
                        pltpu.make_async_copy(fb.at[1, at.x], xr.at[1, at.x], own_sem.at[0]),
                        pltpu.make_async_copy(fb_stat.at[1], xr_stat.at[1, at.x], own_sem.at[1]),
                    ))
                    for copy in own:
                        copy.start()

    work(stages[0])
    finish((0,))
    work(stages[1])
    finish((1, -1))
    for copy in own:
        copy.wait()
    for dz in (0, 1, -1):
        for dx in range(X):
            if dz or dx:
                remote(
                    fb_stat.at[0], xr_stat.at[dz + 1, at.x], x_stat_send.at[dz + 1, dx],
                    x_stat_recv.at[dz + 1, dx], other_core,
                ).wait_recv()
                remote(
                    fb.at[0, 0], xr.at[dz + 1, at.x], x_send.at[dz + 1, dx], x_recv.at[dz + 1, dx],
                    other_core,
                ).wait_recv()

    def columns(y, hb, c):
        first = pl.multiple_of((2 * y + hb) * (GROUP * HD) + c * (2 * HD), 2 * HD)
        return out_ref.at[:, pl.ds(first, 2 * HD)]

    def cross(hb, dy):
        part = columns((at.y - dy + Y) % Y, hb, at.c)
        copy = remote(part, part, cross_send.at[hb, dy], cross_recv.at[hb, dy], other_core)
        copy.start()
        sent.append(copy)

    near = sorted(range(1, Y), key=lambda dy: min(dy, Y - dy))
    for hb, pair in enumerate(((0, 3), (1, 2))):
        sources = [(d, n) for n in pair for d in range(3)]
        tops = [xr_stat[d, n, pl.ds(at.x, 1), :] for d, n in sources]
        totals = [xr_stat[d, n, pl.ds(X + at.x, 1), :] for d, n in sources]
        top = functools.reduce(jnp.maximum, tops)
        factors = [jnp.exp2(t - top) for t in tops]
        total = sum(t * f for t, f in zip(totals, factors))
        value = sum(xr[d, n].astype(jnp.float32) * f for (d, n), f in zip(sources, factors))
        value = (value / total).T.astype(jnp.bfloat16)
        part = columns(at.y, hb, at.c)
        for h in range(2):
            part[:, h * HD : (h + 1) * HD] = value[h * rows : (h + 1) * rows]
        for dy in reversed(near):
            copy = remote(part, part, out_send.at[hb, dy], out_recv.at[hb, dy], ends[dy - 1])
            copy.start()
            sent.append(copy)
        cross(hb, 0)
    for hb in range(2):
        for dy in near:
            part = columns((at.y - dy + Y) % Y, hb, at.c)
            remote(part, part, out_send.at[hb, dy], out_recv.at[hb, dy], other_core).wait_recv()
            cross(hb, dy)
    for hb in range(2):
        for dy in range(Y):
            part = columns((at.y - dy + Y) % Y, hb, 1 - at.c)
            remote(part, part, cross_send.at[hb, dy], cross_recv.at[hb, dy], other_core).wait_recv()
    for copy in sent:
        copy.wait_send()


def body(queries, span_keys, span_values, cache_keys, cache_values, cache_lengths, span_lengths):
    sizes = (lax.axis_size("ctx"), lax.axis_size("head"))
    Y, Z = sizes[0] // 2, sizes[1] // X
    heads = 2 * Y
    rows, tokens = queries.shape[0], cache_keys.shape[0]
    bf16, f32 = jnp.bfloat16, jnp.float32
    lengths = pltpu.SMEM(cache_lengths.shape, jnp.int32)
    vmem = pl.BlockSpec(memory_space=pltpu.VMEM)
    hbm = pl.BlockSpec(memory_space=pltpu.HBM)
    dma = pltpu.SemaphoreType.DMA
    freq = jnp.asarray(inverse_freq())

    q_all, k_all, v_all, sk, sv = pl.pallas_call(
        functools.partial(gather_kernel, sizes),
        out_shape=(
            jax.ShapeDtypeStruct((2, Z, X, 2 * rows, HD), bf16),
            jax.ShapeDtypeStruct((heads, tokens, HD), bf16),
            jax.ShapeDtypeStruct((heads, tokens, HD), bf16),
            jax.ShapeDtypeStruct((2, rows, HD), bf16),
            jax.ShapeDtypeStruct((2, rows, HD), bf16),
        ),
        in_specs=[hbm] * 8,
        out_specs=(hbm,) * 5,
        scratch_shapes=[
            lengths, lengths, VMEM(freq.shape, f32), VMEM((tokens, heads * HD), bf16),
            VMEM((2, rows, 2 * HD), bf16),
            VMEM((2, rows, HD), bf16),
            VMEM((2, 2 * rows, HD), bf16),
            VMEM((Z, X, 2 * rows, HD), bf16),
            VMEM((2, rows, HD), bf16),
            VMEM((heads, tokens, HD), bf16),
            dma((4,)), dma((2,)), dma((3,)), dma((heads,)), dma((heads,)), dma((heads,)), dma((heads,)),
            dma((3, X)), dma((Z, X)), dma((5 * X,)), dma((Z,)), dma((Z,)),
            dma((4,)), dma((Z,)), dma((2,)), dma((2,)),
        ],
        compiler_params=pltpu.CompilerParams(
            collective_id=0, has_side_effects=True, vmem_limit_bytes=60 * 1024 * 1024
        ),
        name="gather",
    )(cache_lengths, span_lengths, freq, queries, span_keys, span_values, cache_keys, cache_values)

    ndoc = cache_lengths.shape[0]
    groups = (heads + 1) * ndoc + 1
    entries = (heads + 1) * (X * Z + ndoc) + 8

    def numbers(n):
        return pltpu.SMEM((n,), jnp.int32)

    parts, stats = pl.pallas_call(
        functools.partial(attend_kernel, sizes),
        out_shape=(
            jax.ShapeDtypeStruct((2, Z, X, HD, 2 * rows), bf16),
            jax.ShapeDtypeStruct((2, Z, 2 * X, 2 * rows), f32),
        ),
        in_specs=[hbm] * 7,
        out_specs=(vmem, vmem),
        scratch_shapes=[
            VMEM((2, Z, X, HD, 2 * rows), f32), lengths, lengths, VMEM(q_all.shape, bf16),
            VMEM((heads + 1, tokens, HD), bf16), VMEM((heads + 1, tokens, HD), bf16),
            VMEM((heads + 1, HD, tokens), bf16),
            VMEM((tokens, 4 * rows), f32), VMEM((tokens, 4 * rows), f32),
            VMEM((tokens, 4 * rows), bf16), VMEM((1, 4 * rows), f32),
            numbers(ndoc + 1), numbers(ndoc + 1), *[numbers(groups)] * 6,
            numbers(entries), numbers(entries), dma((7,)),
        ],
        compiler_params=pltpu.CompilerParams(vmem_limit_bytes=60 * 1024 * 1024),
        name="attend",
    )(cache_lengths, span_lengths, q_all, k_all, v_all, sk, sv)

    piece, stat = (HD, 2 * rows), (2 * X, 2 * rows)
    return pl.pallas_call(
        functools.partial(reduce_kernel, sizes),
        out_shape=jax.ShapeDtypeStruct(queries.shape, bf16),
        in_specs=[hbm, vmem],
        out_specs=vmem,
        scratch_shapes=[
            VMEM((Z, X) + piece, bf16),
            VMEM((Z, X) + piece, bf16), VMEM((Z,) + stat, f32),
            VMEM((5, X) + piece, bf16), VMEM((5,) + stat, f32),
            VMEM((5, X) + piece, bf16), VMEM((5,) + stat, f32),
            VMEM((3, X) + piece, bf16), VMEM((3,) + stat, f32),
            VMEM((3, X) + piece, bf16), VMEM((3, X) + stat, f32),
            VMEM((3, 3, X, 2 * rows), f32),
            dma((Z,)), dma((Z,)), dma((1,)), dma((1,)),
            dma((5, X)), dma((5, X)), dma((5,)), dma((5,)),
            dma((3, X)), dma((3, X)), dma((3, X)), dma((3, X)),
            dma((2, Y)), dma((2, Y)), dma((2, Y)), dma((2, Y)), dma((2,)), dma((1,)),
        ],
        compiler_params=pltpu.CompilerParams(
            collective_id=1, has_side_effects=True, vmem_limit_bytes=53 * 1024 * 1024
        ),
        name="reduce",
    )(parts, stats)


def solution(mesh):
    placed = (
        P("head", None),
        P("head", None),
        P("head", None),
        P(("ctx", "head"), None),
        P(("ctx", "head"), None),
        P(),
        P(),
    )
    return jax.shard_map(
        body, mesh=mesh, in_specs=placed, out_specs=P("head", None), check_vma=False
    )
```

```python
import functools
import math

import jax
import jax.numpy as jnp
import numpy as np
from jax import lax
from jax.experimental import pallas as pl
from jax.experimental.pallas import tpu as pltpu
from jax.sharding import PartitionSpec as P

HD = 128
GROUP = 4
X = 4
FLOOR = -1e30
MESH = pl.DeviceIdType.MESH
VMEM = pltpu.VMEM
SCALE = math.log2(math.e) / math.sqrt(HD)


def inverse_freq():
    counter = np.arange(HD // 2, dtype=np.float64)
    base = 500000.0 ** (-2.0 * counter / HD)
    wavelen = 2.0 * math.pi / base
    smooth = (8192.0 / wavelen - 1.0) / 3.0
    middle = (1.0 - smooth) * base / 8.0 + smooth * base
    freq = np.where(wavelen > 8192.0, base / 8.0, np.where(wavelen < 2048.0, base, middle))
    return np.concatenate([freq, freq]).astype(np.float32)[None, :]


class Place:
    def __init__(self, ctx_size, head_size):
        self.Y = ctx_size // 2
        self.Z = head_size // X
        ctx = lax.axis_index("ctx")
        head = lax.axis_index("head")
        self.ctx, self.head = ctx, head
        self.y = ctx // 2
        self.c = ctx % 2
        self.x = head // self.Z
        self.z = head % self.Z
        self.pair = self.x // 2
        self.hb = self.bit_of(self.x)
        self.k = 2 * self.y + self.hb
        self.mate = self.pair * 3 + (1 - self.hb) * (1 - 2 * self.pair)
        self.sgn = 1 - 2 * self.c

    def bit_of(self, x):
        pair = x // 2
        return pair * 3 + x * (1 - 2 * pair)

    def dev(self, y=None, c=None, x=None, z=None):
        y = self.y if y is None else y
        c = self.c if c is None else c
        x = self.x if x is None else x
        z = self.z if z is None else z
        return (y * 2 + c, x * self.Z + z)

    def z_at(self, offset):
        return (self.z + self.sgn * offset + 2 * self.Z) % self.Z

    def along_z(self, offset):
        return self.dev(z=self.z_at(offset))

    def around(self):
        return [
            (dz, dx, self.dev(x=(self.x + dx) % X, z=self.z_at(dz)))
            for dz in (1, -1, 0)
            for dx in range(X)
            if dz or dx
        ]

    def key_partner(self, d):
        k = (self.k + d) % (2 * self.Y)
        hb = k % 2
        x = self.pair * 3 + hb * (1 - 2 * self.pair)
        return k, self.dev(y=k // 2, x=x)


def barrier(devices):
    sem = pltpu.get_barrier_semaphore()
    for device in devices:
        pl.semaphore_signal(sem, inc=1, device_id=device, device_id_type=MESH)
    pl.semaphore_wait(sem, len(devices))


def remote(src, dst, send, recv, device):
    return pltpu.make_async_remote_copy(
        src_ref=src, dst_ref=dst, send_sem=send, recv_sem=recv, device_id=device, device_id_type=MESH
    )


def turn(data, cosine, sine):
    data = data.astype(jnp.float32)
    return (data * cosine + pltpu.roll(data, HD // 2, 1) * sine).astype(jnp.bfloat16)


def trig(place, freq):
    angle = place.astype(jnp.float32) * freq
    lane = lax.broadcasted_iota(jnp.int32, angle.shape, 1)
    sine = jnp.sin(angle)
    return jnp.cos(angle), jnp.where(lane < HD // 2, -sine, sine)


def gather_kernel(
    sizes, cl_ref, sl_ref, freq_ref, q_ref, sk_ref, sv_ref, k_ref, v_ref,
    qo, ko, vo, sko, svo,
    cl, sl, freq_in, k_in, q_in, sk_in, qs, qb, sks, ks, in_sem,
    q_in_sem, span_sem, v_send, v_recv, k_send, k_recv, q_send, q_recv, on_send,
    core_send, core_recv, own_sem, q_own_sem, pair_send, pair_recv,
):
    at = Place(*sizes)
    Y, Z = at.Y, at.Z
    heads = 2 * Y
    rows, tokens = q_ref.shape[0], k_ref.shape[0]
    ndoc = cl.shape[0]

    reads = [
        pltpu.make_async_copy(cl_ref, cl, in_sem.at[0]),
        pltpu.make_async_copy(sl_ref, sl, in_sem.at[1]),
        pltpu.make_async_copy(freq_ref, freq_in, in_sem.at[2]),
    ]
    k_read = pltpu.make_async_copy(k_ref, k_in, in_sem.at[3])
    for hb in range(2):
        column = pl.multiple_of((2 * at.y + hb) * (GROUP * HD) + at.c * (2 * HD), 2 * HD)
        reads.append(
            pltpu.make_async_copy(q_ref.at[:, pl.ds(column, 2 * HD)], q_in.at[hb], q_in_sem.at[hb])
        )
    own = pl.multiple_of(at.k * HD, HD)
    theirs = pl.multiple_of((at.k + 1 - 2 * at.hb) * HD, HD)
    for i, column in enumerate((own, theirs)):
        reads.append(
            pltpu.make_async_copy(sk_ref.at[:, pl.ds(column, HD)], sk_in.at[i], span_sem.at[i])
        )
    for copy in reads:
        copy.start()
    k_read.start()
    sv_copy = pltpu.make_async_copy(sv_ref.at[:, pl.ds(own, HD)], svo.at[0], span_sem.at[2])
    sv_copy.start()
    v_own = pltpu.make_async_copy(v_ref.at[:, pl.ds(own, HD)], vo.at[at.k], own_sem.at[0])
    v_own.start()

    partners = [at.key_partner(d) for d in range(1, heads)]
    other_core = at.dev(c=1 - at.c)
    around = at.around()
    greet = [at.dev(y=(at.y + dy) % Y, x=x) for dy in range(1, Y) for x in (at.x, at.mate)]
    greet += [device for _, _, device in around] + [at.along_z(2), at.along_z(-2), other_core]
    barrier(greet)

    for copy in reads:
        copy.wait()
    freq = freq_in[...]
    row = at.head * rows + lax.broadcasted_iota(jnp.int32, (rows, HD), 0)
    shift = jnp.zeros((rows, HD), jnp.int32)
    start = jnp.int32(0)
    for d in range(ndoc):
        shift = jnp.where(row >= start, cl[d] - start, shift)
        start = start + sl[d]
    cosine, sine = trig(row + shift, freq)
    for hb in range(2):
        for h in range(2):
            qs[hb, h * rows : (h + 1) * rows, :] = turn(
                q_in[hb, :, h * HD : (h + 1) * HD], cosine, sine
            )
    for i in range(2):
        sks[i] = turn(sk_in[i], cosine, sine)

    q_own = pltpu.make_async_copy(qs.at[at.hb], qb.at[at.z, at.x], own_sem.at[1])
    q_own.start()
    first_copies = []
    for dz, dx, device in around:
        copy = remote(
            qs.at[at.bit_of((at.x + dx) % X)], qb.at[at.z, at.x],
            q_send.at[dz + 1, dx], q_recv.at[-dz + 4, dx], device,
        )
        copy.start()
        first_copies.append(copy)
    pair_copies = [
        remote(sks.at[1], sko.at[1], pair_send.at[0], pair_recv.at[0], at.dev(x=at.mate)),
        remote(
            sv_ref.at[:, pl.ds(theirs, HD)], svo.at[1], pair_send.at[1], pair_recv.at[1],
            at.dev(x=at.mate),
        ),
    ]
    sk_own = pltpu.make_async_copy(sks.at[0], sko.at[0], own_sem.at[2])
    for copy in pair_copies + [sk_own]:
        copy.start()

    onward = []

    def piece(offset, n):
        return qb.at[at.z_at(offset), (at.x - n + X) % X]

    def arrived(offset, n):
        part = piece(offset, n)
        remote(part, part, q_send.at[0, 0], q_recv.at[offset + 4, n], other_core).wait_recv()

    def pass_on(offset, n, far):
        part = piece(offset, n)
        copy = remote(
            part, part, on_send.at[len(onward)], q_recv.at[offset - far + 4, n], at.along_z(far)
        )
        copy.start()
        onward.append(copy)

    slabs = (0, -1, 1, -2, 2, -3, 3, -4)
    cores, kept = [], []

    def to_core(offset):
        i = slabs.index(offset)
        z = at.z_at(offset)
        copy = remote(
            qb.at[z], qo.at[at.c, z], core_send.at[i], core_recv.at[i], other_core
        )
        copy.start()
        cores.append(copy)
        copy = pltpu.make_async_copy(qb.at[z], qo.at[at.c, z], q_own_sem.at[i])
        copy.start()
        kept.append(copy)

    order = sorted(range(1, heads), key=lambda d: -min(d, heads - d))
    v_copies = []
    for d in order:
        k, device = partners[d - 1]
        column = pl.multiple_of(k * HD, HD)
        copy = remote(
            v_ref.at[:, pl.ds(column, HD)], vo.at[at.k], v_send.at[d], v_recv.at[d], device
        )
        copy.start()
        v_copies.append(copy)

    token = (at.ctx * sizes[1] + at.head) * tokens + lax.broadcasted_iota(jnp.int32, (tokens, HD), 0)
    first = jnp.zeros((tokens, HD), jnp.int32)
    start = jnp.int32(0)
    for d in range(ndoc):
        first = jnp.where(token >= start, start, first)
        start = start + cl[d]
    cosine, sine = trig(token - first, freq)
    k_read.wait()
    k_copies = []
    for d in order:
        k, device = partners[d - 1]
        column = pl.multiple_of(k * HD, HD)
        ks[d] = turn(k_in[:, pl.ds(column, HD)], cosine, sine)
        copy = remote(ks.at[d], ko.at[at.k], k_send.at[d], k_recv.at[d], device)
        copy.start()
        k_copies.append(copy)
    ks[0] = turn(k_in[:, pl.ds(own, HD)], cosine, sine)
    k_own = pltpu.make_async_copy(ks.at[0], ko.at[at.k], own_sem.at[3])
    k_own.start()

    for n in range(X):
        for offset in (-1, 1):
            arrived(offset, n)
            pass_on(offset, n, -offset)
    q_own.wait()
    for n in range(1, X):
        arrived(0, n)
    for offset in (0, -1, 1):
        to_core(offset)
    for n in range(X):
        for offset in (-2, 2):
            arrived(offset, n)
            if offset == -2:
                pass_on(offset, n, 2)
            pass_on(offset, n, -offset // 2)
    for offset in (-2, 2):
        to_core(offset)
    for offset in (-3, 3, -4):
        for n in range(X):
            arrived(offset, n)
        to_core(offset)

    for i, offset in enumerate(slabs):
        z = at.z_at(-offset)
        remote(
            qb.at[z], qo.at[1 - at.c, z], core_send.at[i], core_recv.at[i], other_core
        ).wait_recv()
    for copy in v_copies + k_copies + pair_copies:
        copy.wait_recv()
    for copy in v_copies + k_copies + pair_copies + first_copies + onward + cores:
        copy.wait_send()
    for copy in kept + [v_own, k_own, sk_own, sv_copy]:
        copy.wait()


def attend_kernel(
    sizes, cl_ref, sl_ref, q_hbm, k_hbm, v_hbm, sk_hbm, sv_hbm, part_ref, stat_ref,
    acc, cl, sl, q_ref, k_ref, v_ref, vt_ref, s_even, s_odd, w_odd, f_odd,
    cache_at, span_at, g_block, g_low, g_high, g_first, g_end, g_causal, e_group, e_chunk, in_sem,
):
    at = Place(*sizes)
    Z = at.Z
    blocks, tokens, _ = k_hbm.shape
    rows = sk_hbm.shape[1]
    lanes = 4 * rows
    ndoc = cl.shape[0]
    pairs = (
        (cl_ref, cl), (sl_ref, sl), (k_hbm, k_ref.at[pl.ds(0, blocks)]),
        (q_hbm, q_ref), (v_hbm, v_ref.at[pl.ds(0, blocks)]),
        (sk_hbm.at[at.c], k_ref.at[blocks, pl.ds(0, rows)]),
        (sv_hbm.at[at.c], v_ref.at[blocks, pl.ds(0, rows)]),
    )
    reads = [pltpu.make_async_copy(a, b, in_sem.at[i]) for i, (a, b) in enumerate(pairs)]
    for copy in reads:
        copy.start()

    k_ref[blocks, rows:, :] = jnp.zeros((tokens - rows, HD), jnp.bfloat16)
    v_ref[blocks, rows:, :] = jnp.zeros((tokens - rows, HD), jnp.bfloat16)
    half = lax.broadcasted_iota(jnp.int32, (2, Z, 2 * X, 2 * rows), 2)
    stat_ref[...] = jnp.where(half < X, FLOOR, 0.0)
    acc[...] = jnp.zeros_like(acc)
    w_odd[...] = jnp.zeros_like(w_odd)
    f_odd[...] = jnp.ones_like(f_odd)
    reads[0].wait()
    reads[1].wait()

    cache_at[0] = jnp.int32(0)
    span_at[0] = jnp.int32(0)
    for d in range(ndoc):
        cache_at[d + 1] = cache_at[d] + cl[d]
        span_at[d + 1] = span_at[d] + sl[d]

    far = jnp.int32(1 << 20)

    def none(group):
        g_block[group], g_low[group], g_high[group] = jnp.int32(0), jnp.int32(0), jnp.int32(0)
        g_first[group], g_end[group], g_causal[group] = jnp.int32(0), jnp.int32(0), far

    none(0)
    e_group[0], e_chunk[0] = jnp.int32(0), jnp.int32(0)

    def add_block(counts, block, starts, first, width, causal, row_first):
        doc_first, doc_last = jnp.int32(0), jnp.int32(0)
        for d in range(1, ndoc):
            doc_first += (starts[d] <= first).astype(jnp.int32)
            doc_last += (starts[d] < first + width).astype(jnp.int32)

        def add_doc(d, counts):
            group, entry = counts
            g_block[group] = block
            g_low[group] = jnp.maximum(starts[d] - first, 0)
            g_high[group] = jnp.minimum(starts[d + 1] - first, width)
            g_first[group] = jnp.maximum(span_at[d], row_first)
            g_end[group] = span_at[d + 1]
            g_causal[group] = causal
            low = jnp.maximum(span_at[d], row_first) // rows
            high = (span_at[d + 1] + rows - 1) // rows

            def add_chunk(n, entry):
                e_group[entry] = group
                e_chunk[entry] = n
                return entry + 1

            return group + 1, lax.fori_loop(low, high, add_chunk, entry)

        return lax.fori_loop(doc_first, doc_last + 1, add_doc, counts)

    def cache_block(b, counts):
        x = at.pair * 3 + (b % 2) * (1 - 2 * at.pair)
        first = (((b // 2) * 2 + at.c) * sizes[1] + x * Z + at.z) * tokens
        return add_block(counts, b, cache_at, first, tokens, far, 0)

    counts = lax.fori_loop(0, blocks, cache_block, (jnp.int32(1), jnp.int32(1)))
    first = (jnp.where(at.c == 0, at.x, at.mate) * Z + at.z) * rows
    _, count = add_block(counts, jnp.int32(blocks), span_at, first, rows, -first, first)
    for i in range(4):
        e_group[count + i], e_chunk[count + i] = jnp.int32(0), jnp.int32(0)

    for copy in reads[2:]:
        copy.wait()

    def turn_over(b, carry):
        vt_ref[b] = v_ref[b].T
        return carry

    lax.fori_loop(0, blocks + 1, turn_over, 0)

    lane = lax.broadcasted_iota(jnp.int32, (1, lanes), 1) % rows
    token = lax.broadcasted_iota(jnp.int32, (tokens, lanes), 0)

    def scores(i):
        n = e_chunk[i]
        x, z = n // Z, n % Z
        q = jnp.concatenate([q_ref[0, z, x], q_ref[1, z, x]], axis=0)
        return lax.dot_general(
            k_ref[g_block[e_group[i]]], q, (((1,), (1,)), ((), ())),
            preferred_element_type=jnp.float32,
        )

    def soften(i, s):
        group, n = e_group[i], e_chunk[i]
        x, z = n // Z, n % Z
        row = n * rows + lane
        here = (row >= g_first[group]) & (row < g_end[group])
        high = jnp.minimum(g_high[group], row + g_causal[group] + 1)
        s = jnp.where((token >= g_low[group]) & (token < high), s * SCALE, FLOOR)
        m_old = jnp.concatenate([stat_ref[c, z, pl.ds(x, 1), :] for c in range(2)], axis=1)
        l_old = jnp.concatenate([stat_ref[c, z, pl.ds(X + x, 1), :] for c in range(2)], axis=1)
        m_new = jnp.where(here, jnp.maximum(m_old, jnp.max(s, axis=0, keepdims=True)), m_old)
        w = jnp.exp2(s - jnp.where(here, m_new, -FLOOR))
        factor = jnp.exp2(m_old - m_new)
        l_new = l_old * factor + jnp.sum(w, axis=0, keepdims=True)
        for c in range(2):
            part = slice(c * 2 * rows, (c + 1) * 2 * rows)
            stat_ref[c, z, pl.ds(x, 1), :] = m_new[:, part]
            stat_ref[c, z, pl.ds(X + x, 1), :] = l_new[:, part]
        return w.astype(jnp.bfloat16), factor

    def product(i, w):
        return jnp.dot(vt_ref[g_block[e_group[i]]], w, preferred_element_type=jnp.float32)

    def update(i, o, factor):
        n = e_chunk[i]
        x, z = n // Z, n % Z
        for c in range(2):
            part = slice(c * 2 * rows, (c + 1) * 2 * rows)
            acc[c, z, x] = acc[c, z, x] * factor[:, part] + o[:, part]

    s_even[...] = scores(1)

    def step(j, carry):
        i = 2 * j + 1
        s_odd[...] = scores(i + 1)
        o_before = product(i - 1, w_odd[...])
        w, factor = soften(i, s_even[...])
        update(i - 1, o_before, f_odd[...])
        s_even[...] = scores(i + 2)
        o = product(i, w)
        w_next, factor_next = soften(i + 1, s_odd[...])
        update(i, o, factor)
        w_odd[...] = w_next
        f_odd[...] = factor_next
        return carry

    steps = count // 2
    lax.fori_loop(0, steps, step, 0)
    update(2 * steps, product(2 * steps, w_odd[...]), f_odd[...])
    part_ref[...] = acc[...].astype(jnp.bfloat16)


def reduce_kernel(
    sizes, part_hbm, stat_all, out_ref,
    part_ref, cr, cr_stat, sb, sb_stat, rb, rb_stat, fb, fb_stat, xr, xr_stat, factor_ref,
    core_send, core_recv, core_stat_send, core_stat_recv,
    ring_send, ring_recv, ring_stat_send, ring_stat_recv,
    x_send, x_recv, x_stat_send, x_stat_recv, out_send, out_recv, cross_send, cross_recv, own_sem,
    in_sem,
):
    at = Place(*sizes)
    Y, Z = at.Y, at.Z
    rows = out_ref.shape[0]
    read = pltpu.make_async_copy(part_hbm.at[at.c], part_ref, in_sem.at[0])
    read.start()
    stat_ref = stat_all.at[at.c]
    other_core = at.dev(c=1 - at.c)
    around = at.around()
    ends = [at.dev(y=(at.y + dy) % Y) for dy in range(1, Y)]
    greet = [device for _, _, device in around] + ends
    barrier(greet + [at.along_z(2), at.along_z(-2), other_core])

    slabs = (4, 3, -3, 2, -2, 1, -1, 0)
    stats_over = remote(
        stat_all.at[1 - at.c], cr_stat, core_stat_send.at[0], core_stat_recv.at[0], other_core
    )
    stats_over.start()
    sent = [stats_over]
    for i, offset in enumerate(slabs):
        z = at.z_at(-offset)
        copy = remote(
            part_hbm.at[1 - at.c, z], cr.at[z], core_send.at[i], core_recv.at[i], other_core
        )
        copy.start()
        sent.append(copy)

    def both_cores(offset):
        i, z = slabs.index(offset), at.z_at(offset)
        remote(part_ref.at[z], cr.at[z], core_send.at[i], core_recv.at[i], other_core).wait_recv()
        return [(part_ref.at[z], stat_ref.at[z]), (cr.at[z], cr_stat.at[z])]

    def ring_in(n, x):
        if x is None:
            remote(
                sb_stat.at[n], rb_stat.at[n], ring_stat_send.at[n], ring_stat_recv.at[n], other_core
            ).wait_recv()
        else:
            remote(
                sb.at[n, x], rb.at[n, x], ring_send.at[n, x], ring_recv.at[n, x], other_core
            ).wait_recv()

    def ring_out(n, device):
        def emit(x):
            if x is None:
                copy = remote(
                    sb_stat.at[n], rb_stat.at[n], ring_stat_send.at[n], ring_stat_recv.at[n], device
                )
            else:
                copy = remote(
                    sb.at[n, x], rb.at[n, x], ring_send.at[n, x], ring_recv.at[n, x], device
                )
            copy.start()
            sent.append(copy)

        return emit

    def join(sources, came, to, to_stat, emit, hold=None):
        for n in came:
            ring_in(n, None)
            sources = sources + [(rb.at[n], rb_stat.at[n])]
        stats = [stat[...] for _, stat in sources]
        top = functools.reduce(jnp.maximum, [s[:X] for s in stats])
        factors = [jnp.exp2(s[:X] - top) for s in stats]
        to_stat[:X, :] = top
        to_stat[X:, :] = sum(s[X:] * f for s, f in zip(stats, factors))
        emit(None)
        if hold is not None:
            for i, f in enumerate(factors):
                hold[i] = f

        def factor(i, x):
            return factors[i][x : x + 1] if hold is None else hold[i, pl.ds(x, 1), :]

        def piece(x):
            for n in came:
                ring_in(n, x)
            to[x] = sum(
                part[x].astype(jnp.float32) * factor(i, x) for i, (part, _) in enumerate(sources)
            ).astype(jnp.bfloat16)
            emit(x)

        return piece

    read.wait()
    stats_over.wait_recv()
    stages = (
        ((4, 2, 0, ()),),
        ((3, 1, 1, ()), (-3, -1, 2, ())),
        ((2, 1, 3, (0, 1)), (-2, -1, 4, (2,))),
    )
    def work(stage):
        pieces = [
            join(
                both_cores(offset), came, sb.at[n], sb_stat.at[n], ring_out(n, at.along_z(far))
            )
            for offset, far, n, came in stage
        ]
        for x in range(X):
            for piece in pieces:
                piece(x)

    def column_out(dz):
        def emit(x):
            for dx in range(X):
                if (dz or dx) and x is None:
                    copy = remote(
                        fb_stat.at[dz + 1], xr_stat.at[-dz + 1, at.x], x_stat_send.at[dz + 1, dx],
                        x_stat_recv.at[-dz + 1, dx], at.dev(x=(at.x + dx) % X, z=at.z_at(dz)),
                    )
                    copy.start()
                    sent.append(copy)

        return emit

    own = []

    def finish(last):
        pieces = [
            join(
                both_cores(dz), {0: (), 1: (3,), -1: (4,)}[dz], fb.at[dz + 1], fb_stat.at[dz + 1],
                column_out(dz), factor_ref.at[dz + 1],
            )
            for dz in last
        ]
        for dx in range(X):
            for dz, piece in zip(last, pieces):
                x = (at.x + dx) % X
                piece(x)
                if dz or dx:
                    copy = remote(
                        fb.at[dz + 1, x], xr.at[-dz + 1, at.x], x_send.at[dz + 1, dx],
                        x_recv.at[-dz + 1, dx], at.dev(x=x, z=at.z_at(dz)),
                    )
                    copy.start()
                    sent.append(copy)
                else:
                    own.extend((
                        pltpu.make_async_copy(fb.at[1, at.x], xr.at[1, at.x], own_sem.at[0]),
                        pltpu.make_async_copy(fb_stat.at[1], xr_stat.at[1, at.x], own_sem.at[1]),
                    ))
                    for copy in own:
                        copy.start()

    work(stages[0])
    work(stages[1])
    finish((0,))
    work(stages[2])
    finish((1, -1))
    for copy in own:
        copy.wait()
    for dz in (0, 1, -1):
        for dx in range(X):
            if dz or dx:
                remote(
                    fb_stat.at[0], xr_stat.at[dz + 1, at.x], x_stat_send.at[dz + 1, dx],
                    x_stat_recv.at[dz + 1, dx], other_core,
                ).wait_recv()
                remote(
                    fb.at[0, 0], xr.at[dz + 1, at.x], x_send.at[dz + 1, dx], x_recv.at[dz + 1, dx],
                    other_core,
                ).wait_recv()

    def columns(y, hb, c):
        first = pl.multiple_of((2 * y + hb) * (GROUP * HD) + c * (2 * HD), 2 * HD)
        return out_ref.at[:, pl.ds(first, 2 * HD)]

    def cross(hb, dy):
        part = columns((at.y - dy + Y) % Y, hb, at.c)
        copy = remote(part, part, cross_send.at[hb, dy], cross_recv.at[hb, dy], other_core)
        copy.start()
        sent.append(copy)

    near = sorted(range(1, Y), key=lambda dy: min(dy, Y - dy))
    for hb, pair in enumerate(((0, 3), (1, 2))):
        sources = [(d, n) for n in pair for d in range(3)]
        tops = [xr_stat[d, n, pl.ds(at.x, 1), :] for d, n in sources]
        totals = [xr_stat[d, n, pl.ds(X + at.x, 1), :] for d, n in sources]
        top = functools.reduce(jnp.maximum, tops)
        factors = [jnp.exp2(t - top) for t in tops]
        total = sum(t * f for t, f in zip(totals, factors))
        value = sum(xr[d, n].astype(jnp.float32) * f for (d, n), f in zip(sources, factors))
        value = (value / total).T.astype(jnp.bfloat16)
        part = columns(at.y, hb, at.c)
        for h in range(2):
            part[:, h * HD : (h + 1) * HD] = value[h * rows : (h + 1) * rows]
        for dy in reversed(near):
            copy = remote(part, part, out_send.at[hb, dy], out_recv.at[hb, dy], ends[dy - 1])
            copy.start()
            sent.append(copy)
        cross(hb, 0)
    for hb in range(2):
        for dy in near:
            part = columns((at.y - dy + Y) % Y, hb, at.c)
            remote(part, part, out_send.at[hb, dy], out_recv.at[hb, dy], other_core).wait_recv()
            cross(hb, dy)
    for hb in range(2):
        for dy in range(Y):
            part = columns((at.y - dy + Y) % Y, hb, 1 - at.c)
            remote(part, part, cross_send.at[hb, dy], cross_recv.at[hb, dy], other_core).wait_recv()
    for copy in sent:
        copy.wait_send()


def body(queries, span_keys, span_values, cache_keys, cache_values, cache_lengths, span_lengths):
    sizes = (lax.axis_size("ctx"), lax.axis_size("head"))
    Y, Z = sizes[0] // 2, sizes[1] // X
    heads = 2 * Y
    rows, tokens = queries.shape[0], cache_keys.shape[0]
    bf16, f32 = jnp.bfloat16, jnp.float32
    lengths = pltpu.SMEM(cache_lengths.shape, jnp.int32)
    vmem = pl.BlockSpec(memory_space=pltpu.VMEM)
    hbm = pl.BlockSpec(memory_space=pltpu.HBM)
    dma = pltpu.SemaphoreType.DMA
    freq = jnp.asarray(inverse_freq())

    q_all, k_all, v_all, sk, sv = pl.pallas_call(
        functools.partial(gather_kernel, sizes),
        out_shape=(
            jax.ShapeDtypeStruct((2, Z, X, 2 * rows, HD), bf16),
            jax.ShapeDtypeStruct((heads, tokens, HD), bf16),
            jax.ShapeDtypeStruct((heads, tokens, HD), bf16),
            jax.ShapeDtypeStruct((2, rows, HD), bf16),
            jax.ShapeDtypeStruct((2, rows, HD), bf16),
        ),
        in_specs=[hbm] * 8,
        out_specs=(hbm,) * 5,
        scratch_shapes=[
            lengths, lengths, VMEM(freq.shape, f32), VMEM((tokens, heads * HD), bf16),
            VMEM((2, rows, 2 * HD), bf16),
            VMEM((2, rows, HD), bf16),
            VMEM((2, 2 * rows, HD), bf16),
            VMEM((Z, X, 2 * rows, HD), bf16),
            VMEM((2, rows, HD), bf16),
            VMEM((heads, tokens, HD), bf16),
            dma((4,)), dma((2,)), dma((3,)), dma((heads,)), dma((heads,)), dma((heads,)), dma((heads,)),
            dma((3, X)), dma((Z, X)), dma((5 * X,)), dma((Z,)), dma((Z,)),
            dma((4,)), dma((Z,)), dma((2,)), dma((2,)),
        ],
        compiler_params=pltpu.CompilerParams(
            collective_id=0, has_side_effects=True, vmem_limit_bytes=60 * 1024 * 1024
        ),
        name="gather",
    )(cache_lengths, span_lengths, freq, queries, span_keys, span_values, cache_keys, cache_values)

    ndoc = cache_lengths.shape[0]
    groups = (heads + 1) * ndoc + 1
    entries = (heads + 1) * (X * Z + ndoc) + 8

    def numbers(n):
        return pltpu.SMEM((n,), jnp.int32)

    parts, stats = pl.pallas_call(
        functools.partial(attend_kernel, sizes),
        out_shape=(
            jax.ShapeDtypeStruct((2, Z, X, HD, 2 * rows), bf16),
            jax.ShapeDtypeStruct((2, Z, 2 * X, 2 * rows), f32),
        ),
        in_specs=[hbm] * 7,
        out_specs=(vmem, vmem),
        scratch_shapes=[
            VMEM((2, Z, X, HD, 2 * rows), f32), lengths, lengths, VMEM(q_all.shape, bf16),
            VMEM((heads + 1, tokens, HD), bf16), VMEM((heads + 1, tokens, HD), bf16),
            VMEM((heads + 1, HD, tokens), bf16),
            VMEM((tokens, 4 * rows), f32), VMEM((tokens, 4 * rows), f32),
            VMEM((tokens, 4 * rows), bf16), VMEM((1, 4 * rows), f32),
            numbers(ndoc + 1), numbers(ndoc + 1), *[numbers(groups)] * 6,
            numbers(entries), numbers(entries), dma((7,)),
        ],
        compiler_params=pltpu.CompilerParams(vmem_limit_bytes=60 * 1024 * 1024),
        name="attend",
    )(cache_lengths, span_lengths, q_all, k_all, v_all, sk, sv)

    piece, stat = (HD, 2 * rows), (2 * X, 2 * rows)
    return pl.pallas_call(
        functools.partial(reduce_kernel, sizes),
        out_shape=jax.ShapeDtypeStruct(queries.shape, bf16),
        in_specs=[hbm, vmem],
        out_specs=vmem,
        scratch_shapes=[
            VMEM((Z, X) + piece, bf16),
            VMEM((Z, X) + piece, bf16), VMEM((Z,) + stat, f32),
            VMEM((5, X) + piece, bf16), VMEM((5,) + stat, f32),
            VMEM((5, X) + piece, bf16), VMEM((5,) + stat, f32),
            VMEM((3, X) + piece, bf16), VMEM((3,) + stat, f32),
            VMEM((3, X) + piece, bf16), VMEM((3, X) + stat, f32),
            VMEM((3, 3, X, 2 * rows), f32),
            dma((Z,)), dma((Z,)), dma((1,)), dma((1,)),
            dma((5, X)), dma((5, X)), dma((5,)), dma((5,)),
            dma((3, X)), dma((3, X)), dma((3, X)), dma((3, X)),
            dma((2, Y)), dma((2, Y)), dma((2, Y)), dma((2, Y)), dma((2,)), dma((1,)),
        ],
        compiler_params=pltpu.CompilerParams(
            collective_id=1, has_side_effects=True, vmem_limit_bytes=53 * 1024 * 1024
        ),
        name="reduce",
    )(parts, stats)


def solution(mesh):
    placed = (
        P("head", None),
        P("head", None),
        P("head", None),
        P(("ctx", "head"), None),
        P(("ctx", "head"), None),
        P(),
        P(),
    )
    return jax.shard_map(
        body, mesh=mesh, in_specs=placed, out_specs=P("head", None), check_vma=False
    )
```

```python
import functools
import math

import jax
import jax.numpy as jnp
import numpy as np
from jax import lax
from jax.experimental import pallas as pl
from jax.experimental.pallas import tpu as pltpu
from jax.sharding import PartitionSpec as P

HD = 128
GROUP = 4
X = 4
FLOOR = -1e30
MESH = pl.DeviceIdType.MESH
VMEM = pltpu.VMEM
SCALE = math.log2(math.e) / math.sqrt(HD)


def inverse_freq():
    counter = np.arange(HD // 2, dtype=np.float64)
    base = 500000.0 ** (-2.0 * counter / HD)
    wavelen = 2.0 * math.pi / base
    smooth = (8192.0 / wavelen - 1.0) / 3.0
    middle = (1.0 - smooth) * base / 8.0 + smooth * base
    freq = np.where(wavelen > 8192.0, base / 8.0, np.where(wavelen < 2048.0, base, middle))
    return np.concatenate([freq, freq]).astype(np.float32)[None, :]


class Place:
    def __init__(self, ctx_size, head_size):
        self.Y = ctx_size // 2
        self.Z = head_size // X
        ctx = lax.axis_index("ctx")
        head = lax.axis_index("head")
        self.ctx, self.head = ctx, head
        self.y = ctx // 2
        self.c = ctx % 2
        self.x = head // self.Z
        self.z = head % self.Z
        self.pair = self.x // 2
        self.hb = self.bit_of(self.x)
        self.k = 2 * self.y + self.hb
        self.mate = self.pair * 3 + (1 - self.hb) * (1 - 2 * self.pair)
        self.sgn = 1 - 2 * self.c

    def bit_of(self, x):
        pair = x // 2
        return pair * 3 + x * (1 - 2 * pair)

    def dev(self, y=None, c=None, x=None, z=None):
        y = self.y if y is None else y
        c = self.c if c is None else c
        x = self.x if x is None else x
        z = self.z if z is None else z
        return (y * 2 + c, x * self.Z + z)

    def z_at(self, offset):
        return (self.z + self.sgn * offset + 2 * self.Z) % self.Z

    def along_z(self, offset):
        return self.dev(z=self.z_at(offset))

    def around(self):
        return [
            (dz, dx, self.dev(x=(self.x + dx) % X, z=self.z_at(dz)))
            for dz in (1, -1, 0)
            for dx in range(X)
            if dz or dx
        ]

    def key_partner(self, d):
        k = (self.k + d) % (2 * self.Y)
        hb = k % 2
        x = self.pair * 3 + hb * (1 - 2 * self.pair)
        return k, self.dev(y=k // 2, x=x)


def barrier(devices):
    sem = pltpu.get_barrier_semaphore()
    for device in devices:
        pl.semaphore_signal(sem, inc=1, device_id=device, device_id_type=MESH)
    pl.semaphore_wait(sem, len(devices))


def remote(src, dst, send, recv, device):
    return pltpu.make_async_remote_copy(
        src_ref=src, dst_ref=dst, send_sem=send, recv_sem=recv, device_id=device, device_id_type=MESH
    )


def turn(data, cosine, sine):
    data = data.astype(jnp.float32)
    return (data * cosine + pltpu.roll(data, HD // 2, 1) * sine).astype(jnp.bfloat16)


def trig(place, freq):
    angle = place.astype(jnp.float32) * freq
    lane = lax.broadcasted_iota(jnp.int32, angle.shape, 1)
    sine = jnp.sin(angle)
    return jnp.cos(angle), jnp.where(lane < HD // 2, -sine, sine)


def gather_kernel(
    sizes, cl_ref, sl_ref, freq_ref, q_ref, sk_ref, sv_ref, k_ref, v_ref,
    qo, ko, vo, sko, svo,
    cl, sl, freq_in, k_in, q_in, sk_in, qs, qb, sks, ks, in_sem,
    q_in_sem, span_sem, v_send, v_recv, k_send, k_recv, q_send, q_recv, on_send,
    core_send, core_recv, own_sem, q_own_sem, pair_send, pair_recv,
):
    at = Place(*sizes)
    Y, Z = at.Y, at.Z
    heads = 2 * Y
    rows, tokens = q_ref.shape[0], k_ref.shape[0]
    ndoc = cl.shape[0]

    reads = [
        pltpu.make_async_copy(cl_ref, cl, in_sem.at[0]),
        pltpu.make_async_copy(sl_ref, sl, in_sem.at[1]),
        pltpu.make_async_copy(freq_ref, freq_in, in_sem.at[2]),
    ]
    k_read = pltpu.make_async_copy(k_ref, k_in, in_sem.at[3])
    for hb in range(2):
        column = pl.multiple_of((2 * at.y + hb) * (GROUP * HD) + at.c * (2 * HD), 2 * HD)
        reads.append(
            pltpu.make_async_copy(q_ref.at[:, pl.ds(column, 2 * HD)], q_in.at[hb], q_in_sem.at[hb])
        )
    own = pl.multiple_of(at.k * HD, HD)
    theirs = pl.multiple_of((at.k + 1 - 2 * at.hb) * HD, HD)
    for i, column in enumerate((own, theirs)):
        reads.append(
            pltpu.make_async_copy(sk_ref.at[:, pl.ds(column, HD)], sk_in.at[i], span_sem.at[i])
        )
    for copy in reads:
        copy.start()
    k_read.start()
    sv_copy = pltpu.make_async_copy(sv_ref.at[:, pl.ds(own, HD)], svo.at[0], span_sem.at[2])
    sv_copy.start()
    v_own = pltpu.make_async_copy(v_ref.at[:, pl.ds(own, HD)], vo.at[at.k], own_sem.at[0])
    v_own.start()

    partners = [at.key_partner(d) for d in range(1, heads)]
    other_core = at.dev(c=1 - at.c)
    around = at.around()
    greet = [at.dev(y=(at.y + dy) % Y, x=x) for dy in range(1, Y) for x in (at.x, at.mate)]
    greet += [device for _, _, device in around] + [at.along_z(2), at.along_z(-2), other_core]
    barrier(greet)

    for copy in reads:
        copy.wait()
    freq = freq_in[...]
    row = at.head * rows + lax.broadcasted_iota(jnp.int32, (rows, HD), 0)
    shift = jnp.zeros((rows, HD), jnp.int32)
    start = jnp.int32(0)
    for d in range(ndoc):
        shift = jnp.where(row >= start, cl[d] - start, shift)
        start = start + sl[d]
    cosine, sine = trig(row + shift, freq)
    for hb in range(2):
        for h in range(2):
            qs[hb, h * rows : (h + 1) * rows, :] = turn(
                q_in[hb, :, h * HD : (h + 1) * HD], cosine, sine
            )
    for i in range(2):
        sks[i] = turn(sk_in[i], cosine, sine)

    q_own = pltpu.make_async_copy(qs.at[at.hb], qb.at[at.z, at.x], own_sem.at[1])
    q_own.start()
    first_copies = []
    for dz, dx, device in around:
        copy = remote(
            qs.at[at.bit_of((at.x + dx) % X)], qb.at[at.z, at.x],
            q_send.at[dz + 1, dx], q_recv.at[-dz + 4, dx], device,
        )
        copy.start()
        first_copies.append(copy)
    pair_copies = [
        remote(sks.at[1], sko.at[1], pair_send.at[0], pair_recv.at[0], at.dev(x=at.mate)),
        remote(
            sv_ref.at[:, pl.ds(theirs, HD)], svo.at[1], pair_send.at[1], pair_recv.at[1],
            at.dev(x=at.mate),
        ),
    ]
    sk_own = pltpu.make_async_copy(sks.at[0], sko.at[0], own_sem.at[2])
    for copy in pair_copies + [sk_own]:
        copy.start()

    onward = []

    def piece(offset, n):
        return qb.at[at.z_at(offset), (at.x - n + X) % X]

    def arrived(offset, n):
        part = piece(offset, n)
        remote(part, part, q_send.at[0, 0], q_recv.at[offset + 4, n], other_core).wait_recv()

    def pass_on(offset, n, far):
        part = piece(offset, n)
        copy = remote(
            part, part, on_send.at[len(onward)], q_recv.at[offset - far + 4, n], at.along_z(far)
        )
        copy.start()
        onward.append(copy)

    slabs = (0, -1, 1, -2, 2, -3, 3, -4)
    cores, kept = [], []

    def to_core(offset):
        i = slabs.index(offset)
        z = at.z_at(offset)
        copy = remote(
            qb.at[z], qo.at[at.c, z], core_send.at[i], core_recv.at[i], other_core
        )
        copy.start()
        cores.append(copy)
        copy = pltpu.make_async_copy(qb.at[z], qo.at[at.c, z], q_own_sem.at[i])
        copy.start()
        kept.append(copy)

    order = sorted(range(1, heads), key=lambda d: -min(d, heads - d))
    v_copies = []
    for d in order:
        k, device = partners[d - 1]
        column = pl.multiple_of(k * HD, HD)
        copy = remote(
            v_ref.at[:, pl.ds(column, HD)], vo.at[at.k], v_send.at[d], v_recv.at[d], device
        )
        copy.start()
        v_copies.append(copy)

    token = (at.ctx * sizes[1] + at.head) * tokens + lax.broadcasted_iota(jnp.int32, (tokens, HD), 0)
    first = jnp.zeros((tokens, HD), jnp.int32)
    start = jnp.int32(0)
    for d in range(ndoc):
        first = jnp.where(token >= start, start, first)
        start = start + cl[d]
    cosine, sine = trig(token - first, freq)
    k_read.wait()
    k_copies = []
    for d in order:
        k, device = partners[d - 1]
        column = pl.multiple_of(k * HD, HD)
        ks[d] = turn(k_in[:, pl.ds(column, HD)], cosine, sine)
        copy = remote(ks.at[d], ko.at[at.k], k_send.at[d], k_recv.at[d], device)
        copy.start()
        k_copies.append(copy)
    ks[0] = turn(k_in[:, pl.ds(own, HD)], cosine, sine)
    k_own = pltpu.make_async_copy(ks.at[0], ko.at[at.k], own_sem.at[3])
    k_own.start()

    for n in range(X):
        for offset in (-1, 1):
            arrived(offset, n)
            pass_on(offset, n, -offset)
    q_own.wait()
    for n in range(1, X):
        arrived(0, n)
    for offset in (0, -1, 1):
        to_core(offset)
    for n in range(X):
        for offset in (-2, 2):
            arrived(offset, n)
            if offset == -2:
                pass_on(offset, n, 2)
            pass_on(offset, n, -offset // 2)
    for offset in (-2, 2):
        to_core(offset)
    for offset in (-3, 3, -4):
        for n in range(X):
            arrived(offset, n)
        to_core(offset)

    for i, offset in enumerate(slabs):
        z = at.z_at(-offset)
        remote(
            qb.at[z], qo.at[1 - at.c, z], core_send.at[i], core_recv.at[i], other_core
        ).wait_recv()
    for copy in v_copies + k_copies + pair_copies:
        copy.wait_recv()
    for copy in v_copies + k_copies + pair_copies + first_copies + onward + cores:
        copy.wait_send()
    for copy in kept + [v_own, k_own, sk_own, sv_copy]:
        copy.wait()


def attend_kernel(
    sizes, cl_ref, sl_ref, q_hbm, k_hbm, v_hbm, sk_hbm, sv_hbm, part_ref, stat_hbm,
    stat_ref, acc, cl, sl, q_ref, k_ref, v_ref, vt_ref, s_even, s_odd, w_odd, f_odd,
    cache_at, span_at, g_block, g_low, g_high, g_first, g_end, g_causal, e_group, e_chunk, in_sem, out_sem,
):
    at = Place(*sizes)
    Z = at.Z
    blocks, tokens, _ = k_hbm.shape
    rows = sk_hbm.shape[1]
    lanes = 4 * rows
    ndoc = cl.shape[0]
    pairs = (
        (cl_ref, cl), (sl_ref, sl), (k_hbm, k_ref.at[pl.ds(0, blocks)]),
        (q_hbm, q_ref), (v_hbm, v_ref.at[pl.ds(0, blocks)]),
        (sk_hbm.at[at.c], k_ref.at[blocks, pl.ds(0, rows)]),
        (sv_hbm.at[at.c], v_ref.at[blocks, pl.ds(0, rows)]),
    )
    reads = [pltpu.make_async_copy(a, b, in_sem.at[i]) for i, (a, b) in enumerate(pairs)]
    for copy in reads:
        copy.start()

    k_ref[blocks, rows:, :] = jnp.zeros((tokens - rows, HD), jnp.bfloat16)
    v_ref[blocks, rows:, :] = jnp.zeros((tokens - rows, HD), jnp.bfloat16)
    half = lax.broadcasted_iota(jnp.int32, (2, Z, 2 * X, 2 * rows), 2)
    stat_ref[...] = jnp.where(half < X, FLOOR, 0.0)
    acc[...] = jnp.zeros_like(acc)
    w_odd[...] = jnp.zeros_like(w_odd)
    f_odd[...] = jnp.ones_like(f_odd)
    reads[0].wait()
    reads[1].wait()

    cache_at[0] = jnp.int32(0)
    span_at[0] = jnp.int32(0)
    for d in range(ndoc):
        cache_at[d + 1] = cache_at[d] + cl[d]
        span_at[d + 1] = span_at[d] + sl[d]

    far = jnp.int32(1 << 20)

    def none(group):
        g_block[group], g_low[group], g_high[group] = jnp.int32(0), jnp.int32(0), jnp.int32(0)
        g_first[group], g_end[group], g_causal[group] = jnp.int32(0), jnp.int32(0), far

    none(0)
    e_group[0], e_chunk[0] = jnp.int32(0), jnp.int32(0)

    def add_block(counts, block, starts, first, width, causal, row_first):
        doc_first, doc_last = jnp.int32(0), jnp.int32(0)
        for d in range(1, ndoc):
            doc_first += (starts[d] <= first).astype(jnp.int32)
            doc_last += (starts[d] < first + width).astype(jnp.int32)

        def add_doc(d, counts):
            group, entry = counts
            g_block[group] = block
            g_low[group] = jnp.maximum(starts[d] - first, 0)
            g_high[group] = jnp.minimum(starts[d + 1] - first, width)
            g_first[group] = jnp.maximum(span_at[d], row_first)
            g_end[group] = span_at[d + 1]
            g_causal[group] = causal
            low = jnp.maximum(span_at[d], row_first) // rows
            high = (span_at[d + 1] + rows - 1) // rows

            def add_chunk(n, entry):
                e_group[entry] = group
                e_chunk[entry] = n
                return entry + 1

            return group + 1, lax.fori_loop(low, high, add_chunk, entry)

        return lax.fori_loop(doc_first, doc_last + 1, add_doc, counts)

    def cache_block(b, counts):
        x = at.pair * 3 + (b % 2) * (1 - 2 * at.pair)
        first = (((b // 2) * 2 + at.c) * sizes[1] + x * Z + at.z) * tokens
        return add_block(counts, b, cache_at, first, tokens, far, 0)

    counts = lax.fori_loop(0, blocks, cache_block, (jnp.int32(1), jnp.int32(1)))
    first = (jnp.where(at.c == 0, at.x, at.mate) * Z + at.z) * rows
    _, count = add_block(counts, jnp.int32(blocks), span_at, first, rows, -first, first)
    for i in range(4):
        e_group[count + i], e_chunk[count + i] = jnp.int32(0), jnp.int32(0)

    for copy in reads[2:]:
        copy.wait()

    def turn_over(b, carry):
        vt_ref[b] = v_ref[b].T
        return carry

    lax.fori_loop(0, blocks + 1, turn_over, 0)

    lane = lax.broadcasted_iota(jnp.int32, (1, lanes), 1) % rows
    token = lax.broadcasted_iota(jnp.int32, (tokens, lanes), 0)

    def scores(i):
        n = e_chunk[i]
        x, z = n // Z, n % Z
        q = jnp.concatenate([q_ref[0, z, x], q_ref[1, z, x]], axis=0)
        return lax.dot_general(
            k_ref[g_block[e_group[i]]], q, (((1,), (1,)), ((), ())),
            preferred_element_type=jnp.float32,
        )

    def soften(i, s):
        group, n = e_group[i], e_chunk[i]
        x, z = n // Z, n % Z
        row = n * rows + lane
        here = (row >= g_first[group]) & (row < g_end[group])
        high = jnp.minimum(g_high[group], row + g_causal[group] + 1)
        s = jnp.where((token >= g_low[group]) & (token < high), s * SCALE, FLOOR)
        m_old = jnp.concatenate([stat_ref[c, z, pl.ds(x, 1), :] for c in range(2)], axis=1)
        l_old = jnp.concatenate([stat_ref[c, z, pl.ds(X + x, 1), :] for c in range(2)], axis=1)
        m_new = jnp.where(here, jnp.maximum(m_old, jnp.max(s, axis=0, keepdims=True)), m_old)
        w = jnp.exp2(s - jnp.where(here, m_new, -FLOOR))
        factor = jnp.exp2(m_old - m_new)
        l_new = l_old * factor + jnp.sum(w, axis=0, keepdims=True)
        for c in range(2):
            part = slice(c * 2 * rows, (c + 1) * 2 * rows)
            stat_ref[c, z, pl.ds(x, 1), :] = m_new[:, part]
            stat_ref[c, z, pl.ds(X + x, 1), :] = l_new[:, part]
        return w.astype(jnp.bfloat16), factor

    def product(i, w):
        return jnp.dot(vt_ref[g_block[e_group[i]]], w, preferred_element_type=jnp.float32)

    def update(i, o, factor):
        n = e_chunk[i]
        x, z = n // Z, n % Z
        for c in range(2):
            part = slice(c * 2 * rows, (c + 1) * 2 * rows)
            acc[c, z, x] = acc[c, z, x] * factor[:, part] + o[:, part]

    s_even[...] = scores(1)

    def step(j, carry):
        i = 2 * j + 1
        s_odd[...] = scores(i + 1)
        o_before = product(i - 1, w_odd[...])
        w, factor = soften(i, s_even[...])
        update(i - 1, o_before, f_odd[...])
        s_even[...] = scores(i + 2)
        o = product(i, w)
        w_next, factor_next = soften(i + 1, s_odd[...])
        update(i, o, factor)
        w_odd[...] = w_next
        f_odd[...] = factor_next
        return carry

    steps = count // 2
    lax.fori_loop(0, steps, step, 0)
    update(2 * steps, product(2 * steps, w_odd[...]), f_odd[...])
    leave = pltpu.make_async_copy(stat_ref, stat_hbm.at[pl.ds(0, 2)], out_sem.at[0])
    leave.start()
    part_ref[...] = acc[...].astype(jnp.bfloat16)
    leave.wait()


def reduce_kernel(
    sizes, part_hbm, stat_hbm, out_ref,
    part_ref, stat_ref, cr, cr_stat, sb, sb_stat, rb, rb_stat, fb, fb_stat, xr, xr_stat, factor_ref,
    core_send, core_recv, core_stat_send, core_stat_recv,
    ring_send, ring_recv, ring_stat_send, ring_stat_recv,
    x_send, x_recv, x_stat_send, x_stat_recv, out_send, out_recv, cross_send, cross_recv, own_sem,
    in_sem,
):
    at = Place(*sizes)
    Y, Z = at.Y, at.Z
    rows = out_ref.shape[0]
    reads = [
        pltpu.make_async_copy(stat_hbm.at[at.c], stat_ref, in_sem.at[0]),
        pltpu.make_async_copy(part_hbm.at[at.c], part_ref, in_sem.at[1]),
    ]
    for copy in reads:
        copy.start()
    other_core = at.dev(c=1 - at.c)
    around = at.around()
    ends = [at.dev(y=(at.y + dy) % Y) for dy in range(1, Y)]
    greet = [device for _, _, device in around] + ends
    barrier(greet + [at.along_z(2), at.along_z(-2), other_core])

    slabs = (4, 3, -3, 2, -2, 1, -1, 0)
    stats_over = remote(
        stat_hbm.at[1 - at.c], cr_stat, core_stat_send.at[0], core_stat_recv.at[0], other_core
    )
    stats_over.start()
    sent = [stats_over]
    for i, offset in enumerate(slabs):
        z = at.z_at(-offset)
        copy = remote(
            part_hbm.at[1 - at.c, z], cr.at[z], core_send.at[i], core_recv.at[i], other_core
        )
        copy.start()
        sent.append(copy)

    def both_cores(offset):
        i, z = slabs.index(offset), at.z_at(offset)
        remote(part_ref.at[z], cr.at[z], core_send.at[i], core_recv.at[i], other_core).wait_recv()
        return [(part_ref.at[z], stat_ref.at[z]), (cr.at[z], cr_stat.at[z])]

    def ring_in(n, x):
        if x is None:
            remote(
                sb_stat.at[n], rb_stat.at[n], ring_stat_send.at[n], ring_stat_recv.at[n], other_core
            ).wait_recv()
        else:
            remote(
                sb.at[n, x], rb.at[n, x], ring_send.at[n, x], ring_recv.at[n, x], other_core
            ).wait_recv()

    def ring_out(n, device):
        def emit(x):
            if x is None:
                copy = remote(
                    sb_stat.at[n], rb_stat.at[n], ring_stat_send.at[n], ring_stat_recv.at[n], device
                )
            else:
                copy = remote(
                    sb.at[n, x], rb.at[n, x], ring_send.at[n, x], ring_recv.at[n, x], device
                )
            copy.start()
            sent.append(copy)

        return emit

    def join(sources, came, to, to_stat, emit, hold=None):
        for n in came:
            ring_in(n, None)
            sources = sources + [(rb.at[n], rb_stat.at[n])]
        stats = [stat[...] for _, stat in sources]
        top = functools.reduce(jnp.maximum, [s[:X] for s in stats])
        factors = [jnp.exp2(s[:X] - top) for s in stats]
        to_stat[:X, :] = top
        to_stat[X:, :] = sum(s[X:] * f for s, f in zip(stats, factors))
        emit(None)
        if hold is not None:
            for i, f in enumerate(factors):
                hold[i] = f

        def factor(i, x):
            return factors[i][x : x + 1] if hold is None else hold[i, pl.ds(x, 1), :]

        def piece(x):
            for n in came:
                ring_in(n, x)
            to[x] = sum(
                part[x].astype(jnp.float32) * factor(i, x) for i, (part, _) in enumerate(sources)
            ).astype(jnp.bfloat16)
            emit(x)

        return piece

    for copy in reads:
        copy.wait()
    stats_over.wait_recv()
    stages = (
        ((4, 2, 0, ()),),
        ((3, 1, 1, ()), (-3, -1, 2, ())),
        ((2, 1, 3, (0, 1)), (-2, -1, 4, (2,))),
    )
    def work(stage):
        pieces = [
            join(
                both_cores(offset), came, sb.at[n], sb_stat.at[n], ring_out(n, at.along_z(far))
            )
            for offset, far, n, came in stage
        ]
        for x in range(X):
            for piece in pieces:
                piece(x)

    def column_out(dz):
        def emit(x):
            for dx in range(X):
                if (dz or dx) and x is None:
                    copy = remote(
                        fb_stat.at[dz + 1], xr_stat.at[-dz + 1, at.x], x_stat_send.at[dz + 1, dx],
                        x_stat_recv.at[-dz + 1, dx], at.dev(x=(at.x + dx) % X, z=at.z_at(dz)),
                    )
                    copy.start()
                    sent.append(copy)

        return emit

    own = []

    def finish(last):
        pieces = [
            join(
                both_cores(dz), {0: (), 1: (3,), -1: (4,)}[dz], fb.at[dz + 1], fb_stat.at[dz + 1],
                column_out(dz), factor_ref.at[dz + 1],
            )
            for dz in last
        ]
        for dx in range(X):
            for dz, piece in zip(last, pieces):
                x = (at.x + dx) % X
                piece(x)
                if dz or dx:
                    copy = remote(
                        fb.at[dz + 1, x], xr.at[-dz + 1, at.x], x_send.at[dz + 1, dx],
                        x_recv.at[-dz + 1, dx], at.dev(x=x, z=at.z_at(dz)),
                    )
                    copy.start()
                    sent.append(copy)
                else:
                    own.extend((
                        pltpu.make_async_copy(fb.at[1, at.x], xr.at[1, at.x], own_sem.at[0]),
                        pltpu.make_async_copy(fb_stat.at[1], xr_stat.at[1, at.x], own_sem.at[1]),
                    ))
                    for copy in own:
                        copy.start()

    work(stages[0])
    work(stages[1])
    finish((0,))
    work(stages[2])
    finish((1, -1))
    for copy in own:
        copy.wait()
    for dz in (0, 1, -1):
        for dx in range(X):
            if dz or dx:
                remote(
                    fb_stat.at[0], xr_stat.at[dz + 1, at.x], x_stat_send.at[dz + 1, dx],
                    x_stat_recv.at[dz + 1, dx], other_core,
                ).wait_recv()
                remote(
                    fb.at[0, 0], xr.at[dz + 1, at.x], x_send.at[dz + 1, dx], x_recv.at[dz + 1, dx],
                    other_core,
                ).wait_recv()

    def columns(y, hb, c):
        first = pl.multiple_of((2 * y + hb) * (GROUP * HD) + c * (2 * HD), 2 * HD)
        return out_ref.at[:, pl.ds(first, 2 * HD)]

    def cross(hb, dy):
        part = columns((at.y - dy + Y) % Y, hb, at.c)
        copy = remote(part, part, cross_send.at[hb, dy], cross_recv.at[hb, dy], other_core)
        copy.start()
        sent.append(copy)

    near = sorted(range(1, Y), key=lambda dy: min(dy, Y - dy))
    for hb, pair in enumerate(((0, 3), (1, 2))):
        sources = [(d, n) for n in pair for d in range(3)]
        tops = [xr_stat[d, n, pl.ds(at.x, 1), :] for d, n in sources]
        totals = [xr_stat[d, n, pl.ds(X + at.x, 1), :] for d, n in sources]
        top = functools.reduce(jnp.maximum, tops)
        factors = [jnp.exp2(t - top) for t in tops]
        total = sum(t * f for t, f in zip(totals, factors))
        value = sum(xr[d, n].astype(jnp.float32) * f for (d, n), f in zip(sources, factors))
        value = (value / total).T.astype(jnp.bfloat16)
        part = columns(at.y, hb, at.c)
        for h in range(2):
            part[:, h * HD : (h + 1) * HD] = value[h * rows : (h + 1) * rows]
        for dy in reversed(near):
            copy = remote(part, part, out_send.at[hb, dy], out_recv.at[hb, dy], ends[dy - 1])
            copy.start()
            sent.append(copy)
        cross(hb, 0)
    for hb in range(2):
        for dy in near:
            part = columns((at.y - dy + Y) % Y, hb, at.c)
            remote(part, part, out_send.at[hb, dy], out_recv.at[hb, dy], other_core).wait_recv()
            cross(hb, dy)
    for hb in range(2):
        for dy in range(Y):
            part = columns((at.y - dy + Y) % Y, hb, 1 - at.c)
            remote(part, part, cross_send.at[hb, dy], cross_recv.at[hb, dy], other_core).wait_recv()
    for copy in sent:
        copy.wait_send()


def body(queries, span_keys, span_values, cache_keys, cache_values, cache_lengths, span_lengths):
    sizes = (lax.axis_size("ctx"), lax.axis_size("head"))
    Y, Z = sizes[0] // 2, sizes[1] // X
    heads = 2 * Y
    rows, tokens = queries.shape[0], cache_keys.shape[0]
    bf16, f32 = jnp.bfloat16, jnp.float32
    lengths = pltpu.SMEM(cache_lengths.shape, jnp.int32)
    vmem = pl.BlockSpec(memory_space=pltpu.VMEM)
    hbm = pl.BlockSpec(memory_space=pltpu.HBM)
    dma = pltpu.SemaphoreType.DMA
    freq = jnp.asarray(inverse_freq())

    q_all, k_all, v_all, sk, sv = pl.pallas_call(
        functools.partial(gather_kernel, sizes),
        out_shape=(
            jax.ShapeDtypeStruct((2, Z, X, 2 * rows, HD), bf16),
            jax.ShapeDtypeStruct((heads, tokens, HD), bf16),
            jax.ShapeDtypeStruct((heads, tokens, HD), bf16),
            jax.ShapeDtypeStruct((2, rows, HD), bf16),
            jax.ShapeDtypeStruct((2, rows, HD), bf16),
        ),
        in_specs=[hbm] * 8,
        out_specs=(hbm,) * 5,
        scratch_shapes=[
            lengths, lengths, VMEM(freq.shape, f32), VMEM((tokens, heads * HD), bf16),
            VMEM((2, rows, 2 * HD), bf16),
            VMEM((2, rows, HD), bf16),
            VMEM((2, 2 * rows, HD), bf16),
            VMEM((Z, X, 2 * rows, HD), bf16),
            VMEM((2, rows, HD), bf16),
            VMEM((heads, tokens, HD), bf16),
            dma((4,)), dma((2,)), dma((3,)), dma((heads,)), dma((heads,)), dma((heads,)), dma((heads,)),
            dma((3, X)), dma((Z, X)), dma((5 * X,)), dma((Z,)), dma((Z,)),
            dma((4,)), dma((Z,)), dma((2,)), dma((2,)),
        ],
        compiler_params=pltpu.CompilerParams(
            collective_id=0, has_side_effects=True, vmem_limit_bytes=60 * 1024 * 1024
        ),
        name="gather",
    )(cache_lengths, span_lengths, freq, queries, span_keys, span_values, cache_keys, cache_values)

    ndoc = cache_lengths.shape[0]
    groups = (heads + 1) * ndoc + 1
    entries = (heads + 1) * (X * Z + ndoc) + 8

    def numbers(n):
        return pltpu.SMEM((n,), jnp.int32)

    parts, stats = pl.pallas_call(
        functools.partial(attend_kernel, sizes),
        out_shape=(
            jax.ShapeDtypeStruct((2, Z, X, HD, 2 * rows), bf16),
            jax.ShapeDtypeStruct((16, Z, 2 * X, 2 * rows), f32),
        ),
        in_specs=[hbm] * 7,
        out_specs=(vmem, hbm),
        scratch_shapes=[
            VMEM((2, Z, 2 * X, 2 * rows), f32),
            VMEM((2, Z, X, HD, 2 * rows), f32), lengths, lengths, VMEM(q_all.shape, bf16),
            VMEM((heads + 1, tokens, HD), bf16), VMEM((heads + 1, tokens, HD), bf16),
            VMEM((heads + 1, HD, tokens), bf16),
            VMEM((tokens, 4 * rows), f32), VMEM((tokens, 4 * rows), f32),
            VMEM((tokens, 4 * rows), bf16), VMEM((1, 4 * rows), f32),
            numbers(ndoc + 1), numbers(ndoc + 1), *[numbers(groups)] * 6,
            numbers(entries), numbers(entries), dma((7,)), dma((1,)),
        ],
        compiler_params=pltpu.CompilerParams(vmem_limit_bytes=60 * 1024 * 1024),
        name="attend",
    )(cache_lengths, span_lengths, q_all, k_all, v_all, sk, sv)

    piece, stat = (HD, 2 * rows), (2 * X, 2 * rows)
    return pl.pallas_call(
        functools.partial(reduce_kernel, sizes),
        out_shape=jax.ShapeDtypeStruct(queries.shape, bf16),
        in_specs=[hbm, hbm],
        out_specs=vmem,
        scratch_shapes=[
            VMEM((Z, X) + piece, bf16), VMEM((Z,) + stat, f32),
            VMEM((Z, X) + piece, bf16), VMEM((Z,) + stat, f32),
            VMEM((5, X) + piece, bf16), VMEM((5,) + stat, f32),
            VMEM((5, X) + piece, bf16), VMEM((5,) + stat, f32),
            VMEM((3, X) + piece, bf16), VMEM((3,) + stat, f32),
            VMEM((3, X) + piece, bf16), VMEM((3, X) + stat, f32),
            VMEM((3, 3, X, 2 * rows), f32),
            dma((Z,)), dma((Z,)), dma((1,)), dma((1,)),
            dma((5, X)), dma((5, X)), dma((5,)), dma((5,)),
            dma((3, X)), dma((3, X)), dma((3, X)), dma((3, X)),
            dma((2, Y)), dma((2, Y)), dma((2, Y)), dma((2, Y)), dma((2,)), dma((2,)),
        ],
        compiler_params=pltpu.CompilerParams(
            collective_id=1, has_side_effects=True, vmem_limit_bytes=53 * 1024 * 1024
        ),
        name="reduce",
    )(parts, stats)


def solution(mesh):
    placed = (
        P("head", None),
        P("head", None),
        P("head", None),
        P(("ctx", "head"), None),
        P(("ctx", "head"), None),
        P(),
        P(),
    )
    return jax.shard_map(
        body, mesh=mesh, in_specs=placed, out_specs=P("head", None), check_vma=False
    )
```
